128 devices in a mesh: dp: 8 (over y, z_lo), ctx: 4 (over z_hi, core), head: 4 (over x).
Axes of the slice: x: 4, y: 4, z: 4 (z_hi: 2, z_lo: 2; z = z_hi * 2 + z_lo), core: 2. Of those that a mesh axis runs over, the one named last changes fastest.
Arguments:
- inputs: bfloat16 [16, 1024, 1536], P('dp', ('ctx', 'head')), may hold values from -6 to 6
- positions: int32 [16, 1024], P('dp', ('ctx', 'head')), may hold values from 0 to 2047
- cotangent: bfloat16 [16, 1024, 1536], P('dp', ('ctx', 'head')), may hold values from -6 to 6
- attn_gain: bfloat16 [2, 1536], P(None, ('dp', 'ctx')), may hold values from 0.5 to 1.5
- query_weight: bfloat16 [2, 1536, 1536], P(None, ('dp', 'ctx')), may hold values from -0.15625 to 0.15625
- key_matrix: bfloat16 [2, 1536, 768], P(None, ('dp', 'ctx')), may hold values from -0.15625 to 0.15625
- value_matrix: bfloat16 [2, 1536, 768], P(None, ('dp', 'ctx')), may hold values from -0.15625 to 0.15625
- out_weight: bfloat16 [2, 1536, 1536], P(None, ('dp', 'ctx')), may hold values from -2.5 to 2.5
- mlp_gain: bfloat16 [2, 1536], P(None, ('dp', 'ctx')), may hold values from 0.5 to 1.5
- gate_weight: bfloat16 [2, 1536, 4096], P(None, ('dp', 'ctx')), may hold values from -0.15625 to 0.15625
- up_weight: bfloat16 [2, 1536, 4096], P(None, ('dp', 'ctx')), may hold values from -0.15625 to 0.15625
- down_weight: bfloat16 [2, 4096, 1536], P(None, ('dp', 'ctx')), may hold values from -0.09375 to 0.09375
Outputs:
- output: bfloat16 [16, 1024, 1536], P('dp', ('ctx', 'head'))
- input_grad: float32 [16, 1024, 1536], P('dp', ('ctx', 'head'))
- grad_attn_gain: float32 [2, 1536], P(None, ('dp', 'ctx'))
- grad_query_weight: float32 [2, 1536, 1536], P(None, ('dp', 'ctx'))
- grad_key_weight: float32 [2, 1536, 768], P(None, ('dp', 'ctx'))
- grad_value_weight: float32 [2, 1536, 768], P(None, ('dp', 'ctx'))
- grad_out_weight: float32 [2, 1536, 1536], P(None, ('dp', 'ctx'))
- grad_mlp_gain: float32 [2, 1536], P(None, ('dp', 'ctx'))
- grad_gate_weight: float32 [2, 1536, 4096], P(None, ('dp', 'ctx'))
- grad_up_weight: float32 [2, 1536, 4096], P(None, ('dp', 'ctx'))
- grad_down_weight: float32 [2, 4096, 1536], P(None, ('dp', 'ctx'))
The draws below stay inside these ranges and needn't reach their ends.
All inputs are finite; a program needn't handle non-finite values.
Results may differ from the reference program's by a relative error of at most 0.035.
Values may be sent and summed in bfloat16 or wider, within the bound.
A program may use at most 320 MiB of HBM per device.

```python
import jax
import jax.numpy as jnp
from jax import lax

MODEL_WIDTH = 1536
QUERY_HEADS = 16
KEY_VALUE_HEADS = 8
HEAD_SIZE = 96
FF = 4096
DECODER_LAYERS = 2
SEQUENCE_TOKENS = 1024
SEQS = 16


def place_ends(drawn, rng, low, high):
    extent = drawn.shape
    index_at = [jax.random.randint(jax.random.fold_in(rng, axis), (), 0, extent[axis]) for axis in range(len(extent))]
    drawn = drawn.at[tuple(index_at)].set(low)
    longest = extent.index(max(extent))
    index_at[longest] = (index_at[longest] + 1) % extent[longest]
    return drawn.at[tuple(index_at)].set(high)


def level_of(own_key, dims, pieces, low, largest):
    level, own = 1.0, jax.random.fold_in(own_key, 6)
    for position, shards_of in pieces:
        heights = jnp.exp(jax.random.uniform(jax.random.fold_in(own, position), (shards_of,), jnp.float32, low / len(pieces), largest / len(pieces)))
        level = level * jnp.repeat(heights, dims[position] // shards_of).reshape([-1 if axis == position else 1 for axis in range(len(dims))])
    return level


def bell_draw(own_key, shape, scale, reach, pieces=(), kind=jnp.bfloat16):
    entries = scale * jax.random.normal(own_key, shape, jnp.float32)
    if pieces:
        entries = entries * level_of(own_key, shape, pieces, -0.22, 0.18)
    return jnp.clip(entries, -reach, reach).astype(kind)


def setup_inputs(seed: int = 0) -> dict:
    key_list = jax.random.split(jax.random.key(seed), 13)
    inputs = bell_draw(key_list[0], (SEQS, SEQUENCE_TOKENS, MODEL_WIDTH), 1.0, 6.0, ((0, 8), (1, 16)))
    positions = place_ends(jax.random.randint(key_list[1], (SEQS, SEQUENCE_TOKENS), 0, 2 * SEQUENCE_TOKENS), jax.random.fold_in(key_list[1], 1), 0, (2 * SEQUENCE_TOKENS) - 1).astype(jnp.int32)
    cotangent = bell_draw(key_list[2], (SEQS, SEQUENCE_TOKENS, MODEL_WIDTH), 1.0, 6.0, ((0, 8), (1, 16)))
    attn_gain = jnp.clip(1.0 + 0.1 * jax.random.normal(key_list[3], (DECODER_LAYERS, MODEL_WIDTH), jnp.float32), 0.5, 1.5).astype(jnp.bfloat16)
    query_weight = bell_draw(key_list[4], (DECODER_LAYERS, MODEL_WIDTH, QUERY_HEADS * HEAD_SIZE), MODEL_WIDTH ** -0.5, 0.15625, ((1, 32),))
    key_matrix = bell_draw(key_list[5], (DECODER_LAYERS, MODEL_WIDTH, KEY_VALUE_HEADS * HEAD_SIZE), MODEL_WIDTH ** -0.5, 0.15625, ((1, 32),))
    value_matrix = bell_draw(key_list[6], (DECODER_LAYERS, MODEL_WIDTH, KEY_VALUE_HEADS * HEAD_SIZE), MODEL_WIDTH ** -0.5, 0.15625, ((1, 32),))
    out_weight = bell_draw(key_list[7], (DECODER_LAYERS, QUERY_HEADS * HEAD_SIZE, MODEL_WIDTH), (max(4, QUERY_HEADS * HEAD_SIZE // 256)) ** -0.5, 2.5, ((1, 32),))
    mlp_gain = jnp.clip(1.0 + 0.1 * jax.random.normal(key_list[8], (DECODER_LAYERS, MODEL_WIDTH), jnp.float32), 0.5, 1.5).astype(jnp.bfloat16)
    gate_weight = bell_draw(key_list[9], (DECODER_LAYERS, MODEL_WIDTH, FF), MODEL_WIDTH ** -0.5, 0.15625, ((1, 32),))
    up_weight = bell_draw(key_list[10], (DECODER_LAYERS, MODEL_WIDTH, FF), MODEL_WIDTH ** -0.5, 0.15625, ((1, 32),))
    down_weight = bell_draw(key_list[11], (DECODER_LAYERS, FF, MODEL_WIDTH), FF ** -0.5, 0.09375, ((1, 32),))
    return dict(inputs=inputs, positions=positions, cotangent=cotangent, attn_gain=attn_gain, query_weight=query_weight, key_matrix=key_matrix, value_matrix=value_matrix, out_weight=out_weight, mlp_gain=mlp_gain, gate_weight=gate_weight, up_weight=up_weight, down_weight=down_weight)


EPS = 1e-05
BASE = 100000.0
NEG = -1e+30
HIGHEST = lax.Precision.HIGHEST

@jax.custom_vjp
def lowered_input(v):
    return lax.optimization_barrier(v.astype(jnp.bfloat16)).astype(jnp.float32)

@jax.custom_vjp
def lowered_backward(v):
    return v

def low_keep(v):
    return (lowered_input(v), None)

def low_pass(kept, grad):
    return (grad,)

def back_keep(v):
    return (v, None)

def back_low(kept, grad):
    return (lowered_input(grad),)
lowered_input.defvjp(low_keep, low_pass)
lowered_backward.defvjp(back_keep, back_low)

def matrix_product(left, right):
    return jnp.dot(left, right, precision=HIGHEST)

def rope_tables(positions):
    half_width = HEAD_SIZE // 2
    frequency = BASE ** (-(jnp.arange(half_width, dtype=jnp.float32) * 2.0 / HEAD_SIZE))
    angles = positions.astype(jnp.float32)[:, None] * frequency[None, :]
    return (jnp.cos(angles), jnp.sin(angles))

def rotate(tensor, cosine, sine_table):
    half_width = HEAD_SIZE // 2
    first = tensor[..., :half_width]
    second = tensor[..., half_width:]
    cos_b = cosine[:, None, :]
    sin_b = sine_table[:, None, :]
    return jnp.concatenate([first * cos_b - second * sin_b, second * cos_b + first * sin_b], axis=-1)

def rms_norm(hidden, gain):
    scale_row = lax.rsqrt(lax.optimization_barrier(jnp.mean(hidden * hidden, axis=-1, keepdims=True)) + EPS)
    return hidden * scale_row * gain

def attention_rows(queries, start, keys, values_kv):
    row_count = queries.shape[0]
    repeat_heads = QUERY_HEADS // KEY_VALUE_HEADS
    keys_all = jnp.repeat(keys, repeat_heads, axis=1)
    values_all = jnp.repeat(values_kv, repeat_heads, axis=1)
    scores = jnp.einsum('qhd,khd->hqk', queries, keys_all, precision=HIGHEST) * HEAD_SIZE ** (-0.5)
    scores = lowered_backward(scores)
    query_pos = start + jnp.arange(row_count, dtype=jnp.int32)
    key_pos = jnp.arange(SEQUENCE_TOKENS, dtype=jnp.int32)
    scores = jnp.where(key_pos[None, None, :] <= query_pos[None, :, None], scores, NEG)
    probability = lowered_input(jax.nn.softmax(scores, axis=-1))
    return jnp.einsum('hqk,khd->qhd', probability, values_all, precision=HIGHEST)

def attention(queries, keys, values_kv):
    row_count = min(512, SEQUENCE_TOKENS)
    blocks = SEQUENCE_TOKENS // row_count
    query_blocks = queries.reshape(blocks, row_count, QUERY_HEADS, HEAD_SIZE)
    starts = jnp.arange(blocks, dtype=jnp.int32) * row_count

    def one_block(block_item):
        return attention_rows(block_item[0], block_item[1], keys, values_kv)
    result = lax.map(jax.checkpoint(one_block), (query_blocks, starts))
    return result.reshape(SEQUENCE_TOKENS, QUERY_HEADS * HEAD_SIZE)

def block_forward(hidden, cosine, sine_table, weight_set):
    attn_gain, query_weight, key_matrix, value_matrix, out_weight, mlp_gain, gate_weight, up_weight, down_weight = weight_set
    normalized_rows = lowered_input(rms_norm(hidden, attn_gain))
    query_p = lowered_backward(matrix_product(normalized_rows, query_weight)).reshape(SEQUENCE_TOKENS, QUERY_HEADS, HEAD_SIZE)
    key_projected = lowered_backward(matrix_product(normalized_rows, key_matrix)).reshape(SEQUENCE_TOKENS, KEY_VALUE_HEADS, HEAD_SIZE)
    value_broadcast = lowered_backward(lowered_input(matrix_product(normalized_rows, value_matrix))).reshape(SEQUENCE_TOKENS, KEY_VALUE_HEADS, HEAD_SIZE)
    queries = lowered_backward(lowered_input(rotate(query_p, cosine, sine_table)))
    keys = lowered_backward(lowered_input(rotate(key_projected, cosine, sine_table)))
    mixed = lowered_backward(lowered_input(attention(queries, keys, value_broadcast)))
    residual = hidden + lowered_backward(matrix_product(mixed, out_weight))
    normed_two = lowered_input(rms_norm(residual, mlp_gain))
    gate = lowered_backward(matrix_product(normed_two, gate_weight))
    up_proj = lowered_backward(matrix_product(normed_two, up_weight))
    activ = lowered_input(jax.nn.silu(gate) * up_proj)
    return residual + lowered_backward(matrix_product(activ, down_weight))

def reference(inputs, positions, cotangent, attn_gain, query_weight, key_matrix, value_matrix, out_weight, mlp_gain, gate_weight, up_weight, down_weight):
    params = tuple((weight.astype(jnp.float32) for weight in (attn_gain, query_weight, key_matrix, value_matrix, out_weight, mlp_gain, gate_weight, up_weight, down_weight)))

    def forward(hidden, sequence_pos, weight_set):
        cosine, sine_table = rope_tables(sequence_pos)
        for layer_idx in range(DECODER_LAYERS):
            hidden = block_forward(hidden, cosine, sine_table, tuple((member[layer_idx] for member in weight_set)))
        return hidden

    def sequence_step(running, sequence):
        seq_in, seq_pos, seq_cot = sequence
        result, pullback = jax.vjp(lambda hidden, weight_set: forward(hidden, seq_pos, weight_set), seq_in.astype(jnp.float32), params)
        grad_in, grad_params = pullback(seq_cot.astype(jnp.float32))
        return (tuple((current + addend for current, addend in zip(running, grad_params))), (result, grad_in))
    zeros = tuple((jnp.zeros_like(weight) for weight in params))
    running, (results, grad_inputs) = lax.scan(sequence_step, zeros, (inputs, positions, cotangent))
    return (results.astype(jnp.bfloat16), grad_inputs, running[0], running[1], running[2], running[3], running[4], running[5], running[6], running[7], running[8])
```

```python
import functools

import jax
import jax.numpy as jnp
from jax import lax
from jax.experimental import pallas as pl
from jax.experimental.pallas import tpu as pltpu
from jax.sharding import PartitionSpec as P

HEAD = 96
LAYERS = 2
D = 1536
EPS = 1e-05
BASE = 100000.0
NEG = -1e30
F32 = jnp.float32
BF = jnp.bfloat16
MESH = pl.DeviceIdType.MESH
VMEM_LIMIT = 56 * 1024 * 1024


def place():
    dp, ctx, head = lax.axis_index("dp"), lax.axis_index("ctx"), lax.axis_index("head")
    y, zlo = lax.div(dp, 2), lax.rem(dp, 2)
    zhi, core = lax.div(ctx, 2), lax.rem(ctx, 2)
    return dict(dp=dp, ctx=ctx, x=head, y=y, zlo=zlo, zhi=zhi, core=core, z=zhi * 2 + zlo)


def dev(p, dx=0, dy=0, dz=0, dc=0):
    x = lax.rem(p["x"] + dx, 4)
    y = lax.rem(p["y"] + dy, 4)
    z = lax.rem(p["z"] + dz, 4)
    core = lax.rem(p["core"] + dc, 2)
    return (y * 2 + lax.rem(z, 2), lax.div(z, 2) * 2 + core, x)


def z_slot(z):
    return lax.rem(z, 2) * 2 + lax.div(z, 2)


class Op:
    def __init__(self, ins, outs, scratch, offsets, run, alias=()):
        self.ins, self.outs, self.scratch = list(ins), list(outs), list(scratch)
        self.offsets, self.run, self.alias = offsets, run, dict(alias)


def sems(n):
    return pltpu.SemaphoreType.DMA((n,))


def build(cid, ops, cost=0):
    ins = [a for op in ops for a in op.ins]
    outs = [o for op in ops for o in op.outs]
    scratch = [s for op in ops for s in op.scratch]
    offsets, alias, i0, o0 = [], {}, 0, 0
    for op in ops:
        for o in op.offsets:
            key = tuple(o.get(k, 0) for k in ("dx", "dy", "dz", "dc"))
            if key not in offsets:
                offsets.append(key)
        for i, o in op.alias.items():
            alias[i0 + i] = o0 + o
        i0, o0 = i0 + len(op.ins), o0 + len(op.outs)
    n_in, n_out = len(ins), len(outs)

    def kernel(*refs):
        p = place()
        if offsets:
            barrier = pltpu.get_barrier_semaphore()
            for o in offsets:
                pl.semaphore_signal(barrier, inc=1, device_id=dev(p, *o), device_id_type=MESH)
            pl.semaphore_wait(barrier, len(offsets))
        i, o, s = 0, n_in, n_in + n_out
        runs = []
        for op in ops:
            runs.append(
                op.run(
                    p,
                    refs[i : i + len(op.ins)],
                    refs[o : o + len(op.outs)],
                    refs[s : s + len(op.scratch)],
                )
            )
            i, o, s = i + len(op.ins), o + len(op.outs), s + len(op.scratch)
        while runs:
            live = []
            for r in runs:
                try:
                    next(r)
                    live.append(r)
                except StopIteration:
                    pass
            runs = live

    results = pl.pallas_call(
        kernel,
        out_shape=[jax.ShapeDtypeStruct(s, d) for s, d in outs],
        in_specs=[pl.BlockSpec(memory_space=pl.ANY)] * n_in,
        out_specs=[pl.BlockSpec(memory_space=pl.ANY)] * n_out,
        scratch_shapes=scratch,
        input_output_aliases=alias,
        compiler_params=pltpu.CompilerParams(
            collective_id=cid, has_side_effects=True, vmem_limit_bytes=VMEM_LIMIT
        ),
    )(*ins)
    split = []
    for op in ops:
        split.append(list(results[: len(op.outs)]))
        results = results[len(op.outs) :]
    return split


def send(src, dst, send_sem, recv_sem, target):
    c = pltpu.make_async_remote_copy(
        src_ref=src,
        dst_ref=dst,
        send_sem=send_sem,
        recv_sem=recv_sem,
        device_id=target,
        device_id_type=MESH,
    )
    c.start()
    return c


def copy(src, dst, sem):
    c = pltpu.make_async_copy(src, dst, sem)
    c.start()
    return c


X_OFF = [dict(dx=d) for d in (1, 3, 2)]
Y_OFF = [dict(dy=d) for d in (1, 3, 2)]
Z_OFF = [dict(dz=d) for d in (1, 3, 2)]
CORE_OFF = [dict(dc=1)]
CTX_OFF = [dict(dz=2, dc=0), dict(dz=2, dc=1), dict(dz=0, dc=1)]
SEQ_OFF = [
    dict(dx=dx, dz=dz, dc=dc) for dx in range(4) for dz in (0, 2) for dc in (0, 1)
][1:]
SHARD_OFF = [
    dict(dy=dy, dz=dz, dc=dc) for dy in range(4) for dz in range(4) for dc in (0, 1)
][1:]


def swap_op(a, out, offsets, near, far):
    block = jax.eval_shape(
        lambda v: near(dict(ctx=0, x=0, core=0, zhi=0), _Shape(v), _Shape(v))[0].value, a
    )
    n = len(offsets)

    def run(p, ins, outs, scratch):
        hold, s, r, k = scratch
        own, spot = near(p, ins[0], outs[0])
        inward = copy(own, hold, k.at[0])
        copies = []
        for i, o in enumerate(offsets):
            t = dev(p, **o)
            src, dst = far(p, ins[0], outs[0], t)
            copies.append(send(src, dst, s.at[i], r.at[i], t))
        yield
        inward.wait()
        outward = copy(hold, spot, k.at[1])
        yield
        outward.wait()
        for c in copies:
            c.wait()

    return Op(
        [a], [out], [pltpu.VMEM(block.shape, block.dtype), sems(n), sems(n), sems(2)], offsets, run
    )


class _Shape:
    def __init__(self, value):
        self.value = value

    @property
    def at(self):
        return self

    def __getitem__(self, index):
        return _Shape(self.value[index])


def gather_x(a):
    out = ((2, 4) + a.shape[1:], a.dtype)

    def near(p, i, o):
        return i, (o.at[:, p["x"]] if not isinstance(o, _Shape) else None)

    return swap_op(a, out, X_OFF, near, lambda p, i, o, t: (i, o.at[:, p["x"]]))


def scatter_x(a):
    out = ((4, 2) + a.shape[2:], a.dtype)
    return swap_op(
        a,
        out,
        X_OFF,
        lambda p, i, o: (i.at[:, p["x"]], o.at[p["x"]]),
        lambda p, i, o, t: (i.at[:, t[2]], o.at[p["x"]]),
    )


def swap_ctx(a):
    return swap_op(
        a,
        (a.shape, a.dtype),
        CTX_OFF,
        lambda p, i, o: (i.at[p["ctx"]], o.at[p["ctx"]]),
        lambda p, i, o, t: (i.at[t[1]], o.at[p["ctx"]]),
    )


def heads_to_tokens(a):
    return swap_op(
        a,
        ((4, 2, 2) + a.shape[2:], a.dtype),
        SEQ_OFF,
        lambda p, i, o: (
            i.at[p["ctx"], p["x"]],
            None if isinstance(o, _Shape) else o.at[p["x"], p["core"], p["zhi"]],
        ),
        lambda p, i, o, t: (i.at[t[1], t[2]], o.at[p["x"], p["core"], p["zhi"]]),
    )


def tokens_to_heads(a):
    return swap_op(
        a,
        ((4, 4) + a.shape[3:], a.dtype),
        SEQ_OFF,
        lambda p, i, o: (
            i.at[p["x"], p["core"], p["zhi"]],
            None if isinstance(o, _Shape) else o.at[p["ctx"], p["x"]],
        ),
        lambda p, i, o, t: (
            i.at[t[2], lax.rem(t[1], 2), lax.div(t[1], 2)],
            o.at[p["ctx"], p["x"]],
        ),
    )


def all_places(a):
    return swap_op(
        a,
        ((4, 4) + a.shape, a.dtype),
        SEQ_OFF,
        lambda p, i, o: (i, None if isinstance(o, _Shape) else o.at[p["ctx"], p["x"]]),
        lambda p, i, o, t: (i, o.at[p["ctx"], p["x"]]),
    )


def all_shards(a):
    return swap_op(
        a,
        ((8, 4) + a.shape, a.dtype),
        SHARD_OFF,
        lambda p, i, o: (i, None if isinstance(o, _Shape) else o.at[p["dp"], p["ctx"]]),
        lambda p, i, o, t: (i, o.at[p["dp"], p["ctx"]]),
    )


def line_off(axis, which=(1, 3, 2)):
    return [{"d" + axis: d} for d in which]


def ag_first(shard, order):
    whole = ((4, 4, 2) + shard.shape, shard.dtype)

    def run(p, ins, outs, scratch):
        hold, s, r, k = scratch
        dst = outs[0].at[p["y"], z_slot(p["z"]), p["core"]]
        inward = copy(ins[0], hold, k.at[0])
        copies = [
            send(ins[0], dst, s.at[i], r.at[i], dev(p, **o))
            for i, o in enumerate(line_off(order[0]))
        ]
        yield
        inward.wait()
        outward = copy(hold, dst, k.at[1])
        yield
        outward.wait()
        for c in copies:
            c.wait()

    return Op(
        [shard],
        [whole],
        [pltpu.VMEM(shard.shape, shard.dtype), sems(3), sems(3), sems(2)],
        line_off(order[0]),
        run,
    )


def ag_second(whole, order, which=(1, 3, 2)):
    def run(p, ins, outs, scratch):
        s, r = scratch
        if order == "zy":
            block = outs[0].at[p["y"], :, p["core"]]
        else:
            block = outs[0].at[:, z_slot(p["z"]), p["core"]]
        copies = [
            send(block, block, s.at[i], r.at[i], dev(p, **o))
            for i, o in enumerate(line_off(order[1], which))
        ]
        yield
        yield
        for c in copies:
            c.wait()

    n = len(which)
    return Op(
        [whole],
        [(whole.shape, whole.dtype)],
        [sems(n), sems(n)],
        line_off(order[1], which),
        run,
        {0: 0},
    )


def ag_third(whole):
    def run(p, ins, outs, scratch):
        s, r = scratch
        block = outs[0].at[:, :, p["core"]]
        c = send(block, block, s.at[0], r.at[0], dev(p, dc=1))
        yield
        yield
        c.wait()

    return Op([whole], [(whole.shape, whole.dtype)], [sems(1), sems(1)], CORE_OFF, run, {0: 0})


def ag_all(shard, order):
    first = ag_first(shard, order)

    def run(p, ins, outs, scratch):
        yield from first.run(p, ins, outs, scratch[:4])
        yield from ag_second(jax.ShapeDtypeStruct(*first.outs[0]), order).run(
            p, outs, outs, scratch[4:6]
        )
        yield
        yield from ag_third(jax.ShapeDtypeStruct(*first.outs[0])).run(p, outs, outs, scratch[6:8])

    return Op(
        [shard],
        first.outs,
        first.scratch + [sems(3), sems(3), sems(1), sems(1)],
        first.offsets + line_off(order[1]) + CORE_OFF,
        run,
    )


def ag_rest(whole, order):
    second, third = ag_second(whole, order), ag_third(whole)

    def run(p, ins, outs, scratch):
        yield from second.run(p, ins, outs, scratch[:2])
        yield
        yield from third.run(p, ins, outs, scratch[2:])

    return Op(
        [whole],
        second.outs,
        second.scratch + third.scratch,
        second.offsets + CORE_OFF,
        run,
        {0: 0},
    )


def rs_cross(g):
    def run(p, ins, outs, scratch):
        s, r = scratch
        c = send(ins[0].at[:, :, 1 - p["core"]], outs[0], s.at[0], r.at[0], dev(p, dc=1))
        yield
        yield
        c.wait()

    return Op([g], [((4, 4) + g.shape[3:], g.dtype)], [sems(1), sems(1)], CORE_OFF, run)


def add_into(dst, terms, rows):
    def body(k, carry):
        at = pl.ds(pl.multiple_of(k * 16, 16), 16)
        for n in range(dst.shape[0]):
            total = terms[0][n, at].astype(F32)
            for t in terms[1:]:
                total = total + t[n, at].astype(F32)
            dst[n, at] = total.astype(BF)
        return carry

    lax.fori_loop(0, rows // 16, body, 0)


def along(p, axis, d):
    return lax.rem(p["y"] + d, 4) if axis == "y" else z_slot(lax.rem(p["z"] + d, 4))


def rs_line(g, crossed, order):
    rows, cols = g.shape[3:]
    chunk = (4, rows, cols)

    def run(p, ins, outs, scratch):
        mine, other, got, load, s, r, k = scratch
        loads = []
        for d in (1, 3, 2, 0):
            at = along(p, order[0], d)
            if order[0] == "y":
                a, b = ins[0].at[at, :, p["core"]], ins[1].at[at]
            else:
                a, b = ins[0].at[:, at, p["core"]], ins[1].at[:, at]
            loads.append(
                (d, copy(a, mine.at[d], load.at[d]), copy(b, other.at[d], load.at[4 + d]))
            )
        yield
        copies = []
        for d, a, b in loads:
            a.wait()
            b.wait()
            add_into(mine.at[d], [mine.at[d], other.at[d]], rows)
            if d:
                copies.append(
                    send(
                        mine.at[d],
                        got.at[d - 1],
                        s.at[d - 1],
                        r.at[d - 1],
                        dev(p, **{"d" + order[0]: d}),
                    )
                )
        yield
        yield
        for c in copies:
            c.wait()
        add_into(other.at[0], [mine.at[0], got.at[0], got.at[1], got.at[2]], rows)
        out = copy(other.at[0], outs[0], k.at[0])
        yield
        out.wait()

    return Op(
        [g, crossed],
        [(chunk, BF)],
        [
            pltpu.VMEM((4,) + chunk, BF),
            pltpu.VMEM((4,) + chunk, BF),
            pltpu.VMEM((3,) + chunk, BF),
            sems(8),
            sems(3),
            sems(3),
            sems(1),
        ],
        line_off(order[0]),
        run,
    )


def rs_last(part, order):
    rows, cols = part.shape[1:]

    def run(p, ins, outs, scratch):
        own, got, total, k, s, r, sx, rx = scratch
        load = copy(ins[0].at[pl.ds(along(p, order[1], 0), 1)], own, k.at[0])
        copies = []
        for i, o in enumerate(line_off(order[1])):
            d = o["d" + order[1]]
            copies.append(
                send(
                    ins[0].at[pl.ds(along(p, order[1], d), 1)],
                    got.at[i],
                    s.at[i],
                    r.at[i],
                    dev(p, **o),
                )
            )
        yield
        load.wait()
        yield
        for c in copies:
            c.wait()
        add_into(total, [own, got.at[0], got.at[1], got.at[2]], rows)
        dst = outs[0].at[pl.ds(p["x"], 1)]
        near = copy(total, dst, k.at[1])
        copies = [
            send(total, dst, sx.at[i], rx.at[i], dev(p, **o)) for i, o in enumerate(X_OFF)
        ]
        yield
        near.wait()
        for c in copies:
            c.wait()

    one = (1, rows, cols)
    return Op(
        [part],
        [((4, rows, cols), BF)],
        [
            pltpu.VMEM(one, BF),
            pltpu.VMEM((3,) + one, BF),
            pltpu.VMEM(one, BF),
            sems(2),
            sems(3),
            sems(3),
            sems(3),
            sems(3),
        ],
        line_off(order[1]) + X_OFF,
        run,
    )


def sum_all(a):
    shape = a.shape
    axes = ("dx", "dy", "dz")

    def run(p, ins, outs, scratch):
        acc, got, k, s, r = scratch
        copy(ins[0], acc.at[0], k.at[0]).wait()
        for n, axis in enumerate(axes):
            copies = [
                send(
                    acc.at[n],
                    got.at[3 * n + d - 1],
                    s.at[3 * n + d - 1],
                    r.at[3 * n + d - 1],
                    dev(p, **{axis: d}),
                )
                for d in (1, 2, 3)
            ]
            yield
            for c in copies:
                c.wait()
            acc[n + 1] = acc[n] + got[3 * n] + got[3 * n + 1] + got[3 * n + 2]
        c = send(acc.at[3], got.at[9], s.at[9], r.at[9], dev(p, dc=1))
        yield
        c.wait()
        acc[4] = acc[3] + got[9]
        copy(acc.at[4], outs[0], k.at[0]).wait()

    return Op(
        [a],
        [(shape, F32)],
        [pltpu.VMEM((5,) + shape, F32), pltpu.VMEM((10,) + shape, F32), sems(1), sems(10), sems(10)],
        X_OFF + Y_OFF + Z_OFF + CORE_OFF,
        run,
    )


def pick(a, index, axis):
    return lax.dynamic_index_in_dim(a, index, axis, keepdims=False)


def rotated(y, cosine, sine):
    lane = lax.broadcasted_iota(jnp.int32, y.shape, 1)
    low = lax.rem(lane, HEAD) < HEAD // 2
    width = y.shape[1]
    turned = jnp.where(low, pltpu.roll(y, width - HEAD // 2, 1), pltpu.roll(y, HEAD // 2, 1))
    return y * cosine + turned * sine


def qkv_kernel(x_ref, w_ref, cos_ref, sin_ref, o_ref):
    for u in range(2):
        for s in range(2):
            rows = pl.ds(s * 256, 256)
            y = jnp.dot(
                x_ref[rows], w_ref[:, u * 384 : (u + 1) * 384], preferred_element_type=F32
            )
            o_ref[s * 2 + u] = rotated(y, cos_ref[rows], sin_ref[rows]).astype(BF)


def project(x, w, cosine, sine):
    return pl.pallas_call(
        qkv_kernel,
        out_shape=jax.ShapeDtypeStruct((4, 256, 384), BF),
        compiler_params=pltpu.CompilerParams(vmem_limit_bytes=VMEM_LIMIT),
        cost_estimate=pl.CostEstimate(flops=1208 * 10**6, bytes_accessed=6 * 10**6, transcendentals=0),
    )(x, w, cosine, sine)


def contract(a, b, da, db):
    return lax.dot_general(a, b, (((da,), (db,)), ((), ())), preferred_element_type=F32)


SCALE = HEAD ** (-0.5)


def masked(st, i):
    width = st.shape[0]
    key = lax.broadcasted_iota(jnp.int32, (256, 256), 0)
    query = lax.broadcasted_iota(jnp.int32, (256, 256), 1)
    last = jnp.where(key <= query, st[width - 256 :], NEG)
    return last if width == 256 else jnp.concatenate([st[: width - 256], last], axis=0)


def attend_kernel(qkv_ref, o_ref, lse_ref):
    for i in range(4):
        rows = pl.ds(i * 256, 256)
        width = (i + 1) * 256
        k = qkv_ref[:width, 2 * HEAD : 3 * HEAD]
        v = qkv_ref[:width, 3 * HEAD : 4 * HEAD]
        outs = []
        for n in range(2):
            q = qkv_ref[rows, n * HEAD : (n + 1) * HEAD]
            st = masked(contract(k, q, 1, 1) * SCALE, i)
            top = jnp.max(st, axis=0, keepdims=True)
            e = jnp.exp(st - top)
            total = jnp.sum(e, axis=0, keepdims=True)
            ot = contract(v, e.astype(BF), 0, 0)
            outs.append(ot * (1.0 / total))
            lse_ref[n : n + 1, rows] = top + jnp.log(total)
        o_ref[rows] = jnp.concatenate(outs, axis=0).T.astype(BF)


def attend(qkv):
    return pl.pallas_call(
        attend_kernel,
        out_shape=[jax.ShapeDtypeStruct((1024, 192), BF), jax.ShapeDtypeStruct((2, 1024), F32)],
        compiler_params=pltpu.CompilerParams(vmem_limit_bytes=VMEM_LIMIT),
        cost_estimate=pl.CostEstimate(flops=10**9, bytes_accessed=10**6, transcendentals=1310720),
    )(qkv)


def attend_back_kernel(qkv_ref, do_ref, lse_ref, cos_ref, sin_ref, o_ref, dq_ref, dk_ref, dv_ref):
    dk_ref[...] = jnp.zeros_like(dk_ref)
    dv_ref[...] = jnp.zeros_like(dv_ref)
    for i in range(4):
        rows = pl.ds(i * 256, 256)
        width = (i + 1) * 256
        k = qkv_ref[:width, 2 * HEAD : 3 * HEAD]
        v = qkv_ref[:width, 3 * HEAD : 4 * HEAD]
        for n in range(2):
            q = qkv_ref[rows, n * HEAD : (n + 1) * HEAD]
            do = do_ref[rows, n * HEAD : (n + 1) * HEAD]
            st = masked(contract(k, q, 1, 1) * SCALE, i)
            p = jnp.exp(st - lse_ref[n : n + 1, rows])
            dpt = contract(v, do, 1, 1)
            delta = jnp.sum(p * dpt, axis=0, keepdims=True)
            ds = (p * (dpt - delta)).astype(BF)
            dq_ref[n * HEAD : (n + 1) * HEAD, rows] = contract(k, ds, 0, 0)
            dk_ref[:width] += jnp.dot(ds, q, preferred_element_type=F32)
            dv_ref[:width] += jnp.dot(p.astype(BF), do, preferred_element_type=F32)
    for i in range(4):
        rows = pl.ds(i * 256, 256)
        g = jnp.concatenate(
            [dq_ref[:, rows].T * SCALE, dk_ref[rows] * SCALE, dv_ref[rows]], axis=1
        )
        g = g.astype(BF).astype(F32)
        o_ref[rows] = rotated(g, cos_ref[rows], -sin_ref[rows]).astype(BF)


def attend_back(qkv, do, lse, cosine, sine):
    return pl.pallas_call(
        attend_back_kernel,
        out_shape=jax.ShapeDtypeStruct((1024, 384), BF),
        scratch_shapes=[
            pltpu.VMEM((192, 1024), F32),
            pltpu.VMEM((1024, HEAD), F32),
            pltpu.VMEM((1024, HEAD), F32),
        ],
        compiler_params=pltpu.CompilerParams(vmem_limit_bytes=VMEM_LIMIT),
        cost_estimate=pl.CostEstimate(flops=3 * 10**9, bytes_accessed=10**6, transcendentals=1310720),
    )(qkv, do, lse, cosine, sine)


def out_kernel(m_ref, w_ref, hidden_ref, gain_ref, res_ref, norm_ref, scale_ref, tok_ref):
    tok_ref[...] = jnp.concatenate([m_ref[g] for g in range(8)], axis=1)
    for c in range(3):
        cols = slice(c * 512, (c + 1) * 512)
        res_ref[:, cols] = hidden_ref[:, cols] + jnp.dot(
            tok_ref[...], w_ref[:, cols], preferred_element_type=F32
        )
    res = res_ref[...]
    scale = lax.rsqrt(jnp.mean(res * res, axis=-1, keepdims=True) + EPS)
    scale_ref[...] = scale
    norm_ref[...] = (res * scale * gain_ref[...]).astype(BF)


def out_project(m, w, hidden, gain):
    return pl.pallas_call(
        out_kernel,
        out_shape=[
            jax.ShapeDtypeStruct((128, D), F32),
            jax.ShapeDtypeStruct((128, D), BF),
            jax.ShapeDtypeStruct((128, 1), F32),
            jax.ShapeDtypeStruct((128, D), BF),
        ],
        compiler_params=pltpu.CompilerParams(vmem_limit_bytes=VMEM_LIMIT),
        cost_estimate=pl.CostEstimate(flops=604 * 10**6, bytes_accessed=7 * 10**6, transcendentals=0),
    )(m, w, hidden, gain)


def rope_columns(positions):
    half = HEAD // 2
    frequency = BASE ** (-(jnp.arange(half, dtype=F32) * 2.0 / HEAD))
    angles = positions.astype(F32)[:, None] * frequency
    cosine, sine = jnp.cos(angles), jnp.sin(angles)
    one, zero = jnp.ones_like(cosine), jnp.zeros_like(sine)
    return (
        jnp.concatenate([cosine] * 6 + [one] * 2, axis=1),
        jnp.concatenate([-sine, sine] * 3 + [zero] * 2, axis=1),
    )


def norm(hidden, gain):
    scale = lax.rsqrt(jnp.mean(hidden * hidden, axis=-1, keepdims=True) + EPS)
    return (hidden * scale * gain).astype(BF), scale


def norm_back(hidden, scale, gain, upstream):
    unit = hidden * scale
    gain_grad = jnp.sum(upstream * unit, axis=0)
    weighted = upstream * gain
    return (
        scale * (weighted - unit * jnp.mean(weighted * unit, axis=-1, keepdims=True)),
        gain_grad,
    )


def dot(a, b):
    return jnp.dot(a, b, preferred_element_type=F32)


def dot_t(a, b):
    return contract(a, b, 1, 1)


def t_dot(a, b):
    return contract(a, b, 0, 0)


def ff_quarter(a, x):
    rows = a.shape[0]
    return pick(a.reshape(rows, 32, 4, 32), x, 2).reshape(rows, 1024)


def pack_qkv(q, k, v, x):
    rows = q.shape[0]
    q = lax.dynamic_slice_in_dim(q, x * 384, 384, 1).reshape(rows, 2, 192)
    k = lax.dynamic_slice_in_dim(k, x * 192, 192, 1).reshape(rows, 2, 96)
    v = lax.dynamic_slice_in_dim(v, x * 192, 192, 1).reshape(rows, 2, 96)
    return jnp.concatenate([q, k, v], axis=2).reshape(rows, 768)


def per_device(
    inputs,
    positions,
    cotangent,
    attn_gain,
    query_weight,
    key_matrix,
    value_matrix,
    out_weight,
    mlp_gain,
    gate_weight,
    up_weight,
    down_weight,
):
    p = place()
    x = p["x"]

    shards = []
    for l in range(LAYERS):
        gu = jnp.concatenate([ff_quarter(gate_weight[l], x), ff_quarter(up_weight[l], x)], axis=1)
        down = lax.dynamic_slice_in_dim(down_weight[l], x * 32, 32, 0)
        qkv = pack_qkv(query_weight[l], key_matrix[l], value_matrix[l], x)
        shards.append((qkv, out_weight[l], down, gu))
    orders = ("zy", "yz", "yz", "zy")

    gains = jnp.zeros((8, 128), F32)
    gains = gains.at[:2, :48].set(attn_gain.astype(F32)).at[2:4, :48].set(mlp_gain.astype(F32))
    places = jnp.broadcast_to(positions.reshape(1, 128), (8, 128))
    first = build(
        1,
        [gather_x(inputs), all_places(places), all_shards(gains)]
        + [ag_all(s, o) for s, o in zip(shards[0], orders)],
    )
    ((tokens_g,), (places_g,), (gains_g,)) = first[:3]
    whole = [[w[0] for w in first[3:]], None]
    gains_all = gains_g.reshape(32, 8, 128)[:, :4, :48].transpose(1, 0, 2).reshape(4, 1, D)
    place_all = places_g[:, :, 0, :].reshape(4, 4, 2, 64)
    cos_c, sin_c = rope_columns(pick(place_all, p["ctx"], 0).transpose(1, 0, 2).reshape(512))
    cos_s, sin_s = rope_columns(pick(place_all, p["zhi"], 2).reshape(1024))

    def stage(ws, order_list, f):
        return [f(w, o) for w, o in zip(ws, order_list)]

    hidden = inputs.reshape(128, D).astype(F32)
    saved = []
    for l in range(LAYERS):
        if l == 0:
            normed_g, _ = norm(tokens_g.reshape(512, D).astype(F32), gains_all[0])
            scale_one = lax.rsqrt(jnp.mean(hidden * hidden, axis=-1, keepdims=True) + EPS)
        else:
            normed, scale_one = norm(hidden, gains_all[l])
            (ng,), *rest = build(
                2,
                [gather_x(normed.reshape(2, 64, D))]
                + [ag_second(w, o, (2,)) for w, o in zip(whole[1][1:], orders[1:])],
            )
            whole[1][1:] = [w[0] for w in rest]
            normed_g = ng.reshape(512, D)
        w_qkv = whole[l][0].reshape(D, 768)
        units = project(normed_g, w_qkv, cos_c, sin_c)
        if l == 0:
            ((qkv,),) = build(3, [swap_ctx(units)])
        else:
            (qkv,), *rest = build(4, [swap_ctx(units)] + [ag_third(w) for w in whole[1][1:]])
            whole[1][1:] = [w[0] for w in rest]
        qkv = qkv.reshape(1024, 384)
        mixed, lse = attend(qkv)
        ((mixed_t,),) = build(5, [heads_to_tokens(mixed.reshape(4, 4, 64, 192))])
        w_out, w_down, w_gu = whole[l][1:]
        w_out, w_down, w_gu = w_out.reshape(D, D), w_down.reshape(1024, D), w_gu.reshape(D, 2048)
        residual, normed_two, scale_two, mixed_tok = out_project(
            mixed_t.reshape(8, 128, 192), w_out, hidden, gains_all[2 + l]
        )
        fg = gather_x(normed_two.reshape(2, 64, D))
        if l == 0:
            (ng,), *rest = build(6, [fg] + [ag_first(s, o) for s, o in zip(shards[1], orders)])
            whole[1] = [w[0] for w in rest]
        else:
            ((ng,),) = build(7, [fg])
        normed_two_g = ng.reshape(512, D)
        gate_up = dot(normed_two_g, w_gu)
        gate, up = gate_up[:, :1024], gate_up[:, 1024:]
        activ = (jax.nn.silu(gate) * up).astype(BF)
        partial = dot(activ, w_down).astype(BF)
        fg = scatter_x(partial.reshape(2, 4, 64, D))
        if l == 0:
            (terms,), *rest = build(
                8,
                [fg, ag_rest(whole[1][0], "zy")]
                + [ag_second(w, o, (1, 3)) for w, o in zip(whole[1][1:], orders[1:])],
            )
            whole[1] = [w[0] for w in rest]
        else:
            ((terms,),) = build(9, [fg])
        saved.append(
            (
                hidden, normed_g, scale_one, qkv, lse, mixed_tok, residual, normed_two_g, scale_two,
                gate_up, activ, w_qkv, w_out, w_down, w_gu,
            )
        )
        hidden = residual + jnp.sum(terms.astype(F32), axis=0).reshape(128, D)
    output = hidden.astype(BF).reshape(2, 64, D)

    gradient = cotangent.reshape(128, D).astype(F32)
    ends = [[None] * 4 for _ in range(LAYERS)]
    gain_grads = [None] * 4
    later = None
    for l in reversed(range(LAYERS)):
        (
            hidden, normed_g, scale_one, qkv, lse, mixed_tok, residual, normed_two_g, scale_two,
            gate_up, activ, w_qkv, w_out, w_down, w_gu,
        ) = saved[l]
        grad_b = cotangent if l == LAYERS - 1 else gradient.astype(BF).reshape(2, 64, D)
        fg = gather_x(grad_b)
        if l == 1:
            ((gb,),) = build(7, [fg])
        else:
            g_out1, c_out1, g_qkv1, part_gu1, part_down1 = later
            (gb,), (part_out1,), (c_qkv1,) = build(
                10, [fg, rs_line(g_out1, c_out1, "yz"), rs_cross(g_qkv1)]
            )
        grad_b_g = gb.reshape(512, D)
        grad_act = dot_t(grad_b_g, w_down)
        gate, up = gate_up[:, :1024], gate_up[:, 1024:]
        sigma = jax.nn.sigmoid(gate)
        grad_gate = (grad_act * up * sigma * (1.0 + gate * (1.0 - sigma))).astype(BF)
        grad_up = (grad_act * gate * sigma).astype(BF)
        grad_gu = jnp.concatenate([grad_gate, grad_up], axis=1)
        partial = dot_t(grad_gu, w_gu).astype(BF)
        fg = scatter_x(partial.reshape(2, 4, 64, D))
        if l == 1:
            ((terms,),) = build(9, [fg])
        else:
            (terms,), (part_qkv1,), (ends[1][2],) = build(
                11, [fg, rs_line(g_qkv1, c_qkv1, "zy"), rs_last(part_down1, "yz")]
            )
        g_down = t_dot(activ, grad_b_g).astype(BF).reshape(4, 4, 2, 32, D)
        g_gu = t_dot(normed_two_g, grad_gu).astype(BF).reshape(4, 4, 2, 48, 2048)
        grad_normed = jnp.sum(terms.astype(F32), axis=0).reshape(128, D)
        back, gain_grads[2 + l] = norm_back(residual, scale_two, gains_all[2 + l], grad_normed)
        grad_res = gradient + back
        grad_rb = grad_res.astype(BF)
        grad_mix = dot_t(grad_rb, w_out).astype(BF)
        grad_mix = grad_mix.reshape(128, 8, 192).transpose(1, 0, 2).reshape(4, 2, 2, 64, 192)
        fg = tokens_to_heads(grad_mix)
        if l == 1:
            (gm,), (c_down,), (c_gu,) = build(12, [fg, rs_cross(g_down), rs_cross(g_gu)])
        else:
            (gm,), (c_down,), (c_gu,), (ends[1][3],), (ends[1][1],) = build(
                13,
                [fg, rs_cross(g_down), rs_cross(g_gu), rs_last(part_gu1, "zy"), rs_last(part_out1, "yz")],
            )
        g_out = t_dot(mixed_tok, grad_rb).astype(BF).reshape(4, 4, 2, 48, D)
        grad_units = attend_back(qkv, gm.reshape(1024, 192), lse, cos_s, sin_s)
        fg = swap_ctx(grad_units.reshape(4, 256, 384))
        (gu4,), (part_down,), (c_out,) = build(
            14, [fg, rs_line(g_down, c_down, "yz"), rs_cross(g_out)]
        )
        grad_qkv = gu4.reshape(2, 2, 256, 384).transpose(0, 2, 1, 3).reshape(512, 768)
        partial = dot_t(grad_qkv, w_qkv).astype(BF)
        fg = scatter_x(partial.reshape(2, 4, 64, D))
        g_qkv = t_dot(normed_g, grad_qkv).astype(BF).reshape(4, 4, 2, 48, 768)
        if l == 1:
            (terms,), (part_gu,) = build(15, [fg, rs_line(g_gu, c_gu, "zy")])
            later = (g_out, c_out, g_qkv, part_gu, part_down)
        else:
            (terms,), (part_gu,), (c_qkv,) = build(
                16, [fg, rs_line(g_gu, c_gu, "zy"), rs_cross(g_qkv)]
            )
        grad_normed = jnp.sum(terms.astype(F32), axis=0).reshape(128, D)
        back, gain_grads[l] = norm_back(hidden, scale_one, gains_all[l], grad_normed)
        gradient = grad_res + back

    sums = jnp.zeros((8, D), F32).at[:4].set(jnp.stack(gain_grads))
    (part_qkv,), (part_out,), (ends[0][2],), (ends[0][3],), (ends[1][0],), (gain_sum,) = build(
        17,
        [
            rs_line(g_qkv, c_qkv, "zy"),
            rs_line(g_out, c_out, "yz"),
            rs_last(part_down, "yz"),
            rs_last(part_gu, "zy"),
            rs_last(part_qkv1, "zy"),
            sum_all(sums),
        ],
    )
    (ends[0][0],), (ends[0][1],) = build(18, [rs_last(part_qkv, "zy"), rs_last(part_out, "yz")])

    reduced = []
    for l in range(LAYERS):
        a_qkv, s_out, a_down, a_gu = ends[l]
        a_gu = a_gu.reshape(4, 48, 2, 32, 32).transpose(2, 1, 3, 0, 4).reshape(2, 48, 4096).astype(F32)
        a_qkv = a_qkv.reshape(4, 48, 2, 384).transpose(1, 0, 2, 3).astype(F32)
        reduced.append(
            (
                a_qkv[..., :192].reshape(48, D),
                a_qkv[..., 192:288].reshape(48, 768),
                a_qkv[..., 288:].reshape(48, 768),
                jnp.sum(s_out.astype(F32), axis=0),
                a_gu[0],
                a_gu[1],
                a_down.reshape(128, D).astype(F32),
            )
        )

    block = p["dp"] * 4 + p["ctx"]
    gain_own = pick(gain_sum[:4].reshape(4, 32, 48), block, 1)
    stacked = [jnp.stack([reduced[l][k] for l in range(LAYERS)]) for k in range(7)]
    return (
        output,
        gradient.reshape(2, 64, D),
        gain_own[:2],
        stacked[0],
        stacked[1],
        stacked[2],
        stacked[3],
        gain_own[2:],
        stacked[4],
        stacked[5],
        stacked[6],
    )


def solution(mesh):
    tokens = P("dp", ("ctx", "head"), None)
    vector = P(None, ("dp", "ctx"))
    matrix = P(None, ("dp", "ctx"), None)
    return jax.shard_map(
        per_device,
        mesh=mesh,
        in_specs=(
            tokens,
            P("dp", ("ctx", "head")),
            tokens,
            vector,
            matrix,
            matrix,
            matrix,
            matrix,
            vector,
            matrix,
            matrix,
            matrix,
        ),
        out_specs=(
            tokens,
            tokens,
            vector,
            matrix,
            matrix,
            matrix,
            matrix,
            vector,
            matrix,
            matrix,
            matrix,
        ),
        check_vma=False,
    )
```

```python
import functools

import jax
import jax.numpy as jnp
from jax import lax
from jax.experimental import pallas as pl
from jax.experimental.pallas import tpu as pltpu
from jax.sharding import PartitionSpec as P

HEAD = 96
LAYERS = 2
D = 1536
EPS = 1e-05
BASE = 100000.0
NEG = -1e30
F32 = jnp.float32
BF = jnp.bfloat16
MESH = pl.DeviceIdType.MESH
VMEM_LIMIT = 56 * 1024 * 1024


def place():
    dp, ctx, head = lax.axis_index("dp"), lax.axis_index("ctx"), lax.axis_index("head")
    y, zlo = lax.div(dp, 2), lax.rem(dp, 2)
    zhi, core = lax.div(ctx, 2), lax.rem(ctx, 2)
    return dict(dp=dp, ctx=ctx, x=head, y=y, zlo=zlo, zhi=zhi, core=core, z=zhi * 2 + zlo)


def dev(p, dx=0, dy=0, dz=0, dc=0):
    x = lax.rem(p["x"] + dx, 4)
    y = lax.rem(p["y"] + dy, 4)
    z = lax.rem(p["z"] + dz, 4)
    core = lax.rem(p["core"] + dc, 2)
    return (y * 2 + lax.rem(z, 2), lax.div(z, 2) * 2 + core, x)


def z_slot(z):
    return lax.rem(z, 2) * 2 + lax.div(z, 2)


class Op:
    def __init__(self, ins, outs, scratch, offsets, run, alias=()):
        self.ins, self.outs, self.scratch = list(ins), list(outs), list(scratch)
        self.offsets, self.run, self.alias = offsets, run, dict(alias)


class From:
    def __init__(self, op, k=0):
        self.op, self.k = op, k
        self.shape, self.dtype = op.outs[k]


def sems(n):
    return pltpu.SemaphoreType.DMA((n,))


def build(cid, ops):
    ins = [a for op in ops for a in op.ins if not isinstance(a, From)]
    outs = [o for op in ops for o in op.outs]
    scratch = [s for op in ops for s in op.scratch]
    offsets, alias, i0, o0 = [], {}, 0, 0
    for op in ops:
        for o in op.offsets:
            key = tuple(o.get(k, 0) for k in ("dx", "dy", "dz", "dc"))
            if key not in offsets:
                offsets.append(key)
        for i, o in op.alias.items():
            alias[i0 + i] = o0 + o
        i0 += sum(not isinstance(a, From) for a in op.ins)
        o0 += len(op.outs)
    n_in, n_out = len(ins), len(outs)

    def kernel(*refs):
        p = place()
        if offsets:
            barrier = pltpu.get_barrier_semaphore()
            for o in offsets:
                pl.semaphore_signal(barrier, inc=1, device_id=dev(p, *o), device_id_type=MESH)
            pl.semaphore_wait(barrier, len(offsets))
        i, o, s = 0, n_in, n_in + n_out
        runs, results = [], {}
        for op in ops:
            own = []
            for a in op.ins:
                if isinstance(a, From):
                    own.append(results[id(a.op)][a.k])
                else:
                    own.append(refs[i])
                    i += 1
            results[id(op)] = refs[o : o + len(op.outs)]
            runs.append(op.run(p, own, results[id(op)], refs[s : s + len(op.scratch)]))
            o, s = o + len(op.outs), s + len(op.scratch)
        while runs:
            live = []
            for r in runs:
                try:
                    next(r)
                    live.append(r)
                except StopIteration:
                    pass
            runs = live

    results = pl.pallas_call(
        kernel,
        out_shape=[jax.ShapeDtypeStruct(s, d) for s, d in outs],
        in_specs=[pl.BlockSpec(memory_space=pl.ANY)] * n_in,
        out_specs=[pl.BlockSpec(memory_space=pl.ANY)] * n_out,
        scratch_shapes=scratch,
        input_output_aliases=alias,
        compiler_params=pltpu.CompilerParams(
            collective_id=cid, has_side_effects=True, vmem_limit_bytes=VMEM_LIMIT
        ),
    )(*ins)
    split = []
    for op in ops:
        split.append(list(results[: len(op.outs)]))
        results = results[len(op.outs) :]
    return split


def idle(n):
    for _ in range(n):
        yield


def timed(op, *rounds):
    def run(*refs):
        steps = op.run(*refs)
        now = 0
        for r in rounds:
            yield from idle(r - now)
            now = r
            try:
                next(steps)
            except StopIteration:
                return
        yield
        for _ in steps:
            yield

    return Op(op.ins, op.outs, op.scratch, op.offsets, run, op.alias)


def chain(*ops):
    def run(p, ins, outs, scratch):
        for n, op in enumerate(ops):
            yield from op.run(p, ins if n == 0 else outs, outs, scratch[: len(op.scratch)])
            scratch = scratch[len(op.scratch) :]

    first = ops[0]
    return Op(
        first.ins,
        first.outs,
        [c for op in ops for c in op.scratch],
        [f for op in ops for f in op.offsets],
        run,
        first.alias,
    )


def send(src, dst, send_sem, recv_sem, target):
    c = pltpu.make_async_remote_copy(
        src_ref=src,
        dst_ref=dst,
        send_sem=send_sem,
        recv_sem=recv_sem,
        device_id=target,
        device_id_type=MESH,
    )
    c.start()
    return c


def copy(src, dst, sem):
    c = pltpu.make_async_copy(src, dst, sem)
    c.start()
    return c


X_OFF = [dict(dx=d) for d in (1, 3, 2)]
Y_OFF = [dict(dy=d) for d in (1, 3, 2)]
Z_OFF = [dict(dz=d) for d in (1, 3, 2)]
CORE_OFF = [dict(dc=1)]
CTX_OFF = [dict(dz=2, dc=0), dict(dz=2, dc=1), dict(dz=0, dc=1)]
SEQ_OFF = [
    dict(dx=dx, dz=dz, dc=dc) for dx in range(4) for dz in (0, 2) for dc in (0, 1)
][1:]
SHARD_OFF = [
    dict(dy=dy, dz=dz, dc=dc) for dy in range(4) for dz in range(4) for dc in (0, 1)
][1:]


def swap_op(a, out, offsets, near, far):
    block = jax.eval_shape(
        lambda v: near(dict(ctx=0, x=0, core=0, zhi=0), _Shape(v), _Shape(v))[0].value, a
    )
    n = len(offsets)

    def run(p, ins, outs, scratch):
        hold, s, r, k = scratch
        own, spot = near(p, ins[0], outs[0])
        inward = copy(own, hold, k.at[0])
        copies = []
        for i, o in enumerate(offsets):
            t = dev(p, **o)
            src, dst = far(p, ins[0], outs[0], t)
            copies.append(send(src, dst, s.at[i], r.at[i], t))
        inward.wait()
        outward = copy(hold, spot, k.at[1])
        yield
        outward.wait()
        for c in copies:
            c.wait()

    return Op(
        [a], [out], [pltpu.VMEM(block.shape, block.dtype), sems(n), sems(n), sems(2)], offsets, run
    )


class _Shape:
    def __init__(self, value):
        self.value = value

    @property
    def at(self):
        return self

    def __getitem__(self, index):
        return _Shape(self.value[index])


def gather_x(a):
    out = ((2, 4) + a.shape[1:], a.dtype)

    def near(p, i, o):
        return i, (o.at[:, p["x"]] if not isinstance(o, _Shape) else None)

    return swap_op(a, out, X_OFF, near, lambda p, i, o, t: (i, o.at[:, p["x"]]))


def scatter_x(a):
    out = ((4, 2) + a.shape[2:], a.dtype)
    return swap_op(
        a,
        out,
        X_OFF,
        lambda p, i, o: (i.at[:, p["x"]], o.at[p["x"]]),
        lambda p, i, o, t: (i.at[:, t[2]], o.at[p["x"]]),
    )


def swap_ctx(a):
    return swap_op(
        a,
        (a.shape, a.dtype),
        CTX_OFF,
        lambda p, i, o: (i.at[p["ctx"]], o.at[p["ctx"]]),
        lambda p, i, o, t: (i.at[t[1]], o.at[p["ctx"]]),
    )


def heads_to_tokens(a):
    return swap_op(
        a,
        ((4, 2, 2) + a.shape[2:], a.dtype),
        SEQ_OFF,
        lambda p, i, o: (
            i.at[p["ctx"], p["x"]],
            None if isinstance(o, _Shape) else o.at[p["x"], p["core"], p["zhi"]],
        ),
        lambda p, i, o, t: (i.at[t[1], t[2]], o.at[p["x"], p["core"], p["zhi"]]),
    )


def tokens_to_heads(a):
    return swap_op(
        a,
        ((4, 4) + a.shape[3:], a.dtype),
        SEQ_OFF,
        lambda p, i, o: (
            i.at[p["x"], p["core"], p["zhi"]],
            None if isinstance(o, _Shape) else o.at[p["ctx"], p["x"]],
        ),
        lambda p, i, o, t: (
            i.at[t[2], lax.rem(t[1], 2), lax.div(t[1], 2)],
            o.at[p["ctx"], p["x"]],
        ),
    )


def rows_x(a):
    return swap_op(
        a,
        ((4,) + a.shape, a.dtype),
        X_OFF,
        lambda p, i, o: (i, None if isinstance(o, _Shape) else o.at[p["x"]]),
        lambda p, i, o, t: (i, o.at[p["x"]]),
    )


def all_shards(a):
    return swap_op(
        a,
        ((8, 4) + a.shape, a.dtype),
        SHARD_OFF,
        lambda p, i, o: (i, None if isinstance(o, _Shape) else o.at[p["dp"], p["ctx"]]),
        lambda p, i, o, t: (i, o.at[p["dp"], p["ctx"]]),
    )


def line_off(axis, which=(1, 3, 2)):
    return [{"d" + axis: d} for d in which]


def ag_first(shard, order):
    whole = ((4, 4, 2) + shard.shape, shard.dtype)

    def run(p, ins, outs, scratch):
        hold, s, r, k = scratch
        dst = outs[0].at[p["y"], z_slot(p["z"]), p["core"]]
        inward = copy(ins[0], hold, k.at[0])
        copies = [
            send(ins[0], dst, s.at[i], r.at[i], dev(p, **o))
            for i, o in enumerate(line_off(order[0]))
        ]
        inward.wait()
        outward = copy(hold, dst, k.at[1])
        yield
        outward.wait()
        for c in copies:
            c.wait()

    return Op(
        [shard],
        [whole],
        [pltpu.VMEM(shard.shape, shard.dtype), sems(3), sems(3), sems(2)],
        line_off(order[0]),
        run,
    )


def ag_second(whole, order, which=(1, 3, 2)):
    def run(p, ins, outs, scratch):
        s, r = scratch
        if order == "zy":
            block = outs[0].at[p["y"], :, p["core"]]
        else:
            block = outs[0].at[:, z_slot(p["z"]), p["core"]]
        copies = [
            send(block, block, s.at[i], r.at[i], dev(p, **o))
            for i, o in enumerate(line_off(order[1], which))
        ]
        yield
        for c in copies:
            c.wait()

    n = len(which)
    return Op(
        [whole],
        [(whole.shape, whole.dtype)],
        [sems(n), sems(n)],
        line_off(order[1], which),
        run,
        {0: 0},
    )


def ag_third(whole):
    def run(p, ins, outs, scratch):
        s, r = scratch
        block = outs[0].at[:, :, p["core"]]
        c = send(block, block, s.at[0], r.at[0], dev(p, dc=1))
        yield
        c.wait()

    return Op([whole], [(whole.shape, whole.dtype)], [sems(1), sems(1)], CORE_OFF, run, {0: 0})


def ag_all(shard, order):
    first = ag_first(shard, order)
    whole = jax.ShapeDtypeStruct(*first.outs[0])
    return chain(first, ag_second(whole, order), ag_third(whole))


def _whole(shard):
    return jax.ShapeDtypeStruct((4, 4, 2) + shard.shape, shard.dtype)


def ag_rest(whole, order):
    return chain(ag_second(whole, order), ag_third(whole))


def add_into(dst, terms, rows):
    def body(k, carry):
        at = pl.ds(pl.multiple_of(k * 16, 16), 16)
        for n in range(dst.shape[0]):
            total = terms[0][n, at].astype(F32)
            for t in terms[1:]:
                total = total + t[n, at].astype(F32)
            dst[n, at] = total.astype(BF)
        return carry

    lax.fori_loop(0, rows // 16, body, 0)


def along(p, axis, d):
    return lax.rem(p["y"] + d, 4) if axis == "y" else z_slot(lax.rem(p["z"] + d, 4))


def rs_line(g, crossed, order):
    rows, cols = g.shape[2:]
    chunk = (4, rows, cols)

    def run(p, ins, outs, scratch):
        mine, other, got, load, s, r, k = scratch
        loads = []
        for d in (1, 3, 2, 0):
            at = along(p, order[0], d)
            if order[0] == "y":
                a, b = ins[0].at[at], ins[1].at[at]
            else:
                a, b = ins[0].at[:, at], ins[1].at[:, at]
            loads.append(
                (d, copy(a, mine.at[d], load.at[d]), copy(b, other.at[d], load.at[4 + d]))
            )
        copies = []
        for d, a, b in loads:
            a.wait()
            b.wait()
            add_into(mine.at[d], [mine.at[d], other.at[d]], rows)
            if d:
                copies.append(
                    send(
                        mine.at[d],
                        got.at[d - 1],
                        s.at[d - 1],
                        r.at[d - 1],
                        dev(p, **{"d" + order[0]: d}),
                    )
                )
        yield
        for c in copies:
            c.wait()
        add_into(other.at[0], [mine.at[0], got.at[0], got.at[1], got.at[2]], rows)
        out = copy(other.at[0], outs[0], k.at[0])
        yield
        out.wait()

    return Op(
        [g, crossed],
        [(chunk, BF)],
        [
            pltpu.VMEM((4,) + chunk, BF),
            pltpu.VMEM((4,) + chunk, BF),
            pltpu.VMEM((3,) + chunk, BF),
            sems(8),
            sems(3),
            sems(3),
            sems(1),
        ],
        line_off(order[0]),
        run,
    )


def rs_second(part, order):
    rows, cols = part.shape[1:]
    one = (1, rows, cols)

    def run(p, ins, outs, scratch):
        own, got, total, k, s, r = scratch
        load = copy(ins[0].at[pl.ds(along(p, order[1], 0), 1)], own, k.at[0])
        copies = []
        for i, o in enumerate(line_off(order[1])):
            d = o["d" + order[1]]
            copies.append(
                send(
                    ins[0].at[pl.ds(along(p, order[1], d), 1)],
                    got.at[i],
                    s.at[i],
                    r.at[i],
                    dev(p, **o),
                )
            )
        yield
        load.wait()
        for c in copies:
            c.wait()
        add_into(total, [own, got.at[0], got.at[1], got.at[2]], rows)
        out = copy(total, outs[0], k.at[1])
        yield
        out.wait()

    return Op(
        [part],
        [(one, BF)],
        [
            pltpu.VMEM(one, BF),
            pltpu.VMEM((3,) + one, BF),
            pltpu.VMEM(one, BF),
            sems(2),
            sems(3),
            sems(3),
        ],
        line_off(order[1]),
        run,
    )


def share_x(part):
    rows, cols = part.shape[1:]

    def run(p, ins, outs, scratch):
        hold, k, s, r = scratch
        inward = copy(ins[0], hold, k.at[0])
        dst = outs[0].at[pl.ds(p["x"], 1)]
        copies = [send(ins[0], dst, s.at[i], r.at[i], dev(p, **o)) for i, o in enumerate(X_OFF)]
        inward.wait()
        near = copy(hold, dst, k.at[1])
        yield
        near.wait()
        for c in copies:
            c.wait()

    return Op(
        [part],
        [((4, rows, cols), BF)],
        [pltpu.VMEM(part.shape, BF), sems(2), sems(3), sems(3)],
        X_OFF,
        run,
    )


def series(*ops):
    def run(p, ins, outs, scratch):
        for n, op in enumerate(ops):
            here, outs = outs[: len(op.outs)], outs[len(op.outs) :]
            yield from op.run(p, ins, here, scratch[: len(op.scratch)])
            scratch = scratch[len(op.scratch) :]
            ins = here

    return Op(
        ops[0].ins,
        [o for op in ops for o in op.outs],
        [c for op in ops for c in op.scratch],
        [f for op in ops for f in op.offsets],
        run,
    )


def shaped(op):
    return jax.ShapeDtypeStruct(*op.outs[-1])


def rs_finish(part, order):
    second = rs_second(part, order)
    return series(second, share_x(shaped(second)))


def rs_whole(mine, crossed, order):
    line = rs_line(mine, crossed, order)
    second = rs_second(shaped(line), order)
    return series(line, second, share_x(shaped(second)))


def sum_all(a):
    shape = a.shape
    axes = ("dx", "dy", "dz")

    def run(p, ins, outs, scratch):
        acc, got, k, s, r = scratch
        copy(ins[0], acc.at[0], k.at[0]).wait()
        for n, axis in enumerate(axes):
            copies = [
                send(
                    acc.at[n],
                    got.at[3 * n + d - 1],
                    s.at[3 * n + d - 1],
                    r.at[3 * n + d - 1],
                    dev(p, **{axis: d}),
                )
                for d in (1, 2, 3)
            ]
            yield
            for c in copies:
                c.wait()
            acc[n + 1] = acc[n] + got[3 * n] + got[3 * n + 1] + got[3 * n + 2]
        c = send(acc.at[3], got.at[9], s.at[9], r.at[9], dev(p, dc=1))
        yield
        c.wait()
        acc[4] = acc[3] + got[9]
        copy(acc.at[4], outs[0], k.at[0]).wait()

    return Op(
        [a],
        [(shape, F32)],
        [pltpu.VMEM((5,) + shape, F32), pltpu.VMEM((10,) + shape, F32), sems(1), sems(10), sems(10)],
        X_OFF + Y_OFF + Z_OFF + CORE_OFF,
        run,
    )


def pick(a, index, axis):
    return lax.dynamic_index_in_dim(a, index, axis, keepdims=False)


def rotated(y, cosine, sine):
    lane = lax.broadcasted_iota(jnp.int32, y.shape, 1)
    low = lax.rem(lane, HEAD) < HEAD // 2
    width = y.shape[1]
    turned = jnp.where(low, pltpu.roll(y, width - HEAD // 2, 1), pltpu.roll(y, HEAD // 2, 1))
    return y * cosine + turned * sine


def contract(a, b, da, db):
    return lax.dot_general(a, b, (((da,), (db,)), ((), ())), preferred_element_type=F32)


SCALE = HEAD ** (-0.5)


def masked(st, i):
    width = st.shape[0]
    key = lax.broadcasted_iota(jnp.int32, (256, 256), 0)
    query = lax.broadcasted_iota(jnp.int32, (256, 256), 1)
    last = jnp.where(key <= query, st[width - 256 :], NEG)
    return last if width == 256 else jnp.concatenate([st[: width - 256], last], axis=0)


def attend(qkv, out, lse):
    for i in range(4):
        rows = pl.ds(i * 256, 256)
        k = jnp.concatenate([qkv[j, :, 2 * HEAD : 3 * HEAD] for j in range(i + 1)], axis=0)
        v = jnp.concatenate([qkv[j, :, 3 * HEAD : 4 * HEAD] for j in range(i + 1)], axis=0)
        outs = []
        for n in range(2):
            q = qkv[i, :, n * HEAD : (n + 1) * HEAD]
            st = masked(contract(k, q, 1, 1) * SCALE, i)
            top = jnp.max(st, axis=0, keepdims=True)
            e = jnp.exp(st - top)
            total = jnp.sum(e, axis=0, keepdims=True)
            ot = contract(v, e.astype(BF), 0, 0)
            outs.append(ot * (1.0 / total))
            lse[n : n + 1, rows] = top + jnp.log(total)
        out[i] = jnp.concatenate(outs, axis=0).T.astype(BF)


def attend_back(qkv, do, lse, out, dq, dk, dv):
    dk[...] = jnp.zeros_like(dk)
    dv[...] = jnp.zeros_like(dv)
    for i in range(4):
        rows = pl.ds(i * 256, 256)
        width = (i + 1) * 256
        k = jnp.concatenate([qkv[j, :, 2 * HEAD : 3 * HEAD] for j in range(i + 1)], axis=0)
        v = jnp.concatenate([qkv[j, :, 3 * HEAD : 4 * HEAD] for j in range(i + 1)], axis=0)
        for n in range(2):
            cols = slice(n * HEAD, (n + 1) * HEAD)
            q, go = qkv[i, :, cols], do[i, :, cols]
            st = masked(contract(k, q, 1, 1) * SCALE, i)
            pr = jnp.exp(st - lse[n : n + 1, rows])
            dpt = contract(v, go, 1, 1)
            delta = jnp.sum(pr * dpt, axis=0, keepdims=True)
            ds = (pr * (dpt - delta)).astype(BF)
            dq[cols, rows] = contract(k, ds, 0, 0)
            dk[:width] += jnp.dot(ds, q, preferred_element_type=F32)
            dv[:width] += jnp.dot(pr.astype(BF), go, preferred_element_type=F32)
    for i in range(4):
        rows = pl.ds(i * 256, 256)
        g = jnp.concatenate([dq[:, rows].T * SCALE, dk[rows] * SCALE, dv[rows]], axis=1)
        out[i] = g.astype(BF)


def sigmoid(v):
    return 1.0 / (1.0 + jnp.exp(-v))


def row_scale(h):
    return lax.rsqrt(jnp.mean(h * h, axis=-1, keepdims=True) + EPS)


def own_rows(x):
    return pl.ds(pl.multiple_of(x * 64, 64), 64)


def tables(tab):
    cosine, sine = tab[:, :48], tab[:, 48:96]
    one = jnp.ones((tab.shape[0], 96), F32)
    return (
        jnp.concatenate([cosine] * 6 + [one], axis=1),
        jnp.concatenate([-sine, sine] * 3 + [one * 0.0], axis=1),
    )


def gain_row(gains, k):
    return jnp.concatenate(
        [gains[d, c, k : k + 1, :48] for d in range(8) for c in range(4)], axis=1
    )


class Links:
    def __init__(self, p, s, r, k):
        self.p, self.s, self.r, self.k, self.n, self.m = p, s, r, k, 0, 0

    def to(self, src, dst, target):
        c = send(src, dst, self.s.at[self.n], self.r.at[self.n], target)
        self.n += 1
        return c

    def near(self, src, dst):
        c = copy(src, dst, self.k.at[self.m])
        self.m += 1
        return c


def wait(copies):
    for c in copies:
        c.wait()


def gather_halves(net, x, own, dst):
    halves = []
    for s in range(2):
        at = dst.at[pl.ds(pl.multiple_of(s * 256 + x * 64, 64), 64)]
        halves.append(
            [net.to(own.at[s], at, dev(net.p, **o)) for o in X_OFF] + [net.near(own.at[s], at)]
        )
    return halves


def scatter_half(net, s, part, terms):
    copies = []
    for i, o in enumerate(X_OFF):
        t = dev(net.p, **o)
        src = part.at[pl.ds(pl.multiple_of(s * 256 + t[2] * 64, 64), 64)]
        copies.append(net.to(src, terms.at[i, s], t))
    return copies


def summed(x, s, part, terms):
    own = part[pl.ds(pl.multiple_of(s * 256 + x * 64, 64), 64)].astype(F32)
    return own + terms[0, s].astype(F32) + terms[1, s].astype(F32) + terms[2, s].astype(F32)


def swap_units(net, un, qv):
    p = net.p
    copies = []
    for o in CTX_OFF:
        t = dev(p, **o)
        copies.append(net.to(un.at[t[1]], qv.at[p["ctx"]], t))
    qv[pl.ds(p["ctx"], 1)] = un[pl.ds(p["ctx"], 1)]
    return copies


def columns(whole, cols):
    w = whole[:, :, :, :, cols]
    return w.reshape(32 * w.shape[3], w.shape[4])


N_SEMS = 96
LINK_SCRATCH = [sems(N_SEMS), sems(N_SEMS), sems(N_SEMS)]


def forward_op(l, normed, w_qkv, tabs, wholes, hidden, gains):
    last = l == LAYERS - 1
    ins = [normed, w_qkv, tabs, hidden, gains] + list(wholes)
    outs = {
        "qv": ((4, 256, 384), BF),
        "lse": ((2, 1024), F32),
        "tok": ((128, D), BF),
        "res": ((128, D), F32),
        "x2": ((512, D), BF),
        "gu": ((512, 2048), F32),
        "ac": ((512, 1024), BF),
        "hid": ((2, 64, D), F32),
        "nxt": ((2, 64, D), BF),
    }
    outs["xg"] = ((512, D), BF)
    names = list(outs)
    scratch = {
        "xg": ((512, D), BF),
        "wq": (w_qkv.shape, BF),
        "tab": ((512, 128), F32),
        "cs": ((512, 384), F32),
        "sn": ((512, 384), F32),
        "un": ((4, 256, 384), BF),
        "qv": ((4, 256, 384), BF),
        "lse": ((2, 1024), F32),
        "mx": ((4, 256, 192), BF),
        "mr": ((8, 128, 192), BF),
        "tok": ((128, D), BF),
        "wo": (wholes[0].shape, BF),
        "hid": ((2, 64, D), F32),
        "res": ((128, D), F32),
        "n2": ((2, 64, D), BF),
        "x2": ((512, D), BF),
        "wgu": (wholes[2].shape, BF),
        "wd": (wholes[1].shape, BF),
        "gu": ((512, 2048), F32),
        "ac": ((512, 1024), BF),
        "pt": ((512, D), BF),
        "tm": ((3, 2, 64, D), BF),
        "gains": ((8, 4, 8, 128), F32),
        "nxt": ((2, 64, D), BF),
    }
    keys = list(scratch)

    def run(p, ins, out_refs, refs):
        v = dict(zip(keys, refs[: len(keys)]))
        net = Links(p, *refs[len(keys) :])
        o = dict(zip(names, out_refs))
        whole = ins[5:]
        x = p["x"]
        saves = []

        def save(key):
            saves.append(net.near(v[key], o[key]))

        if l:
            halves = gather_halves(net, x, ins[0], v["xg"])
        else:
            halves = [
                [
                    net.near(ins[0].at[s, k], v["xg"].at[pl.ds(s * 256 + k * 64, 64)])
                    for k in range(4)
                ]
                for s in range(2)
            ]
        early = [net.near(ins[1], v["wq"]), net.near(ins[4], v["gains"])]
        for s in range(2):
            for k in range(4):
                early.append(
                    net.near(
                        ins[2].at[k, pl.ds(64 * s, 64)],
                        v["tab"].at[pl.ds(s * 256 + k * 64, 64)],
                    )
                )
        late = [net.near(ins[3], v["hid"])]
        wait(early)
        cosine, sine = tables(v["tab"][...])
        v["cs"][...] = cosine
        v["sn"][...] = sine
        for s in range(2):
            wait(halves[s])
            rows = pl.ds(s * 256, 256)
            if not l:
                gain = gain_row(v["gains"], 0)
                for k in range(4):
                    part = pl.ds(s * 256 + k * 64, 64)
                    h = v["xg"][part].astype(F32)
                    v["xg"][part] = (h * row_scale(h) * gain).astype(BF)
            for u in range(2):
                y = jnp.dot(
                    v["xg"][rows], columns(v["wq"], slice(u * 384, u * 384 + 384)), preferred_element_type=F32
                )
                v["un"][s * 2 + u] = rotated(y, v["cs"][rows], v["sn"][rows]).astype(BF)
        moves = swap_units(net, v["un"], v["qv"])
        save("xg")
        yield
        wait(moves)
        save("qv")
        attend(v["qv"], v["mx"], v["lse"])
        save("lse")
        moves = []
        for off in SEQ_OFF:
            t = dev(p, **off)
            moves.append(
                net.to(
                    v["mx"].at[t[1], own_rows(t[2])],
                    v["mr"].at[p["x"] * 2 + p["core"], own_rows(p["zhi"])],
                    t,
                )
            )
        v["mr"][pl.ds(x * 2 + p["core"], 1), own_rows(p["zhi"])] = v["mx"][
            pl.ds(p["ctx"], 1), own_rows(x)
        ]
        yield
        load = net.near(whole[0], v["wo"])
        wait(moves)
        v["tok"][...] = jnp.concatenate([v["mr"][g] for g in range(8)], axis=1)
        save("tok")
        load.wait()
        wait(late)
        gain = gain_row(v["gains"], 2 + l)
        for s in range(2):
            rows = pl.ds(s * 64, 64)
            for c in range(3):
                cols = slice(c * 512, (c + 1) * 512)
                v["res"][rows, cols] = v["hid"][s, :, cols] + jnp.dot(
                    v["tok"][rows], columns(v["wo"], cols), preferred_element_type=F32
                )
            h = v["res"][rows]
            v["n2"][s] = (h * row_scale(h) * gain).astype(BF)
        halves = gather_halves(net, x, v["n2"], v["x2"])
        save("res")
        yield
        yield
        loads = [net.near(whole[2], v["wgu"]), net.near(whole[1], v["wd"])]
        wait(loads[:1])
        backs = []
        for s in range(2):
            wait(halves[s])
            rows = pl.ds(s * 256, 256)
            for j in range(2):
                cols, more = slice(j * 512, (j + 1) * 512), slice(1024 + j * 512, 1536 + j * 512)
                gate = jnp.dot(v["x2"][rows], columns(v["wgu"], cols), preferred_element_type=F32)
                up = jnp.dot(v["x2"][rows], columns(v["wgu"], more), preferred_element_type=F32)
                v["gu"][rows, cols] = gate
                v["gu"][rows, more] = up
                v["ac"][rows, cols] = (gate * sigmoid(gate) * up).astype(BF)
            if s == 0:
                wait(loads[1:])
            for c in range(3):
                cols = slice(c * 512, (c + 1) * 512)
                v["pt"][rows, cols] = jnp.dot(
                    v["ac"][rows], columns(v["wd"], cols), preferred_element_type=F32
                ).astype(BF)
            backs.append(scatter_half(net, s, v["pt"], v["tm"]))
            yield
        save("x2")
        save("gu")
        save("ac")
        gain = gain_row(v["gains"], 1)
        for s in range(2):
            wait(backs[s])
            h = v["res"][pl.ds(s * 64, 64)] + summed(x, s, v["pt"], v["tm"])
            v["hid"][s] = h
            if last:
                v["nxt"][s] = h.astype(BF)
            else:
                v["nxt"][s] = (h * row_scale(h) * gain).astype(BF)
        save("hid")
        save("nxt")
        yield
        wait(saves)

    return names, Op(
        ins,
        list(outs.values()),
        [pltpu.VMEM(*scratch[k]) for k in keys] + LINK_SCRATCH,
        X_OFF + CTX_OFF + SEQ_OFF,
        run,
    )


def norm_back_rows(h, gain, upstream):
    scale = row_scale(h)
    unit = h * scale
    weighted = upstream * gain
    back = scale * (weighted - unit * jnp.mean(weighted * unit, axis=-1, keepdims=True))
    return back, jnp.sum(upstream * unit, axis=0, keepdims=True)


def cross(net, g, mine, crossed):
    p = net.p
    return [
        net.to(g.at[:, 1 - p["core"]], crossed, dev(p, dc=1)),
        net.near(g.at[:, p["core"]], mine),
    ]


def mlp_back_op(l, grad_b, gradient, w_gu, w_down, w_out, gu, ac, x2, res, tok, gains):
    ins = [grad_b, gradient, w_gu, w_down, w_out, gu, ac, x2, res, tok, gains]
    outs = {
        "md": ((16, 32, D), BF),
        "cd": ((16, 32, D), BF),
        "mg": ((16, 48, 2048), BF),
        "cg": ((16, 48, 2048), BF),
        "mo": ((16, 48, D), BF),
        "co": ((16, 48, D), BF),
        "gr": ((128, D), F32),
        "gg": ((1, D), F32),
        "gm": ((8, 128, 192), BF),
    }
    names = list(outs)
    scratch = {
        "gb": ((512, D), BF),
        "gr": ((128, D), F32),
        "wgu": ((D, 2048), BF),
        "wd": ((1024, D), BF),
        "wo": ((D, D), BF),
        "gu": ((512, 2048), F32),
        "ac": ((512, 1024), BF),
        "x2": ((512, D), BF),
        "res": ((128, D), F32),
        "tok": ((128, D), BF),
        "gains": ((8, 4, 8, 128), F32),
        "dgu": ((512, 2048), BF),
        "pt": ((512, D), BF),
        "tm": ((3, 2, 64, D), BF),
        "gd": ((16, 2, 32, D), BF),
        "gg2": ((16, 2, 48, 2048), BF),
        "go": ((16, 2, 48, D), BF),
        "rb": ((128, D), BF),
        "gg": ((1, D), F32),
        "gm": ((8, 128, 192), BF),
    }
    keys = list(scratch)

    def run(p, ins, out_refs, refs):
        v = dict(zip(keys, refs[: len(keys)]))
        net = Links(p, *refs[len(keys) :])
        o = dict(zip(names, out_refs))
        x = p["x"]
        if l == LAYERS - 1:
            halves = [
                [net.near(ins[0].at[pl.ds(s * 256, 256)], v["gb"].at[pl.ds(s * 256, 256)])]
                for s in range(2)
            ]
        else:
            halves = gather_halves(net, x, ins[0], v["gb"])
        loads = [net.near(ins[3], v["wd"]), net.near(ins[5], v["gu"]), net.near(ins[2], v["wgu"])]
        more = [
            net.near(ins[6], v["ac"]),
            net.near(ins[7], v["x2"]),
            net.near(ins[8], v["res"]),
            net.near(ins[1], v["gr"]),
            net.near(ins[10], v["gains"]),
            net.near(ins[4], v["wo"]),
            net.near(ins[9], v["tok"]),
        ]
        yield
        wait(loads[:2])
        backs = []
        for s in range(2):
            wait(halves[s])
            rows = pl.ds(s * 256, 256)
            for j in range(2):
                cols, high = slice(j * 512, (j + 1) * 512), slice(1024 + j * 512, 1536 + j * 512)
                ga = contract(v["gb"][rows], v["wd"][cols], 1, 1)
                gate, up = v["gu"][rows, cols], v["gu"][rows, high]
                sg = sigmoid(gate)
                v["dgu"][rows, cols] = (ga * up * sg * (1.0 + gate * (1.0 - sg))).astype(BF)
                v["dgu"][rows, high] = (ga * gate * sg).astype(BF)
            if s == 0:
                wait(loads[2:])
            for c in range(3):
                cols = slice(c * 512, (c + 1) * 512)
                v["pt"][rows, cols] = contract(v["dgu"][rows], v["wgu"][cols], 1, 1).astype(BF)
            backs.append(scatter_half(net, s, v["pt"], v["tm"]))
            yield
        wait(more)
        for i in range(4):
            for c in range(3):
                cols = slice(c * 512, (c + 1) * 512)
                g = contract(v["ac"][:, i * 256 : (i + 1) * 256], v["gb"][:, cols], 0, 0)
                v["gd"][i * 4 : (i + 1) * 4, :, :, cols] = g.astype(BF).reshape(4, 2, 32, 512)
        ends = cross(net, v["gd"], o["md"], o["cd"])
        for i in range(4):
            for c in range(4):
                cols = slice(c * 512, (c + 1) * 512)
                g = contract(v["x2"][:, i * 384 : (i + 1) * 384], v["dgu"][:, cols], 0, 0)
                v["gg2"][i * 4 : (i + 1) * 4, :, :, cols] = g.astype(BF).reshape(4, 2, 48, 512)
        ends += cross(net, v["gg2"], o["mg"], o["cg"])
        yield
        total = jnp.zeros((1, D), F32)
        gain = gain_row(v["gains"], 2 + l)
        for s in range(2):
            wait(backs[s])
            rows = pl.ds(s * 64, 64)
            back, gain_grad = norm_back_rows(
                v["res"][rows], gain, summed(x, s, v["pt"], v["tm"])
            )
            total = total + gain_grad
            gr = v["gr"][rows] + back
            v["gr"][rows] = gr
            v["rb"][rows] = gr.astype(BF)
        v["gg"][...] = total
        ends += [net.near(v["gr"], o["gr"]), net.near(v["gg"], o["gg"])]
        for j in range(4):
            g = contract(v["rb"][...], v["wo"][j * 384 : (j + 1) * 384], 1, 1).astype(BF)
            v["gm"][2 * j] = g[:, :192]
            v["gm"][2 * j + 1] = g[:, 192:]
        ends += [net.near(v["gm"], o["gm"])]
        for i in range(4):
            for c in range(3):
                cols = slice(c * 512, (c + 1) * 512)
                g = contract(v["tok"][:, i * 384 : (i + 1) * 384], v["rb"][:, cols], 0, 0)
                v["go"][i * 4 : (i + 1) * 4, :, :, cols] = g.astype(BF).reshape(4, 2, 48, 512)
        ends += cross(net, v["go"], o["mo"], o["co"])
        yield
        wait(ends)

    return names, Op(
        ins,
        list(outs.values()),
        [pltpu.VMEM(*scratch[k]) for k in keys] + LINK_SCRATCH,
        X_OFF + CORE_OFF,
        run,
    )


def attend_back_op(l, gm, qv, lse, tabs, w_qkv, xg, hidden, gains, gr):
    ins = [gm, qv, lse, tabs, w_qkv, xg, hidden, gains, gr]
    outs = {
        "mq": ((16, 48, 768), BF),
        "cq": ((16, 48, 768), BF),
        "gr": ((2, 64, D), F32),
        "gb": ((2, 64, D), BF),
        "gg": ((1, D), F32),
    }
    names = list(outs)
    scratch = {
        "do": ((4, 256, 192), BF),
        "qv": ((4, 256, 384), BF),
        "lse": ((2, 1024), F32),
        "tab": ((512, 128), F32),
        "cs": ((512, 384), F32),
        "sn": ((512, 384), F32),
        "un": ((4, 256, 384), BF),
        "dqkv": ((4, 256, 384), BF),
        "dq": ((192, 1024), F32),
        "dk": ((1024, HEAD), F32),
        "dv": ((1024, HEAD), F32),
        "wq": ((D, 768), BF),
        "xg": ((512, D), BF),
        "hid": ((2, 64, D), F32),
        "gains": ((8, 4, 8, 128), F32),
        "gr": ((2, 64, D), F32),
        "gb": ((2, 64, D), BF),
        "gg": ((1, D), F32),
        "pt": ((512, D), BF),
        "tm": ((3, 2, 64, D), BF),
        "gq": ((16, 2, 48, 768), BF),
    }
    keys = list(scratch)

    def run(p, ins, out_refs, refs):
        v = dict(zip(keys, refs[: len(keys)]))
        net = Links(p, *refs[len(keys) :])
        o = dict(zip(names, out_refs))
        x = p["x"]
        dst = v["do"].at[p["ctx"], own_rows(x)]
        moves = []
        for off in SEQ_OFF:
            t = dev(p, **off)
            src = ins[0].at[t[2] * 2 + lax.rem(t[1], 2), own_rows(lax.div(t[1], 2))]
            moves.append(net.to(src, dst, t))
        moves.append(net.near(ins[0].at[x * 2 + p["core"], own_rows(p["zhi"])], dst))
        moves += [net.near(ins[1], v["qv"]), net.near(ins[2], v["lse"])]
        tabs = []
        for n in range(2):
            for k in range(4):
                tabs.append(
                    net.near(
                        ins[3].at[k, pl.ds(64 * n, 64)],
                        v["tab"].at[pl.ds(n * 256 + k * 64, 64)],
                    )
                )
        loads = [net.near(ins[4], v["wq"]), net.near(ins[5], v["xg"]), net.near(ins[6], v["hid"])]
        loads += [net.near(ins[7], v["gains"]), net.near(ins[8], v["gr"])]
        wait(tabs)
        cosine, sine = tables(v["tab"][...])
        v["cs"][...] = cosine
        v["sn"][...] = sine
        yield
        wait(moves)
        attend_back(v["qv"], v["do"], v["lse"], v["un"], v["dq"], v["dk"], v["dv"])
        moves = swap_units(net, v["un"], v["dqkv"])
        yield
        wait(loads)
        wait(moves)
        backs = []
        for s in range(2):
            rows = pl.ds(s * 256, 256)
            for u in range(2):
                g = v["dqkv"][2 * s + u].astype(F32)
                v["dqkv"][2 * s + u] = rotated(g, v["cs"][rows], -v["sn"][rows]).astype(BF)
            d = jnp.concatenate([v["dqkv"][2 * s], v["dqkv"][2 * s + 1]], axis=1)
            for c in range(3):
                cols = slice(c * 512, (c + 1) * 512)
                v["pt"][rows, cols] = contract(d, v["wq"][cols], 1, 1).astype(BF)
            backs.append(scatter_half(net, s, v["pt"], v["tm"]))
        yield
        for u in range(2):
            d = jnp.concatenate([v["dqkv"][u], v["dqkv"][2 + u]], axis=0)
            for i in range(4):
                g = contract(v["xg"][:, i * 384 : (i + 1) * 384], d, 0, 0)
                v["gq"][i * 4 : (i + 1) * 4, :, :, u * 384 : (u + 1) * 384] = g.astype(BF).reshape(
                    4, 2, 48, 384
                )
        ends = cross(net, v["gq"], o["mq"], o["cq"])
        yield
        total = jnp.zeros((1, D), F32)
        gain = gain_row(v["gains"], l)
        for s in range(2):
            wait(backs[s])
            back, gain_grad = norm_back_rows(v["hid"][s], gain, summed(x, s, v["pt"], v["tm"]))
            total = total + gain_grad
            gr = v["gr"][s] + back
            v["gr"][s] = gr
            v["gb"][s] = gr.astype(BF)
        v["gg"][...] = total
        ends += [net.near(v[k], o[k]) for k in ("gr", "gb", "gg")]
        yield
        wait(ends)

    return names, Op(
        ins,
        list(outs.values()),
        [pltpu.VMEM(*scratch[k]) for k in keys] + LINK_SCRATCH,
        X_OFF + CTX_OFF + SEQ_OFF,
        run,
    )


def rope_rows(positions):
    half = HEAD // 2
    frequency = BASE ** (-(jnp.arange(half, dtype=F32) * 2.0 / HEAD))
    angles = positions.astype(F32)[:, None] * frequency
    return jnp.concatenate([jnp.cos(angles), jnp.sin(angles), jnp.zeros((128, 32), F32)], axis=1)


def ff_quarter(a, x):
    rows = a.shape[0]
    return pick(a.reshape(rows, 32, 4, 32), x, 2).reshape(rows, 1024)


def pack_qkv(q, k, v, x):
    rows = q.shape[0]
    q = lax.dynamic_slice_in_dim(q, x * 384, 384, 1).reshape(rows, 2, 192)
    k = lax.dynamic_slice_in_dim(k, x * 192, 192, 1).reshape(rows, 2, 96)
    v = lax.dynamic_slice_in_dim(v, x * 192, 192, 1).reshape(rows, 2, 96)
    return jnp.concatenate([q, k, v], axis=2).reshape(rows, 768)


def unpack_kernel(*refs):
    ins, (q_ref, k_ref, v_ref, o_ref, gate_ref, up_ref, down_ref) = refs[:-7], refs[-7:]
    row = lax.broadcasted_iota(jnp.int32, (512, 512), 0)
    col = lax.broadcasted_iota(jnp.int32, (512, 512), 1)
    place_of = lax.rem(row, 128) // 32 * 128 + row // 128 * 32 + lax.rem(row, 32)
    turn = jnp.where(place_of == col, 1.0, 0.0).astype(BF)
    for l in range(LAYERS):
        qkv, out, down, gu = ins[4 * l : 4 * l + 4]
        q_ref[l] = jnp.concatenate(
            [qkv[x, :, u * 384 : u * 384 + 192] for x in range(4) for u in range(2)], axis=1
        ).astype(F32)
        k_ref[l] = jnp.concatenate(
            [qkv[x, :, u * 384 + 192 : u * 384 + 288] for x in range(4) for u in range(2)], axis=1
        ).astype(F32)
        v_ref[l] = jnp.concatenate(
            [qkv[x, :, u * 384 + 288 : u * 384 + 384] for x in range(4) for u in range(2)], axis=1
        ).astype(F32)
        o_ref[l] = (out[0].astype(F32) + out[1].astype(F32)) + (
            out[2].astype(F32) + out[3].astype(F32)
        )
        for x in range(4):
            down_ref[l, x * 32 : (x + 1) * 32] = down[x].astype(F32)
        for n, ref in enumerate((gate_ref, up_ref)):
            for t in range(8):
                at = n * 1024 + t * 128
                piece = jnp.concatenate([gu[x, :, at : at + 128] for x in range(4)], axis=1)
                ref[l, :, t * 512 : (t + 1) * 512] = jnp.dot(
                    piece, turn, preferred_element_type=F32
                )


def unpack(ends):
    sizes = [(48, D), (48, 768), (48, 768), (48, D), (48, 4096), (48, 4096), (128, D)]
    return pl.pallas_call(
        unpack_kernel,
        out_shape=[jax.ShapeDtypeStruct((LAYERS,) + z, F32) for z in sizes],
        compiler_params=pltpu.CompilerParams(vmem_limit_bytes=VMEM_LIMIT),
        cost_estimate=pl.CostEstimate(flops=10**9, bytes_accessed=10**7, transcendentals=0),
    )(*ends)


AG_ROUNDS = ((0, 1, 2, 3), (0, 1, 4, 5), (0, 2, 6, 7), (0, 2, 6, 7))
RS_QKV, RS_OUT, RS_DOWN, RS_GU = "yz", "zy", "yz", "yz"


def per_device(
    inputs,
    positions,
    cotangent,
    attn_gain,
    query_weight,
    key_matrix,
    value_matrix,
    out_weight,
    mlp_gain,
    gate_weight,
    up_weight,
    down_weight,
):
    p = place()
    x = p["x"]

    shards = []
    for l in range(LAYERS):
        gu = jnp.concatenate([ff_quarter(gate_weight[l], x), ff_quarter(up_weight[l], x)], axis=1)
        down = lax.dynamic_slice_in_dim(down_weight[l], x * 32, 32, 0)
        qkv = pack_qkv(query_weight[l], key_matrix[l], value_matrix[l], x)
        shards.append((qkv, out_weight[l], down, gu))
    orders = ("zy", "yz", "yz", "zy")

    gains = jnp.zeros((8, 128), F32)
    gains = gains.at[:2, :48].set(attn_gain.astype(F32)).at[2:4, :48].set(mlp_gain.astype(F32))
    hidden = inputs.astype(F32)
    saved = []
    whole = []
    tokens = timed(gather_x(inputs), 0, 3)
    tab = timed(rows_x(rope_rows(positions.reshape(128))), 0, 3)
    gain = timed(all_shards(gains), 0, 3)
    w = [timed(ag_all(a, o), *t) for a, o, t in zip(shards[0], orders, AG_ROUNDS)]
    names, fg = forward_op(
        0, From(tokens), From(w[0]), From(tab), [From(a) for a in w[1:]], hidden, From(gain)
    )
    nxt = [
        timed(ag_all(shards[1][0], orders[0]), 5, 6, 8, 9),
        timed(chain(ag_first(shards[1][1], orders[1]), ag_second(_whole(shards[1][1]), orders[1])), 5, 6, 9),
        timed(ag_first(shards[1][2], orders[2]), 5, 6),
        timed(ag_first(shards[1][3], orders[3]), 5, 6),
    ]
    done = build(1, w + [tokens, tab, gain, timed(fg, 3)] + nxt)
    whole.append([d[0] for d in done[:4]])
    tabs, gains_g = done[5][0], done[6][0]
    kept = dict(zip(names, done[7]))
    kept["hidden"] = hidden
    saved.append(kept)
    second = [d[0] for d in done[8:]]
    hidden = kept["hid"]
    w = [
        timed(ag_third(second[1]), 0, 1),
        timed(ag_rest(second[2], orders[2]), 0, 3, 4),
        timed(ag_rest(second[3], orders[3]), 0, 3, 4),
    ]
    names, fg = forward_op(
        1, kept["nxt"], second[0], tabs, [From(a) for a in w], hidden, gains_g
    )
    done = build(2, w + [fg, timed(gather_x(cotangent), 0, 4)])
    whole.append([second[0]] + [d[0] for d in done[:3]])
    kept = dict(zip(names, done[3]))
    kept["hidden"] = hidden
    saved.append(kept)
    output = kept["nxt"]
    cot_g = done[4][0]

    gradient = cotangent.astype(F32)
    grad_b = cot_g.reshape(512, D)
    ends = [[None] * 4 for _ in range(LAYERS)]
    gain_grads = [None] * 4
    by_line = lambda a: a.reshape((4, 4) + a.shape[1:])
    for l in reversed(range(LAYERS)):
        kept = saved[l]
        w_qkv, w_out, w_down, w_gu = whole[l]
        w_qkv, w_out = w_qkv.reshape(D, 768), w_out.reshape(D, D)
        w_down, w_gu = w_down.reshape(1024, D), w_gu.reshape(D, 2048)
        names, fg = mlp_back_op(
            l, grad_b, gradient.reshape(128, D), w_gu, w_down, w_out, kept["gu"], kept["ac"],
            kept["x2"], kept["res"], kept["tok"], gains_g,
        )
        if l == 1:
            (r,) = build(4, [fg])
        else:
            r, (part_out1,), (part_qkv1,), (one_gu,), (one_down,) = build(
                5,
                [
                    fg,
                    timed(rs_line(r["mo"], r["co"], RS_OUT), 0, 3, 4),
                    timed(rs_line(q["mq"], q["cq"], RS_QKV), 0, 3, 4),
                    timed(rs_second(part_gu, RS_GU), 0, 3, 4),
                    timed(rs_second(part_down, RS_DOWN), 0, 3, 4),
                ],
            )
        r = {k: by_line(a) if a.shape[0] == 16 else a for k, a in zip(names, r)}
        gain_grads[2 + l] = r["gg"]
        names, fg = attend_back_op(
            l, r["gm"], kept["qv"], kept["lse"], tabs, w_qkv, kept["xg"], kept["hidden"], gains_g,
            r["gr"].reshape(2, 64, D),
        )
        bg = [
            timed(rs_line(r["mg"], r["cg"], RS_GU), 0, 4, 5),
            timed(rs_line(r["md"], r["cd"], RS_DOWN), 0, 4, 5),
        ]
        if l == 0:
            bg.append(timed(rs_line(r["mo"], r["co"], RS_OUT), 1, 4, 5))
            bg += [share_x(one_gu), share_x(one_down)]
            bg += [rs_finish(part_out1, RS_OUT), rs_finish(part_qkv1, RS_QKV)]
        q, *rest = build(6 + (l == 0), [fg] + bg)
        part_gu, part_down = rest[0][0], rest[1][0]
        if l == 0:
            part_out = rest[2][0]
            ends[1] = [rest[6][-1], rest[5][-1], rest[4][-1], rest[3][-1]]
        q = {k: by_line(a) if a.shape[0] == 16 else a for k, a in zip(names, q)}
        gain_grads[l] = q["gg"]
        gradient, grad_b = q["gr"], q["gb"]

    sums = jnp.zeros((8, D), F32).at[:4].set(jnp.concatenate(gain_grads, axis=0))
    tail = build(
        8,
        [
            rs_whole(q["mq"], q["cq"], RS_QKV),
            rs_finish(part_gu, RS_GU),
            rs_finish(part_down, RS_DOWN),
            rs_finish(part_out, RS_OUT),
            sum_all(sums),
        ],
    )
    ends[0][0], ends[0][3], ends[0][2], ends[0][1], gain_sum = [t[-1] for t in tail]
    grads = unpack(ends[0] + ends[1])

    block = p["dp"] * 4 + p["ctx"]
    gain_own = pick(gain_sum[:4].reshape(4, 32, 48), block, 1)
    return (
        output,
        gradient.reshape(2, 64, D),
        gain_own[:2],
        grads[0],
        grads[1],
        grads[2],
        grads[3],
        gain_own[2:],
        grads[4],
        grads[5],
        grads[6],
    )


def solution(mesh):
    tokens = P("dp", ("ctx", "head"), None)
    vector = P(None, ("dp", "ctx"))
    matrix = P(None, ("dp", "ctx"), None)
    return jax.shard_map(
        per_device,
        mesh=mesh,
        in_specs=(
            tokens,
            P("dp", ("ctx", "head")),
            tokens,
            vector,
            matrix,
            matrix,
            matrix,
            matrix,
            vector,
            matrix,
            matrix,
            matrix,
        ),
        out_specs=(
            tokens,
            tokens,
            vector,
            matrix,
            matrix,
            matrix,
            matrix,
            vector,
            matrix,
            matrix,
            matrix,
        ),
        check_vma=False,
    )
```

```python
from types import SimpleNamespace

import jax
import jax.numpy as jnp
from jax import lax
from jax.experimental import pallas as pl
from jax.experimental.pallas import tpu as pltpu
from jax.sharding import PartitionSpec as P

HEAD = 96
LAYERS = 2
D = 1536
EPS = 1e-05
BASE = 100000.0
NEG = -1e30
F32 = jnp.float32
BF = jnp.bfloat16
MESH = pl.DeviceIdType.MESH
VMEM_LIMIT = 60 * 1024 * 1024


def named(names, values):
    return SimpleNamespace(**dict(zip(names, values)))


def place():
    dp, ctx, head = lax.axis_index("dp"), lax.axis_index("ctx"), lax.axis_index("head")
    y, zlo = lax.div(dp, 2), lax.rem(dp, 2)
    zhi, core = lax.div(ctx, 2), lax.rem(ctx, 2)
    return SimpleNamespace(dp=dp, ctx=ctx, x=head, y=y, zlo=zlo, zhi=zhi, core=core, z=zhi * 2 + zlo)


def dev(p, dx=0, dy=0, dz=0, dc=0):
    x = lax.rem(p.x + dx, 4)
    y = lax.rem(p.y + dy, 4)
    z = lax.rem(p.z + dz, 4)
    core = lax.rem(p.core + dc, 2)
    return (y * 2 + lax.rem(z, 2), lax.div(z, 2) * 2 + core, x)


def z_slot(z):
    return lax.rem(z, 2) * 2 + lax.div(z, 2)


class Op:
    def __init__(self, ins, outs, scratch, offsets, run, alias=()):
        self.ins, self.outs, self.scratch = list(ins), list(outs), list(scratch)
        self.offsets, self.run, self.alias = offsets, run, dict(alias)
        self.early = False


class From:
    def __init__(self, op, k=0):
        self.op, self.k = op, k
        self.near = k >= len(op.outs)
        if self.near:
            self.shape, self.dtype = op.scratch[0].shape, op.scratch[0].dtype
        else:
            self.shape, self.dtype = op.outs[k]


def sems(n):
    return pltpu.SemaphoreType.DMA((n,))


def build(cid, ops):
    ins = [a for op in ops for a in op.ins if not isinstance(a, From)]
    outs = [o for op in ops for o in op.outs]
    scratch = [s for op in ops for s in op.scratch]
    offsets, alias, i0, o0 = [], {}, 0, 0
    for op in ops:
        for o in op.offsets:
            key = tuple(o.get(k, 0) for k in ("dx", "dy", "dz", "dc"))
            if key not in offsets:
                offsets.append(key)
        for i, o in op.alias.items():
            alias[i0 + i] = o0 + o
        i0 += sum(not isinstance(a, From) for a in op.ins)
        o0 += len(op.outs)
    n_in, n_out = len(ins), len(outs)

    def kernel(*refs):
        p = place()
        if offsets:
            barrier = pltpu.get_barrier_semaphore()
            for o in offsets:
                pl.semaphore_signal(barrier, inc=1, device_id=dev(p, *o), device_id_type=MESH)
        i, o, s = 0, n_in, n_in + n_out
        runs, results = [], {}
        for op in ops:
            own = []
            for a in op.ins:
                if isinstance(a, From):
                    own.append(results[id(a.op)][a.k])
                else:
                    own.append(refs[i])
                    i += 1
            results[id(op)] = tuple(refs[o : o + len(op.outs)]) + tuple(refs[s : s + 1])
            runs.append(
                op.run(p, own, refs[o : o + len(op.outs)], refs[s : s + len(op.scratch)])
            )
            o, s = o + len(op.outs), s + len(op.scratch)
        for op, r in zip(ops, list(runs)):
            if op.early:
                for _ in r:
                    pass
                runs.remove(r)
        if offsets:
            pl.semaphore_wait(barrier, len(offsets))
        while runs:
            live = []
            for r in runs:
                try:
                    next(r)
                    live.append(r)
                except StopIteration:
                    pass
            runs = live

    results = pl.pallas_call(
        kernel,
        out_shape=[jax.ShapeDtypeStruct(s, d) for s, d in outs],
        in_specs=[pl.BlockSpec(memory_space=pl.ANY)] * n_in,
        out_specs=[pl.BlockSpec(memory_space=pl.ANY)] * n_out,
        scratch_shapes=scratch,
        input_output_aliases=alias,
        compiler_params=pltpu.CompilerParams(
            collective_id=cid, has_side_effects=True, vmem_limit_bytes=VMEM_LIMIT
        ),
    )(*ins)
    split = []
    for op in ops:
        split.append(list(results[: len(op.outs)]))
        results = results[len(op.outs) :]
    return split


def idle(n):
    for _ in range(n):
        yield


def timed(op, *rounds):
    def run(*refs):
        steps = op.run(*refs)
        now = 0
        for r in rounds:
            yield from idle(r - now)
            now = r
            try:
                next(steps)
            except StopIteration:
                return
        yield
        for _ in steps:
            yield

    return Op(op.ins, op.outs, op.scratch, op.offsets, run, op.alias)


def chain(*ops):
    def run(p, ins, outs, scratch):
        for n, op in enumerate(ops):
            yield from op.run(p, ins if n == 0 else outs, outs, scratch[: len(op.scratch)])
            scratch = scratch[len(op.scratch) :]

    first = ops[0]
    return Op(
        first.ins,
        first.outs,
        [c for op in ops for c in op.scratch],
        [f for op in ops for f in op.offsets],
        run,
        first.alias,
    )


def send(src, dst, send_sem, recv_sem, target):
    c = pltpu.make_async_remote_copy(
        src_ref=src,
        dst_ref=dst,
        send_sem=send_sem,
        recv_sem=recv_sem,
        device_id=target,
        device_id_type=MESH,
    )
    c.start()
    return c


def copy(src, dst, sem):
    c = pltpu.make_async_copy(src, dst, sem)
    c.start()
    return c


X_OFF = [dict(dx=d) for d in (1, 3, 2)]
Y_OFF = [dict(dy=d) for d in (1, 3, 2)]
Z_OFF = [dict(dz=d) for d in (1, 3, 2)]
CORE_OFF = [dict(dc=1)]
CTX_OFF = [dict(dz=2, dc=0), dict(dz=2, dc=1), dict(dz=0, dc=1)]
SEQ_OFF = [
    dict(dx=dx, dz=dz, dc=dc) for dx in range(4) for dz in (0, 2) for dc in (0, 1)
][1:]
SHARD_OFF = [
    dict(dy=dy, dz=dz, dc=dc) for dy in range(4) for dz in range(4) for dc in (0, 1)
][1:]


def swap_op(a, out, offsets, near, far):
    block = jax.eval_shape(
        lambda v: near(SimpleNamespace(ctx=0, x=0, core=0, zhi=0), _Shape(v), _Shape(v))[0].value, a
    )
    n = len(offsets)

    def run(p, ins, outs, scratch):
        hold, s, r, k = scratch
        own, spot = near(p, ins[0], outs[0])
        inward = copy(own, hold, k.at[0])
        copies = []
        for i, o in enumerate(offsets):
            t = dev(p, **o)
            src, dst = far(p, ins[0], outs[0], t)
            copies.append(send(src, dst, s.at[i], r.at[i], t))
        inward.wait()
        outward = copy(hold, spot, k.at[1])
        yield
        outward.wait()
        for c in copies:
            c.wait()

    return Op(
        [a], [out], [pltpu.VMEM(block.shape, block.dtype), sems(n), sems(n), sems(2)], offsets, run
    )


class _Shape:
    def __init__(self, value):
        self.value = value

    @property
    def at(self):
        return self

    def __getitem__(self, index):
        return _Shape(self.value[index])


def gather_x(a):
    out = ((2, 4) + a.shape[1:], a.dtype)

    def near(p, i, o):
        return i, (o.at[:, p.x] if not isinstance(o, _Shape) else None)

    return swap_op(a, out, X_OFF, near, lambda p, i, o, t: (i, o.at[:, p.x]))


def scatter_x(a):
    out = ((4, 2) + a.shape[2:], a.dtype)
    return swap_op(
        a,
        out,
        X_OFF,
        lambda p, i, o: (i.at[:, p.x], o.at[p.x]),
        lambda p, i, o, t: (i.at[:, t[2]], o.at[p.x]),
    )


def swap_ctx(a):
    return swap_op(
        a,
        (a.shape, a.dtype),
        CTX_OFF,
        lambda p, i, o: (i.at[p.ctx], o.at[p.ctx]),
        lambda p, i, o, t: (i.at[t[1]], o.at[p.ctx]),
    )


def heads_to_tokens(a):
    return swap_op(
        a,
        ((4, 2, 2) + a.shape[2:], a.dtype),
        SEQ_OFF,
        lambda p, i, o: (
            i.at[p.ctx, p.x],
            None if isinstance(o, _Shape) else o.at[p.x, p.core, p.zhi],
        ),
        lambda p, i, o, t: (i.at[t[1], t[2]], o.at[p.x, p.core, p.zhi]),
    )


def tokens_to_heads(a):
    return swap_op(
        a,
        ((4, 4) + a.shape[3:], a.dtype),
        SEQ_OFF,
        lambda p, i, o: (
            i.at[p.x, p.core, p.zhi],
            None if isinstance(o, _Shape) else o.at[p.ctx, p.x],
        ),
        lambda p, i, o, t: (
            i.at[t[2], lax.rem(t[1], 2), lax.div(t[1], 2)],
            o.at[p.ctx, p.x],
        ),
    )


def rows_x(a):
    return swap_op(
        a,
        ((4,) + a.shape, a.dtype),
        X_OFF,
        lambda p, i, o: (i, None if isinstance(o, _Shape) else o.at[p.x]),
        lambda p, i, o, t: (i, o.at[p.x]),
    )


def line_off(axis, which=(1, 3, 2)):
    return [{"d" + axis: d} for d in which]


def ag_first(src, order, shape, view):
    near = isinstance(src, From) and src.near

    def run(p, ins, outs, scratch):
        hold, s, r, k = scratch
        shard = view(ins[0], p)
        dst = outs[0].at[p.y, z_slot(p.z), p.core]
        copies = [
            send(shard, dst, s.at[i], r.at[i], dev(p, **o))
            for i, o in enumerate(line_off(order[0]))
        ]
        if not near:
            copy(shard, hold, k.at[0]).wait()
            shard = hold
        outward = copy(shard, dst, k.at[1])
        yield
        outward.wait()
        wait(copies)

    return Op(
        [src],
        [((4, 4, 2) + shape, BF)],
        [pltpu.VMEM((16, 128) if near else shape, BF), sems(3), sems(3), sems(2)],
        line_off(order[0]),
        run,
    )


def ag_second(whole, order):
    def run(p, ins, outs, scratch):
        s, r = scratch
        axis = "d" + order[1]

        def block(d, half=None):
            at = slice(None) if half is None else pl.ds(2 * half, 2)
            if order == "zy":
                return outs[0].at[lax.rem(p.y + d, 4), at, p.core]
            return outs[0].at[at, z_slot(lax.rem(p.z + d, 4)), p.core]

        copies = [
            send(block(0), block(0), s.at[i], r.at[i], dev(p, **{axis: d}))
            for i, d in enumerate((1, 3))
        ]
        yield
        wait(copies)
        copies = [
            send(block(4 - d, n), block(4 - d, n), s.at[2 + n], r.at[2 + n], dev(p, **{axis: d}))
            for n, d in enumerate((1, 3))
        ]
        yield
        wait(copies)

    return Op(
        [whole],
        [(whole.shape, whole.dtype)],
        [sems(4), sems(4)],
        line_off(order[1], (1, 3)),
        run,
        {0: 0},
    )


def ag_third(whole):
    def run(p, ins, outs, scratch):
        s, r = scratch
        block = outs[0].at[:, :, p.core]
        c = send(block, block, s.at[0], r.at[0], dev(p, dc=1))
        yield
        c.wait()

    return Op([whole], [(whole.shape, whole.dtype)], [sems(1), sems(1)], CORE_OFF, run, {0: 0})


def ag_all(first, order, stages=3):
    whole = jax.ShapeDtypeStruct(*first.outs[0])
    rest = [ag_second(whole, order), ag_third(whole)]
    return chain(first, *rest[: stages - 1])


def ag_rest(whole, order):
    return chain(ag_second(whole, order), ag_third(whole))


def loaded(p, pairs, k):
    wait([copy(src, dst, k.at[i]) for i, (src, dst) in enumerate(pairs)])


def iotas(shape):
    return lax.broadcasted_iota(jnp.int32, shape, 0), lax.broadcasted_iota(jnp.int32, shape, 1)


def mask_matrix(condition):
    return jnp.where(condition, 1.0, 0.0).astype(BF)


def pack_qkv(l, q, k, v):
    def run(p, ins, outs, scratch):
        packed, qs, ks, vs, sem = scratch
        x = p.x
        loaded(p, [(ins[0].at[l], qs), (ins[1].at[l], ks), (ins[2].at[l], vs)], sem)
        row, col = iotas((768, 192))
        turn = mask_matrix(row == x * 192 + col)
        own_k = jnp.dot(ks[...], turn, preferred_element_type=F32).astype(BF)
        own_v = jnp.dot(vs[...], turn, preferred_element_type=F32).astype(BF)
        own_q = qs[:, pl.ds(pl.multiple_of(x * 384, 128), 384)]
        packed[...] = jnp.concatenate(
            [own_q[:, :192], own_k[:, :96], own_v[:, :96], own_q[:, 192:], own_k[:, 96:], own_v[:, 96:]],
            axis=1,
        )
        yield

    return Op(
        [q, k, v],
        [],
        [
            pltpu.VMEM((48, 768), BF),
            pltpu.VMEM((48, D), BF),
            pltpu.VMEM((48, 768), BF),
            pltpu.VMEM((48, 768), BF),
            sems(3),
        ],
        [],
        run,
    )


def pack_gu(l, gate, up):
    def run(p, ins, outs, scratch):
        packed, gs, us, sem = scratch
        loaded(p, [(ins[0].at[l], gs), (ins[1].at[l], us)], sem)
        row, col = iotas((512, 128))
        inside = lax.rem(row, 128) // 32 == p.x
        turn = mask_matrix(inside & (row // 128 * 32 + lax.rem(row, 32) == col))
        for n, ref in enumerate((gs, us)):
            for t in range(8):
                packed[:, n * 1024 + t * 128 : n * 1024 + (t + 1) * 128] = jnp.dot(
                    ref[:, t * 512 : (t + 1) * 512], turn, preferred_element_type=F32
                ).astype(BF)
        yield

    return Op(
        [gate, up],
        [],
        [
            pltpu.VMEM((48, 2048), BF),
            pltpu.VMEM((48, 4096), BF),
            pltpu.VMEM((48, 4096), BF),
            sems(2),
        ],
        [],
        run,
    )


def output_op(part, res):
    def run(p, ins, outs, scratch):
        own, r0, tm, out, s, r, k = scratch
        net = Links(p, s, r, k)
        backs = [scatter_half(net, q, ins[0], tm) for q in range(2)]
        loads = [net.near(ins[1], r0)]
        for q in range(2):
            loads.append(net.near(ins[0].at[rows_of(q * 4 + p.x, 64)], own.at[q]))
        yield
        wait(loads)
        for q in range(2):
            wait(backs[q])
            total = own[q].astype(F32) + tm[0, q].astype(F32)
            total = total + tm[1, q].astype(F32) + tm[2, q].astype(F32)
            out[q] = (r0[rows_of(q, 64)] + total).astype(BF)
        done = net.near(out, outs[0])
        yield
        done.wait()

    return Op(
        [part, res],
        [((2, 64, D), BF)],
        [
            pltpu.VMEM((2, 64, D), BF),
            pltpu.VMEM((128, D), F32),
            pltpu.VMEM((3, 2, 64, D), BF),
            pltpu.VMEM((2, 64, D), BF),
            sems(8),
            sems(8),
            sems(8),
        ],
        X_OFF,
        run,
    )


def add_into(dst, terms, rows):
    def body(k, carry):
        at = pl.ds(pl.multiple_of(k * 16, 16), 16)
        for n in range(dst.shape[0]):
            total = terms[0][n, at].astype(F32)
            for t in terms[1:]:
                total = total + t[n, at].astype(F32)
            dst[n, at] = total.astype(BF)
        return carry

    lax.fori_loop(0, rows // 16, body, 0)


def along(p, axis, d):
    return lax.rem(p.y + d, 4) if axis == "y" else z_slot(lax.rem(p.z + d, 4))


def rs_line(g, crossed, order, first=0, cols=None):
    rows, cols = g.shape[2], cols or g.shape[3]
    chunk = (4, rows, cols)

    def run(p, ins, outs, scratch):
        mine, other, got, load, s, r, k = scratch
        loads = []
        for d in (1, 3, 2, 0):
            at = along(p, order[0], d)
            if order[0] == "y":
                a, b = ins[0].at[at], ins[1].at[at]
            else:
                a, b = ins[0].at[:, at], ins[1].at[:, at]
            if cols != g.shape[3]:
                a, b = a.at[:, :, pl.ds(first, cols)], b.at[:, :, pl.ds(first, cols)]
            loads.append(
                (d, copy(a, mine.at[d], load.at[d]), copy(b, other.at[d], load.at[4 + d]))
            )
        copies = []
        for d, a, b in loads:
            a.wait()
            b.wait()
            add_into(mine.at[d], [mine.at[d], other.at[d]], rows)
            if d:
                copies.append(
                    send(
                        mine.at[d],
                        got.at[d - 1],
                        s.at[d - 1],
                        r.at[d - 1],
                        dev(p, **{"d" + order[0]: d}),
                    )
                )
        yield
        for c in copies:
            c.wait()
        add_into(other.at[0], [mine.at[0], got.at[0], got.at[1], got.at[2]], rows)
        out = copy(other.at[0], outs[0], k.at[0])
        yield
        out.wait()

    return Op(
        [g, crossed],
        [(chunk, BF)],
        [
            pltpu.VMEM((4,) + chunk, BF),
            pltpu.VMEM((4,) + chunk, BF),
            pltpu.VMEM((3,) + chunk, BF),
            sems(8),
            sems(3),
            sems(3),
            sems(1),
        ],
        line_off(order[0]),
        run,
    )


def rs_ring(g, crossed, order, first=0, cols=None):
    rows, cols = g.shape[2], cols or g.shape[3]
    chunk = (4, rows, cols)

    def run(p, ins, outs, scratch):
        mine, other, half, got, load, s, r, k = scratch
        axis = "d" + order[0]
        loads = []
        for d in (2, 1, 3, 0):
            at = along(p, order[0], d)
            pair = []
            for ref in ins:
                a = ref.at[at] if order[0] == "y" else ref.at[:, at]
                pair.append(a if cols == g.shape[3] else a.at[:, :, pl.ds(first, cols)])
            loads.append(copy(pair[0], mine.at[d], load.at[d]))
            loads.append(copy(pair[1], other.at[d], load.at[4 + d]))
        ways = (1, 3)
        for d in (2, 1, 3, 0):
            wait(loads[:2])
            loads = loads[2:]
            add_into(mine.at[d], [mine.at[d], other.at[d]], rows)
            if d == 2:
                copies = [
                    send(
                        mine.at[2, pl.ds(2 * n, 2)], half.at[n], s.at[n], r.at[n], dev(p, **{axis: w})
                    )
                    for n, w in enumerate(ways)
                ]
        yield
        wait(copies)
        copies = []
        for n, w in enumerate(ways):
            part = mine.at[w, pl.ds(2 * n, 2)]
            add_into(part, [part, half.at[n]], rows)
            copies.append(
                send(mine.at[w], got.at[n], s.at[2 + n], r.at[2 + n], dev(p, **{axis: w}))
            )
        yield
        wait(copies)
        add_into(other.at[0], [mine.at[0], got.at[0], got.at[1]], rows)
        out = copy(other.at[0], outs[0], k.at[0])
        yield
        out.wait()

    return Op(
        [g, crossed],
        [(chunk, BF)],
        [
            pltpu.VMEM((4,) + chunk, BF),
            pltpu.VMEM((4,) + chunk, BF),
            pltpu.VMEM((2, 2, rows, cols), BF),
            pltpu.VMEM((2,) + chunk, BF),
            sems(8),
            sems(4),
            sems(4),
            sems(1),
        ],
        line_off(order[0], (1, 3)),
        run,
    )


def rs_second(part, order):
    rows, cols = part.shape[1:]
    one = (1, rows, cols)

    def run(p, ins, outs, scratch):
        own, got, total, k, s, r = scratch
        load = copy(ins[0].at[pl.ds(along(p, order[1], 0), 1)], own, k.at[0])
        copies = []
        for i, o in enumerate(line_off(order[1])):
            d = o["d" + order[1]]
            copies.append(
                send(
                    ins[0].at[pl.ds(along(p, order[1], d), 1)],
                    got.at[i],
                    s.at[i],
                    r.at[i],
                    dev(p, **o),
                )
            )
        yield
        load.wait()
        for c in copies:
            c.wait()
        add_into(total, [own, got.at[0], got.at[1], got.at[2]], rows)
        out = copy(total, outs[0], k.at[1])
        yield
        out.wait()

    return Op(
        [part],
        [(one, BF)],
        [
            pltpu.VMEM(one, BF),
            pltpu.VMEM((3,) + one, BF),
            pltpu.VMEM(one, BF),
            sems(2),
            sems(3),
            sems(3),
        ],
        line_off(order[1]),
        run,
    )


def share_x(part):
    rows, cols = part.shape[1:]

    def run(p, ins, outs, scratch):
        hold, k, s, r = scratch
        inward = copy(ins[0], hold, k.at[0])
        dst = outs[0].at[pl.ds(p.x, 1)]
        copies = [send(ins[0], dst, s.at[i], r.at[i], dev(p, **o)) for i, o in enumerate(X_OFF)]
        inward.wait()
        near = copy(hold, dst, k.at[1])
        yield
        near.wait()
        for c in copies:
            c.wait()

    return Op(
        [part],
        [((4, rows, cols), BF)],
        [pltpu.VMEM(part.shape, BF), sems(2), sems(3), sems(3)],
        X_OFF,
        run,
    )


def rs_end(part, order):
    rows, cols = part.shape[1:]
    one = (1, rows, cols)

    def run(p, ins, outs, scratch):
        own, got, total, k, s, r = scratch
        load = copy(ins[0].at[pl.ds(along(p, order[1], 0), 1)], own, k.at[0])
        copies = []
        for i, o in enumerate(line_off(order[1])):
            src = ins[0].at[pl.ds(along(p, order[1], o["d" + order[1]]), 1)]
            copies.append(send(src, got.at[i], s.at[i], r.at[i], dev(p, **o)))
        yield
        load.wait()
        wait(copies)
        add_into(total, [own, got.at[0], got.at[1], got.at[2]], rows)
        dst = outs[0].at[pl.ds(p.x, 1)]
        copies = [
            send(total, dst, s.at[3 + i], r.at[3 + i], dev(p, **o)) for i, o in enumerate(X_OFF)
        ]
        copies.append(copy(total, dst, k.at[1]))
        yield
        wait(copies)

    return Op(
        [part],
        [((4, rows, cols), BF)],
        [
            pltpu.VMEM(one, BF),
            pltpu.VMEM((3,) + one, BF),
            pltpu.VMEM(one, BF),
            sems(2),
            sems(6),
            sems(6),
        ],
        line_off(order[1]) + X_OFF,
        run,
    )


def series(*ops):
    def run(p, ins, outs, scratch):
        for n, op in enumerate(ops):
            here, outs = outs[: len(op.outs)], outs[len(op.outs) :]
            yield from op.run(p, ins, here, scratch[: len(op.scratch)])
            scratch = scratch[len(op.scratch) :]
            ins = here

    return Op(
        ops[0].ins,
        [o for op in ops for o in op.outs],
        [c for op in ops for c in op.scratch],
        [f for op in ops for f in op.offsets],
        run,
    )


def shaped(op):
    return jax.ShapeDtypeStruct(*op.outs[-1])


def rs_all(line, order):
    return series(line, rs_end(shaped(line), order))


def sum_all(*rows):
    shape = (8, D)
    axes = ("dx", "dy", "dz")

    def run(p, ins, outs, scratch):
        acc, got, k, s, r = scratch
        acc[0] = jnp.zeros(shape, F32)
        wait([copy(ins[i], acc.at[0, pl.ds(i, 1)], k.at[i]) for i in range(4)])
        for n, axis in enumerate(axes):
            copies = []
            for d in (1, 2, 3):
                i = 3 * n + d - 1
                copies.append(send(acc.at[n], got.at[i], s.at[i], r.at[i], dev(p, **{axis: d})))
            yield
            wait(copies)
            acc[n + 1] = acc[n] + got[3 * n] + got[3 * n + 1] + got[3 * n + 2]
        c = send(acc.at[3], got.at[9], s.at[9], r.at[9], dev(p, dc=1))
        yield
        c.wait()
        acc[4] = acc[3] + got[9]
        copy(acc.at[4], outs[0], k.at[0]).wait()

    return Op(
        rows,
        [(shape, F32)],
        [pltpu.VMEM((5,) + shape, F32), pltpu.VMEM((10,) + shape, F32), sems(4), sems(10), sems(10)],
        X_OFF + Y_OFF + Z_OFF + CORE_OFF,
        run,
    )


def pick(a, index, axis):
    return lax.dynamic_index_in_dim(a, index, axis, keepdims=False)


def rotated(y, cosine, sine):
    lane = lax.broadcasted_iota(jnp.int32, y.shape, 1)
    low = lax.rem(lane, HEAD) < HEAD // 2
    width = y.shape[1]
    turned = jnp.where(low, pltpu.roll(y, width - HEAD // 2, 1), pltpu.roll(y, HEAD // 2, 1))
    return y * cosine + turned * sine


def contract(a, b, da, db):
    return lax.dot_general(a, b, (((da,), (db,)), ((), ())), preferred_element_type=F32)


SCALE = HEAD ** (-0.5)


def masked(st, i):
    width = st.shape[0]
    key = lax.broadcasted_iota(jnp.int32, (256, 256), 0)
    query = lax.broadcasted_iota(jnp.int32, (256, 256), 1)
    last = jnp.where(key <= query, st[width - 256 :], NEG)
    return last if width == 256 else jnp.concatenate([st[: width - 256], last], axis=0)


def attend(qkv, out, lse):
    for i in range(4):
        rows = pl.ds(i * 256, 256)
        k = jnp.concatenate([qkv[j, :, 2 * HEAD : 3 * HEAD] for j in range(i + 1)], axis=0)
        v = jnp.concatenate([qkv[j, :, 3 * HEAD : 4 * HEAD] for j in range(i + 1)], axis=0)
        outs = []
        for n in range(2):
            q = qkv[i, :, n * HEAD : (n + 1) * HEAD]
            st = masked(contract(k, q, 1, 1) * SCALE, i)
            top = jnp.max(st, axis=0, keepdims=True)
            e = jnp.exp(st - top)
            total = jnp.sum(e, axis=0, keepdims=True)
            ot = contract(v, e.astype(BF), 0, 0)
            outs.append(ot * (1.0 / total))
            lse[n : n + 1, rows] = top + jnp.log(total)
        out[i] = jnp.concatenate(outs, axis=0).T.astype(BF)


def attend_back(qkv, do, lse, out, dq, dk, dv):
    dk[...] = jnp.zeros_like(dk)
    dv[...] = jnp.zeros_like(dv)
    for i in range(4):
        rows = pl.ds(i * 256, 256)
        width = (i + 1) * 256
        k = jnp.concatenate([qkv[j, :, 2 * HEAD : 3 * HEAD] for j in range(i + 1)], axis=0)
        v = jnp.concatenate([qkv[j, :, 3 * HEAD : 4 * HEAD] for j in range(i + 1)], axis=0)
        for n in range(2):
            cols = slice(n * HEAD, (n + 1) * HEAD)
            q, go = qkv[i, :, cols], do[i, :, cols]
            st = masked(contract(k, q, 1, 1) * SCALE, i)
            pr = jnp.exp(st - lse[n : n + 1, rows])
            dpt = contract(v, go, 1, 1)
            delta = jnp.sum(pr * dpt, axis=0, keepdims=True)
            ds = (pr * (dpt - delta)).astype(BF)
            dq[cols, rows] = contract(k, ds, 0, 0)
            dk[:width] += jnp.dot(ds, q, preferred_element_type=F32)
            dv[:width] += jnp.dot(pr.astype(BF), go, preferred_element_type=F32)
    for i in range(4):
        rows = pl.ds(i * 256, 256)
        g = jnp.concatenate([dq[:, rows].T * SCALE, dk[rows] * SCALE, dv[rows]], axis=1)
        out[i] = g.astype(BF)


def sigmoid(v):
    return 1.0 / (1.0 + jnp.exp(-v))


def row_scale(h):
    return lax.rsqrt(jnp.mean(h * h, axis=-1, keepdims=True) + EPS)


def own_rows(x):
    return pl.ds(pl.multiple_of(x * 64, 64), 64)


def tables(tab):
    cosine, sine = tab[:, :48], tab[:, 48:96]
    one = jnp.ones((tab.shape[0], 96), F32)
    return (
        jnp.concatenate([cosine] * 6 + [one], axis=1),
        jnp.concatenate([-sine, sine] * 3 + [one * 0.0], axis=1),
    )


GAINS = (4, 4, 2, 16, 128)


def gain_row(gains, k):
    rows = [
        gains[y, j, c, k : k + 1, :48].astype(F32)
        for y in range(4)
        for j in range(4)
        for c in range(2)
    ]
    return jnp.concatenate(rows, axis=1)


class Links:
    def __init__(self, p, s, r, k):
        self.p, self.s, self.r, self.k, self.n, self.m = p, s, r, k, 0, 0

    def to(self, src, dst, target):
        c = send(src, dst, self.s.at[self.n], self.r.at[self.n], target)
        self.n += 1
        return c

    def near(self, src, dst):
        c = copy(src, dst, self.k.at[self.m])
        self.m += 1
        return c


def wait(copies):
    for c in copies:
        c.wait()


def rows_of(s, size=256, first=0):
    return pl.ds(pl.multiple_of(s * size + first, 64), size)


def gather_half(net, s, own, dst):
    at = dst.at[pl.ds(pl.multiple_of(s * 256 + net.p.x * 64, 64), 64)]
    return [net.to(own.at[s], at, dev(net.p, **o)) for o in X_OFF] + [net.near(own.at[s], at)]


def gather_halves(net, own, dst, order=(0, 1)):
    return [gather_half(net, s, own, dst) for s in order]


def scatter_half(net, s, part, terms):
    copies = []
    for i, o in enumerate(X_OFF):
        t = dev(net.p, **o)
        src = part.at[pl.ds(pl.multiple_of(s * 256 + t[2] * 64, 64), 64)]
        copies.append(net.to(src, terms.at[i, s], t))
    return copies


def summed(x, s, part, terms):
    own = part[pl.ds(pl.multiple_of(s * 256 + x * 64, 64), 64)].astype(F32)
    return own + terms[0, s].astype(F32) + terms[1, s].astype(F32) + terms[2, s].astype(F32)


def swap_units(net, un, qv, offsets):
    copies = []
    for o in offsets:
        t = dev(net.p, **o)
        copies.append(net.to(un.at[t[1]], qv.at[net.p.ctx], t))
    return copies


CTX_FAR, CTX_NEAR = CTX_OFF[:2], CTX_OFF[2:]
SEQ_NEAR = [o for o in SEQ_OFF if o["dz"] == 0]
SEQ_FAR = [o for o in SEQ_OFF if o["dz"] == 2]


def columns(whole, cols):
    w = whole[:, :, :, :, cols]
    return w.reshape(32 * w.shape[3], w.shape[4])


N_SEMS = 96
LINK_SCRATCH = [sems(N_SEMS), sems(N_SEMS), sems(N_SEMS)]


def forward_op(l, normed, w_qkv, tabs, wholes, hidden, gains, cotangent=None, gradient=None):
    last = l == LAYERS - 1
    ins = [normed, w_qkv, tabs, hidden, gains] + list(wholes)
    if last:
        ins += [cotangent, gradient]
    outs = dict(
        qv=((4, 256, 384), BF),
        lse=((2, 1024), F32),
        tok=((128, D), BF),
        res=((128, D), F32),
        xg=((512, D), BF),
    )
    if last:
        outs.update(pt2=((512, D), BF), **MLP_BACK_OUTS)
    else:
        outs.update(x2=((512, D), BF))
        outs.update(gu=((512, 2048), F32))
        outs.update(ac=((512, 1024), BF))
        outs.update(hid=((2, 64, D), F32))
        outs.update(nxt=((2, 64, D), BF))
    names = list(outs)
    scratch = dict(
        xg=((512, D), BF),
        wq=(w_qkv.shape, BF),
        tab=((512, 128), F32),
        cs=((512, 384), F32),
        sn=((512, 384), F32),
        un=((4, 256, 384), BF),
        qv=((4, 256, 384), BF),
        lse=((2, 1024), F32),
        mx=((4, 256, 192), BF),
        mr=((8, 128, 192), BF),
        tok=((128, D), BF),
        wo=(wholes[0].shape, BF),
        wo2=(wholes[1].shape, BF),
        hid=((2, 64, D), F32),
        res=((128, D), F32),
        n2=((2, 64, D), BF),
        x2=((512, D), BF),
        wg=(wholes[3].shape, BF),
        wu=(wholes[4].shape, BF),
        wd=(wholes[2].shape, BF),
        ac=((512, 1024), BF),
        pt=((512, D), BF),
        tm=((3, 2, 64, D), BF),
        gains=(GAINS, BF),
        nxt=((2, 64, D), BF),
    )
    if last:
        scratch.update(pt2=((512, D), BF), gb=((512, D), BF), **MLP_BACK_SCRATCH)
    else:
        scratch.update(gu=((512, 2048), F32))
    keys = list(scratch)

    def run(p, ins, out_refs, refs):
        v = named(keys, refs)
        net = Links(p, *refs[len(keys) :])
        o = named(names, out_refs)
        whole = ins[5:10]
        x = p.x
        saves = []

        def save(src, dst):
            saves.append(net.near(src, dst))

        there, here = 1 - p.zhi, p.zhi
        if l:
            halves = gather_halves(net, ins[0], v.xg, (there, here))
            cots = gather_halves(net, ins[10], v.gb, (here, there))
        else:
            halves = [
                [
                    net.near(ins[0].at[s, k], v.xg.at[rows_of(s * 4 + k, 64)])
                    for k in range(4)
                ]
                for s in (there, here)
            ]
        early = [net.near(ins[1], v.wq), net.near(ins[4], v.gains)]
        for s in range(2):
            for k in range(4):
                early.append(
                    net.near(
                        ins[2].at[k, pl.ds(64 * s, 64)],
                        v.tab.at[pl.ds(s * 256 + k * 64, 64)],
                    )
                )
        late = [net.near(ins[3], v.hid if l else v.nxt)]
        yield
        wait(early)
        cosine, sine = tables(v.tab[...])
        v.cs[...] = cosine
        v.sn[...] = sine
        moves = []
        for n, s in enumerate((there, here)):
            wait(halves[n])
            rows = rows_of(s)
            if not l:
                gain = gain_row(v.gains, 0)
                for k in range(4):
                    part = rows_of(s * 4 + k, 64)
                    h = v.xg[part].astype(F32)
                    v.xg[part] = (h * row_scale(h) * gain).astype(BF)
            for u in range(2):
                y = jnp.dot(
                    v.xg[rows], columns(v.wq, slice(u * 384, u * 384 + 384)), preferred_element_type=F32
                )
                v.un[s * 2 + u] = rotated(y, v.cs[rows], v.sn[rows]).astype(BF)
            moves += swap_units(net, v.un, v.qv, (CTX_FAR, CTX_NEAR)[n])
            if n == 0:
                yield
        v.qv[pl.ds(p.ctx, 1)] = v.un[pl.ds(p.ctx, 1)]
        save(v.xg, o.xg)
        yield
        wait(moves)
        save(v.qv, o.qv)
        attend(v.qv, v.mx, v.lse)
        save(v.lse, o.lse)
        moves = []
        for offsets in (SEQ_NEAR, SEQ_FAR):
            group = []
            for off in offsets:
                t = dev(p, **off)
                group.append(
                    net.to(
                        v.mx.at[t[1], own_rows(t[2])],
                        v.mr.at[p.x * 2 + p.core, own_rows(p.zhi)],
                        t,
                    )
                )
            moves.append(group)
        v.mr[pl.ds(x * 2 + p.core, 1), own_rows(p.zhi)] = v.mx[
            pl.ds(p.ctx, 1), own_rows(x)
        ]
        yield
        load = [net.near(whole[0], v.wo), net.near(whole[1], v.wo2)]
        gain = gain_row(v.gains, 2 + l)
        wait(load)
        wait(late)
        if not l:
            v.hid[...] = v.nxt[...].astype(F32)
        halves = []
        for n, s in enumerate((here, there)):
            wait(moves[n])
            rows = rows_of(s, 64)
            v.tok[rows] = jnp.concatenate([v.mr[g, rows] for g in range(8)], axis=1)
            for c in range(2):
                cols = slice(c * 768, (c + 1) * 768)
                w = columns((v.wo, v.wo2)[c], slice(None))
                v.res[rows, cols] = v.hid[s, :, cols] + jnp.dot(
                    v.tok[rows], w, preferred_element_type=F32
                )
            h = v.res[rows]
            v.n2[s] = (h * row_scale(h) * gain).astype(BF)
            halves.append(gather_half(net, s, v.n2, v.x2))
        save(v.tok, o.tok)
        save(v.res, o.res)
        yield
        yield
        loads = [net.near(whole[3], v.wg), net.near(whole[4], v.wu)]
        wait(loads)
        if last:
            net.near(whole[2], v.wd).wait()
            backs = []
            for n, s in enumerate((here, there)):
                wait(halves[n])
                wait(cots[n])
                rows = rows_of(s)
                for j in range(2):
                    cols, high = slice(j * 512, (j + 1) * 512), slice(1024 + j * 512, 1536 + j * 512)
                    gate = jnp.dot(v.x2[rows], columns(v.wg, cols), preferred_element_type=F32)
                    up = jnp.dot(v.x2[rows], columns(v.wu, cols), preferred_element_type=F32)
                    sg = sigmoid(gate)
                    v.ac[rows, cols] = (gate * sg * up).astype(BF)
                    ga = contract(v.gb[rows], v.wd[2 * j : 2 * j + 2].reshape(512, D), 1, 1)
                    v.dgu[rows, cols] = (ga * up * sg * (1.0 + gate * (1.0 - sg))).astype(BF)
                    v.dgu[rows, high] = (ga * gate * sg).astype(BF)
                yield
                for c in range(4):
                    cols = slice(c * 384, (c + 1) * 384)
                    g = contract(v.dgu[rows, :1024], v.wg[c].reshape(384, 1024), 1, 1)
                    g = g + contract(v.dgu[rows, 1024:], v.wu[c].reshape(384, 1024), 1, 1)
                    v.pt[rows, cols] = g.astype(BF)
                backs.append(scatter_half(net, s, v.pt, v.tm))
                yield

            def forward_part():
                for c in range(3):
                    cols = slice(c * 512, (c + 1) * 512)
                    v.pt2[:, cols] = jnp.dot(
                        v.ac[...], columns(v.wd, cols), preferred_element_type=F32
                    ).astype(BF)
                save(v.pt2, o.pt2)

            loads = [net.near(ins[11], v.gr)]
            yield from mlp_back_rest(
                net, o, v, loads, backs, (here, there), l, True, forward_part, saves
            )
            return
        backs = []
        for n, s in enumerate((here, there)):
            wait(halves[n])
            rows = rows_of(s)
            for j in range(2):
                cols, more = slice(j * 512, (j + 1) * 512), slice(1024 + j * 512, 1536 + j * 512)
                gate = jnp.dot(v.x2[rows], columns(v.wg, cols), preferred_element_type=F32)
                up = jnp.dot(v.x2[rows], columns(v.wu, cols), preferred_element_type=F32)
                v.gu[rows, cols] = gate
                v.gu[rows, more] = up
                v.ac[rows, cols] = (gate * sigmoid(gate) * up).astype(BF)
            yield
            if n == 0:
                net.near(whole[2], v.wd).wait()
            for c in range(3):
                cols = slice(c * 512, (c + 1) * 512)
                v.pt[rows, cols] = jnp.dot(
                    v.ac[rows], columns(v.wd, cols), preferred_element_type=F32
                ).astype(BF)
            backs.append(scatter_half(net, s, v.pt, v.tm))
            yield
        save(v.x2, o.x2)
        save(v.gu, o.gu)
        save(v.ac, o.ac)
        gain = gain_row(v.gains, 1)
        for n, s in enumerate((here, there)):
            wait(backs[n])
            h = v.res[rows_of(s, 64)] + summed(x, s, v.pt, v.tm)
            v.hid[s] = h
            if last:
                v.nxt[s] = h.astype(BF)
            else:
                v.nxt[s] = (h * row_scale(h) * gain).astype(BF)
        save(v.hid, o.hid)
        save(v.nxt, o.nxt)
        yield
        wait(saves)

    return names, Op(
        ins,
        list(outs.values()),
        [pltpu.VMEM(*scratch[k]) for k in keys] + LINK_SCRATCH,
        X_OFF + CTX_OFF + SEQ_OFF,
        run,
    )


def norm_back_rows(h, gain, upstream):
    scale = row_scale(h)
    unit = h * scale
    weighted = upstream * gain
    back = scale * (weighted - unit * jnp.mean(weighted * unit, axis=-1, keepdims=True))
    return back, jnp.sum(upstream * unit, axis=0, keepdims=True)


def cross(net, g, mine, crossed):
    p = net.p
    return [
        net.to(g.at[:, :, 1 - p.core], crossed, dev(p, dc=1)),
        net.near(g.at[:, :, p.core], mine),
    ]


MLP_BACK_OUTS = dict(
    md=((4, 4, 32, D), BF),
    cd=((4, 4, 32, D), BF),
    mg=((4, 4, 48, 2048), BF),
    cg=((4, 4, 48, 2048), BF),
    mo=((4, 4, 48, D), BF),
    co=((4, 4, 48, D), BF),
    gr=((128, D), F32),
    gg=((1, D), F32),
    gm=((8, 128, 192), BF),
)
MLP_BACK_SCRATCH = dict(
    gr=((128, D), F32),
    dgu=((512, 2048), BF),
    gd=((4, 4, 2, 32, D), BF),
    gg2=((4, 4, 2, 48, 2048), BF),
    go=((4, 4, 2, 48, D), BF),
    rb=((128, D), BF),
    gg=((1, D), F32),
    gm=((8, 128, 192), BF),
)


def mlp_back_rest(net, o, v, loads, backs, order, l, whole, filler, ends):
    x = net.p.x
    wait(loads)
    for i in range(4):
        for c in range(3):
            cols = slice(c * 512, (c + 1) * 512)
            g = contract(v.ac[:, i * 256 : (i + 1) * 256], v.gb[:, cols], 0, 0)
            v.gd[i, :, :, :, cols] = g.astype(BF).reshape(4, 2, 32, 512)
    ends += cross(net, v.gd, o.md, o.cd)
    for i in range(4):
        for c in range(4):
            cols = slice(c * 512, (c + 1) * 512)
            g = contract(v.x2[:, i * 384 : (i + 1) * 384], v.dgu[:, cols], 0, 0)
            v.gg2[i, :, :, :, cols] = g.astype(BF).reshape(4, 2, 48, 512)
    ends += cross(net, v.gg2, o.mg, o.cg)
    yield
    total = jnp.zeros((1, D), F32)
    gain = gain_row(v.gains, 2 + l)
    for n, s in enumerate(order):
        wait(backs[n])
        rows = rows_of(s, 64)
        back, gain_grad = norm_back_rows(v.res[rows], gain, summed(x, s, v.pt, v.tm))
        total = total + gain_grad
        gr = v.gr[rows] + back
        v.gr[rows] = gr
        v.rb[rows] = gr.astype(BF)
    v.gg[...] = total
    ends += [net.near(v.gr, o.gr), net.near(v.gg, o.gg)]
    for j in range(4):
        if whole:
            w = [a[j].reshape(384, 768) for a in (v.wo, v.wo2)]
        else:
            w = [a[j * 384 : (j + 1) * 384] for a in (v.wo, v.wo2)]
        g = contract(v.rb[:, :768], w[0], 1, 1)
        g = (g + contract(v.rb[:, 768:], w[1], 1, 1)).astype(BF)
        v.gm[2 * j] = g[:, :192]
        v.gm[2 * j + 1] = g[:, 192:]
    ends += [net.near(v.gm, o.gm)]
    for i in range(4):
        for c in range(3):
            cols = slice(c * 512, (c + 1) * 512)
            g = contract(v.tok[:, i * 384 : (i + 1) * 384], v.rb[:, cols], 0, 0)
            v.go[i, :, :, :, cols] = g.astype(BF).reshape(4, 2, 48, 512)
    ends += cross(net, v.go, o.mo, o.co)
    filler()
    yield
    wait(ends)


def mlp_back_op(
    l, grad_b, gradient, w_gate, w_up, w_down, w_out, w_out2, gu, ac, x2, res, tok, gains
):
    ins = [grad_b, gradient, w_gate, w_down, w_out, gu, ac, x2, res, tok, gains, w_out2, w_up]
    outs = MLP_BACK_OUTS
    names = list(outs)
    scratch = dict(
        gb=((512, D), BF),
        wg=((D, 1024), BF),
        wu=((D, 1024), BF),
        wd=((1024, D), BF),
        wo=((D, 768), BF),
        wo2=((D, 768), BF),
        gu=((512, 2048), F32),
        ac=((512, 1024), BF),
        x2=((512, D), BF),
        res=((128, D), F32),
        tok=((128, D), BF),
        gains=(GAINS, BF),
        pt=((512, D), BF),
        tm=((3, 2, 64, D), BF),
        **MLP_BACK_SCRATCH,
    )
    keys = list(scratch)

    def run(p, ins, out_refs, refs):
        v = named(keys, refs)
        net = Links(p, *refs[len(keys) :])
        o = named(names, out_refs)
        x = p.x
        halves = gather_halves(net, ins[0], v.gb)
        loads = [net.near(ins[3], v.wd), net.near(ins[5], v.gu), net.near(ins[2], v.wg)]
        loads.append(net.near(ins[12], v.wu))
        more = [
            net.near(ins[6], v.ac),
            net.near(ins[7], v.x2),
            net.near(ins[8], v.res),
            net.near(ins[1], v.gr),
            net.near(ins[10], v.gains),
            net.near(ins[4], v.wo),
            net.near(ins[11], v.wo2),
            net.near(ins[9], v.tok),
        ]
        yield
        wait(loads[:2])
        backs = []
        for s in range(2):
            wait(halves[s])
            rows = pl.ds(s * 256, 256)
            for j in range(2):
                cols, high = slice(j * 512, (j + 1) * 512), slice(1024 + j * 512, 1536 + j * 512)
                ga = contract(v.gb[rows], v.wd[cols], 1, 1)
                gate, up = v.gu[rows, cols], v.gu[rows, high]
                sg = sigmoid(gate)
                v.dgu[rows, cols] = (ga * up * sg * (1.0 + gate * (1.0 - sg))).astype(BF)
                v.dgu[rows, high] = (ga * gate * sg).astype(BF)
            if s == 0:
                wait(loads[2:])
            for c in range(3):
                cols = slice(c * 512, (c + 1) * 512)
                g = contract(v.dgu[rows, :1024], v.wg[cols], 1, 1)
                g = g + contract(v.dgu[rows, 1024:], v.wu[cols], 1, 1)
                v.pt[rows, cols] = g.astype(BF)
            backs.append(scatter_half(net, s, v.pt, v.tm))
            yield
        yield from mlp_back_rest(net, o, v, more, backs, (0, 1), l, False, lambda: None, [])

    return names, Op(
        ins,
        list(outs.values()),
        [pltpu.VMEM(*scratch[k]) for k in keys] + LINK_SCRATCH,
        X_OFF + CORE_OFF,
        run,
    )


def attend_back_op(l, gm, qv, lse, tabs, w_qkv, xg, hidden, gains, gr):
    ins = [gm, qv, lse, tabs, w_qkv, xg, hidden, gains, gr]
    outs = dict(
        mq=((4, 4, 48, 768), BF),
        cq=((4, 4, 48, 768), BF),
        gr=((2, 64, D), F32),
        gb=((2, 64, D), BF),
        gg=((1, D), F32),
    )
    names = list(outs)
    scratch = dict(
        do=((4, 256, 192), BF),
        qv=((4, 256, 384), BF),
        lse=((2, 1024), F32),
        tab=((512, 128), F32),
        cs=((512, 384), F32),
        sn=((512, 384), F32),
        un=((4, 256, 384), BF),
        dqkv=((4, 256, 384), BF),
        dq=((192, 1024), F32),
        dk=((1024, HEAD), F32),
        dv=((1024, HEAD), F32),
        wq=((D, 768), BF),
        xg=((512, D), BF),
        hid=((2, 64, D), F32),
        gains=(GAINS, BF),
        gr=((2, 64, D), F32),
        gb=((2, 64, D), BF),
        gg=((1, D), F32),
        pt=((512, D), BF),
        tm=((3, 2, 64, D), BF),
        gq=((4, 4, 2, 48, 768), BF),
    )
    keys = list(scratch)

    def run(p, ins, out_refs, refs):
        v = named(keys, refs)
        net = Links(p, *refs[len(keys) :])
        o = named(names, out_refs)
        x = p.x
        dst = v.do.at[p.ctx, own_rows(x)]
        moves = []
        for off in SEQ_OFF:
            t = dev(p, **off)
            src = ins[0].at[t[2] * 2 + lax.rem(t[1], 2), own_rows(lax.div(t[1], 2))]
            moves.append(net.to(src, dst, t))
        moves.append(net.near(ins[0].at[x * 2 + p.core, own_rows(p.zhi)], dst))
        moves += [net.near(ins[1], v.qv), net.near(ins[2], v.lse)]
        tabs = []
        for n in range(2):
            for k in range(4):
                tabs.append(
                    net.near(
                        ins[3].at[k, pl.ds(64 * n, 64)],
                        v.tab.at[pl.ds(n * 256 + k * 64, 64)],
                    )
                )
        loads = [net.near(ins[4], v.wq), net.near(ins[5], v.xg), net.near(ins[6], v.hid)]
        loads += [net.near(ins[7], v.gains), net.near(ins[8], v.gr)]
        wait(tabs)
        cosine, sine = tables(v.tab[...])
        v.cs[...] = cosine
        v.sn[...] = sine
        yield
        wait(moves)
        attend_back(v.qv, v.do, v.lse, v.un, v.dq, v.dk, v.dv)
        there, here = 1 - p.zhi, p.zhi
        far = swap_units(net, v.un, v.dqkv, CTX_FAR)
        near = swap_units(net, v.un, v.dqkv, CTX_NEAR)
        v.dqkv[pl.ds(p.ctx, 1)] = v.un[pl.ds(p.ctx, 1)]
        yield
        wait(loads)
        backs = []
        for n, s in enumerate((here, there)):
            wait((near, far)[n])
            rows = rows_of(s)
            for u in range(2):
                g = v.dqkv[2 * s + u].astype(F32)
                v.dqkv[2 * s + u] = rotated(g, v.cs[rows], -v.sn[rows]).astype(BF)
            d = jnp.concatenate([v.dqkv[2 * s], v.dqkv[2 * s + 1]], axis=1)
            for c in range(3):
                cols = slice(c * 512, (c + 1) * 512)
                v.pt[rows, cols] = contract(d, v.wq[cols], 1, 1).astype(BF)
            backs.append(scatter_half(net, s, v.pt, v.tm))
        yield
        for u in range(2):
            d = jnp.concatenate([v.dqkv[u], v.dqkv[2 + u]], axis=0)
            for i in range(4):
                g = contract(v.xg[:, i * 384 : (i + 1) * 384], d, 0, 0)
                cols = slice(u * 384, (u + 1) * 384)
                v.gq[i, :, :, :, cols] = g.astype(BF).reshape(4, 2, 48, 384)
        ends = cross(net, v.gq, o.mq, o.cq)
        yield
        total = jnp.zeros((1, D), F32)
        gain = gain_row(v.gains, l)
        for n, s in enumerate((here, there)):
            wait(backs[n])
            back, gain_grad = norm_back_rows(v.hid[s], gain, summed(x, s, v.pt, v.tm))
            total = total + gain_grad
            gr = v.gr[s] + back
            v.gr[s] = gr
            v.gb[s] = gr.astype(BF)
        v.gg[...] = total
        ends += [net.near(v.gr, o.gr), net.near(v.gb, o.gb), net.near(v.gg, o.gg)]
        yield
        wait(ends)

    return names, Op(
        ins,
        list(outs.values()),
        [pltpu.VMEM(*scratch[k]) for k in keys] + LINK_SCRATCH,
        X_OFF + CTX_OFF + SEQ_OFF,
        run,
    )


def rope_rows(positions):
    half = HEAD // 2
    frequency = BASE ** (-(jnp.arange(half, dtype=F32) * 2.0 / HEAD))
    angles = positions.astype(F32)[:, None] * frequency
    return jnp.concatenate([jnp.cos(angles), jnp.sin(angles), jnp.zeros((128, 32), F32)], axis=1)


def unpack_kernel(*refs):
    ins, outs, holds, sem = refs[: 7 * LAYERS], refs[7 * LAYERS : -8], refs[-8:-1], refs[-1]
    row, col = iotas((512, 512))
    place_of = lax.rem(row, 128) // 32 * 128 + row // 128 * 32 + lax.rem(row, 32)
    turn = mask_matrix(place_of == col)
    copies = []

    def done(l, n):
        copies.append(copy(holds[n].at[l], outs[n].at[l], sem.at[7 * l + n]))

    q_ref, k_ref, v_ref, o_ref, gate_ref, up_ref, down_ref = holds
    for l in reversed(range(LAYERS)):
        u0, u1, out, out2, down, gate, up = ins[7 * l : 7 * l + 7]
        for x in range(4):
            down_ref[l, x * 32 : (x + 1) * 32] = down[x].astype(F32)
        done(l, 6)
        for n, half in enumerate((out, out2)):
            o_ref[l, :, n * 768 : (n + 1) * 768] = (
                half[0].astype(F32) + half[1].astype(F32)
            ) + (half[2].astype(F32) + half[3].astype(F32))
        done(l, 3)
        for n, part, ref in ((4, gate, gate_ref), (5, up, up_ref)):
            for t in range(8):
                at = t * 128
                piece = jnp.concatenate([part[x, :, at : at + 128] for x in range(4)], axis=1)
                ref[l, :, t * 512 : (t + 1) * 512] = jnp.dot(
                    piece, turn, preferred_element_type=F32
                )
            done(l, n)
        for n, ref, at, width in ((0, q_ref, 0, 192), (1, k_ref, 192, 96), (2, v_ref, 288, 96)):
            ref[l] = jnp.concatenate(
                [u[x, :, at : at + width] for x in range(4) for u in (u0, u1)], axis=1
            ).astype(F32)
            done(l, n)
    wait(copies)


def unpack(ends):
    sizes = [(48, D), (48, 768), (48, 768), (48, D), (48, 4096), (48, 4096), (128, D)]
    return pl.pallas_call(
        unpack_kernel,
        out_shape=[jax.ShapeDtypeStruct((LAYERS,) + z, F32) for z in sizes],
        out_specs=[pl.BlockSpec(memory_space=pl.ANY)] * 7,
        scratch_shapes=[pltpu.VMEM((LAYERS,) + z, F32) for z in sizes] + [sems(7 * LAYERS)],
        compiler_params=pltpu.CompilerParams(vmem_limit_bytes=VMEM_LIMIT),
        cost_estimate=pl.CostEstimate(flops=10**9, bytes_accessed=10**7, transcendentals=0),
    )(*ends)


RS_UNIT, RS_UNIT2, RS_DOWN, RS_GATE, RS_UP, RS_OUT, RS_OUT2 = "yz", "zy", "yz", "yz", "zy", "yz", "zy"


def per_device(
    inputs,
    positions,
    cotangent,
    attn_gain,
    query_weight,
    key_matrix,
    value_matrix,
    out_weight,
    mlp_gain,
    gate_weight,
    up_weight,
    down_weight,
):
    p = place()

    def shard(l, which, packed=None):
        if which == "qkv":
            return ag_first(From(packed), "zy", (48, 768), lambda r, p: r), "zy"
        if which in ("gate", "up"):
            order, at = "zy", 1024 * (which == "up")
            return ag_first(From(packed), order, (48, 1024), lambda r, p: r.at[:, pl.ds(at, 1024)]), order
        if which == "down":
            view = lambda r, p: r.at[l, pl.ds(pl.multiple_of(p.x * 32, 32), 32)]
            return ag_first(down_weight, "yz", (32, D), view), "yz"
        half = 768 * (which == "out2")
        order = "zy" if half else "yz"
        view = lambda r, p: r.at[l, :, pl.ds(half, 768)]
        return ag_first(out_weight, order, (48, 768), view), order

    gains = jnp.pad(jnp.concatenate([attn_gain, mlp_gain], axis=0), ((0, 12), (0, 80)))

    saved = []
    whole = []
    tokens = timed(gather_x(inputs), 0, 4)
    tab = timed(rows_x(rope_rows(positions.reshape(128))), 0, 4)
    gain = timed(ag_all(ag_first(gains, "zy", (16, 128), lambda r, p: r), "zy"), 0, 1, 2, 3, 4)
    packs = [
        pack_qkv(0, query_weight, key_matrix, value_matrix),
        timed(pack_gu(0, gate_weight, up_weight), 1),
    ]
    packs[0].early = True
    w = [
        timed(ag_all(*shard(0, "qkv", packs[0])), 0, 1, 2, 3, 4),
        timed(ag_all(*shard(0, "out")), 0, 1, 3, 7, 8),
        timed(ag_all(*shard(0, "out2")), 1, 3, 4, 7, 8),
        timed(ag_all(*shard(0, "down")), 0, 2, 9, 10, 11),
        timed(ag_all(*shard(0, "gate", packs[1])), 1, 4, 8, 9, 10),
        timed(ag_all(*shard(0, "up", packs[1])), 1, 4, 8, 9, 10),
    ]
    names, fg = forward_op(
        0, From(tokens), From(w[0]), From(tab), [From(a) for a in w[1:]], inputs, From(gain)
    )
    late = [
        timed(pack_qkv(1, query_weight, key_matrix, value_matrix), 6),
        timed(pack_gu(1, gate_weight, up_weight), 6),
    ]
    nxt = [
        timed(ag_all(*shard(1, "qkv", late[0])), 9, 11, 12, 13, 15),
        timed(shard(1, "out")[0], 9, 14),
        timed(shard(1, "out2")[0], 9, 14),
        timed(shard(1, "down")[0], 9, 14),
        timed(shard(1, "gate", late[1])[0], 9, 14),
        timed(shard(1, "up", late[1])[0], 9, 14),
    ]
    fg = timed(fg, 4)
    ops = packs[:1] + w[:1] + [gain] + w[1:3] + [tokens, tab] + packs[1:] + w[4:] + w[3:4] + [fg] + late + nxt
    done = dict(zip(map(id, ops), build(1, ops)))
    whole.append([done[id(a)][0] for a in w])
    tabs, gains_g = done[id(tab)][0], done[id(gain)][0]
    kept = named(names, done[id(fg)])
    kept.hidden = inputs.astype(F32)
    saved.append(kept)
    second = [done[id(a)][0] for a in nxt]
    hidden = kept.hid
    w = [
        timed(ag_rest(second[1], "yz"), 0, 1, 3, 4),
        timed(ag_rest(second[2], "zy"), 0, 1, 3, 4),
        timed(ag_rest(second[3], "yz"), 0, 3, 4, 5),
        timed(ag_rest(second[4], "zy"), 1, 4, 5, 6),
        timed(ag_rest(second[5], "zy"), 2, 4, 5, 6),
    ]
    names, fg = forward_op(
        1, kept.nxt, second[0], tabs, [From(a) for a in w], hidden, gains_g,
        cotangent, cotangent.astype(F32).reshape(128, D),
    )
    done = build(2, w + [fg])
    whole.append([second[0]] + [d[0] for d in done[:5]])
    kept = named(names, done[5])
    kept.hidden = hidden
    saved.append(kept)

    ends = [None] * LAYERS
    gain_grads = [None] * 4
    for l in reversed(range(LAYERS)):
        kept = saved[l]
        w_qkv, w_out, w_out2, w_down, w_gate, w_up = [
            a.reshape(32 * a.shape[3], a.shape[4]) for a in whole[l]
        ]
        if l == 1:
            names = list(MLP_BACK_OUTS)
            r = [getattr(kept, k) for k in names]
        else:
            names, fg = mlp_back_op(
                l, grad_b, gradient.reshape(128, D), w_gate, w_up, w_down, w_out, w_out2, kept.gu,
                kept.ac, kept.x2, kept.res, kept.tok, gains_g,
            )
            r, (gate,), (up,), (down,), (part_u,), (part_u2,), (part_out,), (part_out2,) = build(
                5,
                [
                    fg,
                    timed(rs_second(part_gate, RS_GATE), 0, 4, 5),
                    timed(rs_second(part_up, RS_UP), 0, 4, 5),
                    timed(rs_second(part_down, RS_DOWN), 0, 4, 5),
                    timed(rs_line(q.mq, q.cq, RS_UNIT, 0, 384), 0, 4, 5),
                    timed(rs_line(q.mq, q.cq, RS_UNIT2, 384, 384), 0, 4, 5),
                    timed(rs_line(r.mo, r.co, RS_OUT, 0, 768), 0, 4, 5),
                    timed(rs_line(r.mo, r.co, RS_OUT2, 768, 768), 0, 4, 5),
                ],
            )
            thirds = [down, gate, up]
        r = named(names, r)
        gain_grads[2 + l] = r.gg
        names, fg = attend_back_op(
            l, r.gm, kept.qv, kept.lse, tabs, w_qkv, kept.xg, kept.hidden, gains_g,
            r.gr.reshape(2, 64, D),
        )
        if l == 1:
            out = timed(output_op(kept.pt2, kept.res), 0, 2)
            bg = [
                timed(rs_line(r.mg, r.cg, RS_GATE, 0, 1024), 0, 4, 5),
                timed(rs_line(r.md, r.cd, RS_DOWN), 0, 4, 5),
                timed(rs_line(r.mg, r.cg, RS_UP, 1024, 1024), 1, 4, 5),
            ]
            q, (output,), (part_gate,), (part_down,), (part_up,) = build(6, [fg, out] + bg)
        else:
            first = [
                timed(rs_end(part_u, RS_UNIT), 0, 1, 4),
                timed(rs_end(part_u2, RS_UNIT2), 0, 1, 4),
                timed(rs_end(part_out, RS_OUT), 0, 1, 4),
                timed(rs_end(part_out2, RS_OUT2), 0, 1, 4),
                *[timed(share_x(a), 0, 3) for a in thirds],
            ]
            bg = [
                timed(rs_all(rs_ring(r.mg, r.cg, RS_GATE, 0, 1024), RS_GATE), 0, 1, 3, 4, 5),
                timed(rs_all(rs_ring(r.md, r.cd, RS_DOWN), RS_DOWN), 0, 1, 3, 4, 5),
                timed(rs_all(rs_ring(r.mo, r.co, RS_OUT, 0, 768), RS_OUT), 0, 1, 3, 4, 5),
                timed(rs_all(rs_ring(r.mg, r.cg, RS_UP, 1024, 1024), RS_UP), 1, 2, 4, 5, 6),
                timed(rs_all(rs_ring(r.mo, r.co, RS_OUT2, 768, 768), RS_OUT2), 1, 2, 4, 5, 6),
            ]
            mq, cq, gg = [From(fg, k) for k in (0, 1, 4)]
            bg += [
                timed(rs_all(rs_line(mq, cq, RS_UNIT, 0, 384), RS_UNIT), 5, 6, 7, 8),
                timed(rs_all(rs_line(mq, cq, RS_UNIT2, 384, 384), RS_UNIT2), 5, 6, 7, 8),
                timed(sum_all(gg, gain_grads[1], gain_grads[2], gain_grads[3]), 5),
            ]
            q, *rest = build(7, [fg] + first + bg)
            ends[1] = [a[0] for a in rest[:7]]
            gate, down, out, up, out2, u, u2, sums = [a[-1] for a in rest[7:]]
            ends[0] = [u, u2, out, out2, down, gate, up]
        q = named(names, q)
        gain_grads[l] = q.gg
        gradient, grad_b = q.gr, q.gb

    grads = unpack(ends[0] + ends[1])

    block = p.dp * 4 + p.ctx
    gain_own = pick(sums[:4].reshape(4, 32, 48), block, 1)
    return (
        output,
        gradient.reshape(2, 64, D),
        gain_own[:2],
        grads[0],
        grads[1],
        grads[2],
        grads[3],
        gain_own[2:],
        grads[4],
        grads[5],
        grads[6],
    )


def solution(mesh):
    tokens = P("dp", ("ctx", "head"), None)
    vector = P(None, ("dp", "ctx"))
    matrix = P(None, ("dp", "ctx"), None)
    return jax.shard_map(
        per_device,
        mesh=mesh,
        in_specs=(
            tokens,
            P("dp", ("ctx", "head")),
            tokens,
            vector,
            matrix,
            matrix,
            matrix,
            matrix,
            vector,
            matrix,
            matrix,
            matrix,
        ),
        out_specs=(
            tokens,
            tokens,
            vector,
            matrix,
            matrix,
            matrix,
            matrix,
            vector,
            matrix,
            matrix,
            matrix,
        ),
        check_vma=False,
    )
```

```python
from types import SimpleNamespace

import jax
import jax.numpy as jnp
from jax import lax
from jax.experimental import pallas as pl
from jax.experimental.pallas import tpu as pltpu
from jax.sharding import PartitionSpec as P

HEAD = 96
LAYERS = 2
D = 1536
EPS = 1e-05
BASE = 100000.0
NEG = -1e30
F32 = jnp.float32
BF = jnp.bfloat16
MESH = pl.DeviceIdType.MESH
VMEM_LIMIT = 60 * 1024 * 1024


def named(names, values):
    return SimpleNamespace(**dict(zip(names, values)))


def place():
    dp, ctx, head = lax.axis_index("dp"), lax.axis_index("ctx"), lax.axis_index("head")
    y, zlo = lax.div(dp, 2), lax.rem(dp, 2)
    zhi, core = lax.div(ctx, 2), lax.rem(ctx, 2)
    return SimpleNamespace(dp=dp, ctx=ctx, x=head, y=y, zlo=zlo, zhi=zhi, core=core, z=zhi * 2 + zlo)


def dev(p, dx=0, dy=0, dz=0, dc=0):
    x = lax.rem(p.x + dx, 4)
    y = lax.rem(p.y + dy, 4)
    z = lax.rem(p.z + dz, 4)
    core = lax.rem(p.core + dc, 2)
    return (y * 2 + lax.rem(z, 2), lax.div(z, 2) * 2 + core, x)


def z_slot(z):
    return lax.rem(z, 2) * 2 + lax.div(z, 2)


class Op:
    def __init__(self, ins, outs, scratch, offsets, run, alias=()):
        self.ins, self.outs, self.scratch = list(ins), list(outs), list(scratch)
        self.offsets, self.run, self.alias = offsets, run, dict(alias)
        self.early = False


class From:
    def __init__(self, op, k=0):
        self.op, self.k = op, k
        self.near = k >= len(op.outs)
        if self.near:
            self.shape, self.dtype = op.scratch[0].shape, op.scratch[0].dtype
        else:
            self.shape, self.dtype = op.outs[k]


def sems(n):
    return pltpu.SemaphoreType.DMA((n,))


def build(cid, ops):
    ins = [a for op in ops for a in op.ins if not isinstance(a, From)]
    outs = [o for op in ops for o in op.outs]
    scratch = [s for op in ops for s in op.scratch]
    offsets, alias, i0, o0 = [], {}, 0, 0
    for op in ops:
        for o in op.offsets:
            key = tuple(o.get(k, 0) for k in ("dx", "dy", "dz", "dc"))
            if key not in offsets:
                offsets.append(key)
        for i, o in op.alias.items():
            alias[i0 + i] = o0 + o
        i0 += sum(not isinstance(a, From) for a in op.ins)
        o0 += len(op.outs)
    n_in, n_out = len(ins), len(outs)

    def kernel(*refs):
        p = place()
        if offsets:
            barrier = pltpu.get_barrier_semaphore()
            for o in offsets:
                pl.semaphore_signal(barrier, inc=1, device_id=dev(p, *o), device_id_type=MESH)
        i, o, s = 0, n_in, n_in + n_out
        runs, results = [], {}
        for op in ops:
            own = []
            for a in op.ins:
                if isinstance(a, From):
                    own.append(results[id(a.op)][a.k])
                else:
                    own.append(refs[i])
                    i += 1
            results[id(op)] = tuple(refs[o : o + len(op.outs)]) + tuple(refs[s : s + 1])
            runs.append(
                op.run(p, own, refs[o : o + len(op.outs)], refs[s : s + len(op.scratch)])
            )
            o, s = o + len(op.outs), s + len(op.scratch)
        for op, r in zip(ops, list(runs)):
            if op.early:
                for _ in r:
                    pass
                runs.remove(r)
        if offsets:
            pl.semaphore_wait(barrier, len(offsets))
        while runs:
            live = []
            for r in runs:
                try:
                    next(r)
                    live.append(r)
                except StopIteration:
                    pass
            runs = live

    results = pl.pallas_call(
        kernel,
        out_shape=[jax.ShapeDtypeStruct(s, d) for s, d in outs],
        in_specs=[pl.BlockSpec(memory_space=pl.ANY)] * n_in,
        out_specs=[pl.BlockSpec(memory_space=pl.ANY)] * n_out,
        scratch_shapes=scratch,
        input_output_aliases=alias,
        compiler_params=pltpu.CompilerParams(
            collective_id=cid, has_side_effects=True, vmem_limit_bytes=VMEM_LIMIT
        ),
    )(*ins)
    split = []
    for op in ops:
        split.append(list(results[: len(op.outs)]))
        results = results[len(op.outs) :]
    return split


def idle(n):
    for _ in range(n):
        yield


def timed(op, *rounds):
    def run(*refs):
        steps = op.run(*refs)
        now = 0
        for r in rounds:
            yield from idle(r - now)
            now = r
            try:
                next(steps)
            except StopIteration:
                return
        yield
        for _ in steps:
            yield

    return Op(op.ins, op.outs, op.scratch, op.offsets, run, op.alias)


def chain(*ops):
    def run(p, ins, outs, scratch):
        for n, op in enumerate(ops):
            yield from op.run(p, ins if n == 0 else outs, outs, scratch[: len(op.scratch)])
            scratch = scratch[len(op.scratch) :]

    first = ops[0]
    return Op(
        first.ins,
        first.outs,
        [c for op in ops for c in op.scratch],
        [f for op in ops for f in op.offsets],
        run,
        first.alias,
    )


def send(src, dst, send_sem, recv_sem, target):
    c = pltpu.make_async_remote_copy(
        src_ref=src,
        dst_ref=dst,
        send_sem=send_sem,
        recv_sem=recv_sem,
        device_id=target,
        device_id_type=MESH,
    )
    c.start()
    return c


def copy(src, dst, sem):
    c = pltpu.make_async_copy(src, dst, sem)
    c.start()
    return c


X_OFF = [dict(dx=d) for d in (1, 3, 2)]
Y_OFF = [dict(dy=d) for d in (1, 3, 2)]
Z_OFF = [dict(dz=d) for d in (1, 3, 2)]
CORE_OFF = [dict(dc=1)]
CTX_OFF = [dict(dz=2, dc=0), dict(dz=2, dc=1), dict(dz=0, dc=1)]
SEQ_OFF = [
    dict(dx=dx, dz=dz, dc=dc) for dx in range(4) for dz in (0, 2) for dc in (0, 1)
][1:]
SHARD_OFF = [
    dict(dy=dy, dz=dz, dc=dc) for dy in range(4) for dz in range(4) for dc in (0, 1)
][1:]


def swap_op(a, out, offsets, near, far):
    block = jax.eval_shape(
        lambda v: near(SimpleNamespace(ctx=0, x=0, core=0, zhi=0), _Shape(v), _Shape(v))[0].value, a
    )
    n = len(offsets)

    def run(p, ins, outs, scratch):
        hold, s, r, k = scratch
        own, spot = near(p, ins[0], outs[0])
        inward = copy(own, hold, k.at[0])
        copies = []
        for i, o in enumerate(offsets):
            t = dev(p, **o)
            src, dst = far(p, ins[0], outs[0], t)
            copies.append(send(src, dst, s.at[i], r.at[i], t))
        inward.wait()
        outward = copy(hold, spot, k.at[1])
        yield
        outward.wait()
        for c in copies:
            c.wait()

    return Op(
        [a], [out], [pltpu.VMEM(block.shape, block.dtype), sems(n), sems(n), sems(2)], offsets, run
    )


class _Shape:
    def __init__(self, value):
        self.value = value

    @property
    def at(self):
        return self

    def __getitem__(self, index):
        return _Shape(self.value[index])


def gather_x(a):
    out = ((2, 4) + a.shape[1:], a.dtype)

    def near(p, i, o):
        return i, (o.at[:, p.x] if not isinstance(o, _Shape) else None)

    return swap_op(a, out, X_OFF, near, lambda p, i, o, t: (i, o.at[:, p.x]))


def scatter_x(a):
    out = ((4, 2) + a.shape[2:], a.dtype)
    return swap_op(
        a,
        out,
        X_OFF,
        lambda p, i, o: (i.at[:, p.x], o.at[p.x]),
        lambda p, i, o, t: (i.at[:, t[2]], o.at[p.x]),
    )


def swap_ctx(a):
    return swap_op(
        a,
        (a.shape, a.dtype),
        CTX_OFF,
        lambda p, i, o: (i.at[p.ctx], o.at[p.ctx]),
        lambda p, i, o, t: (i.at[t[1]], o.at[p.ctx]),
    )


def heads_to_tokens(a):
    return swap_op(
        a,
        ((4, 2, 2) + a.shape[2:], a.dtype),
        SEQ_OFF,
        lambda p, i, o: (
            i.at[p.ctx, p.x],
            None if isinstance(o, _Shape) else o.at[p.x, p.core, p.zhi],
        ),
        lambda p, i, o, t: (i.at[t[1], t[2]], o.at[p.x, p.core, p.zhi]),
    )


def tokens_to_heads(a):
    return swap_op(
        a,
        ((4, 4) + a.shape[3:], a.dtype),
        SEQ_OFF,
        lambda p, i, o: (
            i.at[p.x, p.core, p.zhi],
            None if isinstance(o, _Shape) else o.at[p.ctx, p.x],
        ),
        lambda p, i, o, t: (
            i.at[t[2], lax.rem(t[1], 2), lax.div(t[1], 2)],
            o.at[p.ctx, p.x],
        ),
    )


def rows_x(a):
    return swap_op(
        a,
        ((4,) + a.shape, a.dtype),
        X_OFF,
        lambda p, i, o: (i, None if isinstance(o, _Shape) else o.at[p.x]),
        lambda p, i, o, t: (i, o.at[p.x]),
    )


def line_off(axis, which=(1, 3, 2)):
    return [{"d" + axis: d} for d in which]


def ag_first(src, order, shape, view):
    near = isinstance(src, From) and src.near

    def run(p, ins, outs, scratch):
        hold, s, r, k = scratch
        shard = view(ins[0], p)
        dst = outs[0].at[p.y, z_slot(p.z), p.core]
        copies = [
            send(shard, dst, s.at[i], r.at[i], dev(p, **o))
            for i, o in enumerate(line_off(order[0]))
        ]
        if not near:
            copy(shard, hold, k.at[0]).wait()
            shard = hold
        outward = copy(shard, dst, k.at[1])
        yield
        outward.wait()
        wait(copies)

    return Op(
        [src],
        [((4, 4, 2) + shape, BF)],
        [pltpu.VMEM((16, 128) if near else shape, BF), sems(3), sems(3), sems(2)],
        line_off(order[0]),
        run,
    )


def ag_second(whole, order):
    def run(p, ins, outs, scratch):
        s, r = scratch
        axis = "d" + order[1]

        def block(d, half=None):
            at = slice(None) if half is None else pl.ds(2 * half, 2)
            if order == "zy":
                return outs[0].at[lax.rem(p.y + d, 4), at, p.core]
            return outs[0].at[at, z_slot(lax.rem(p.z + d, 4)), p.core]

        copies = [
            send(block(0), block(0), s.at[i], r.at[i], dev(p, **{axis: d}))
            for i, d in enumerate((1, 3))
        ]
        yield
        wait(copies)
        copies = [
            send(block(4 - d, n), block(4 - d, n), s.at[2 + n], r.at[2 + n], dev(p, **{axis: d}))
            for n, d in enumerate((1, 3))
        ]
        yield
        wait(copies)

    return Op(
        [whole],
        [(whole.shape, whole.dtype)],
        [sems(4), sems(4)],
        line_off(order[1], (1, 3)),
        run,
        {0: 0},
    )


def ag_third(whole):
    def run(p, ins, outs, scratch):
        s, r = scratch
        block = outs[0].at[:, :, p.core]
        c = send(block, block, s.at[0], r.at[0], dev(p, dc=1))
        yield
        c.wait()

    return Op([whole], [(whole.shape, whole.dtype)], [sems(1), sems(1)], CORE_OFF, run, {0: 0})


def ag_all(first, order, stages=3):
    whole = jax.ShapeDtypeStruct(*first.outs[0])
    rest = [ag_second(whole, order), ag_third(whole)]
    return chain(first, *rest[: stages - 1])


def ag_rest(whole, order):
    return chain(ag_second(whole, order), ag_third(whole))


def loaded(p, pairs, k):
    wait([copy(src, dst, k.at[i]) for i, (src, dst) in enumerate(pairs)])


def iotas(shape):
    return lax.broadcasted_iota(jnp.int32, shape, 0), lax.broadcasted_iota(jnp.int32, shape, 1)


def mask_matrix(condition):
    return jnp.where(condition, 1.0, 0.0).astype(BF)


def pack_qkv(l, q, k, v):
    def run(p, ins, outs, scratch):
        packed, qs, ks, vs, sem = scratch
        x = p.x
        loaded(p, [(ins[0].at[l], qs), (ins[1].at[l], ks), (ins[2].at[l], vs)], sem)
        row, col = iotas((768, 192))
        turn = mask_matrix(row == x * 192 + col)
        own_k = jnp.dot(ks[...], turn, preferred_element_type=F32).astype(BF)
        own_v = jnp.dot(vs[...], turn, preferred_element_type=F32).astype(BF)
        own_q = qs[:, pl.ds(pl.multiple_of(x * 384, 128), 384)]
        packed[...] = jnp.concatenate(
            [own_q[:, :192], own_k[:, :96], own_v[:, :96], own_q[:, 192:], own_k[:, 96:], own_v[:, 96:]],
            axis=1,
        )
        yield

    return Op(
        [q, k, v],
        [],
        [
            pltpu.VMEM((48, 768), BF),
            pltpu.VMEM((48, D), BF),
            pltpu.VMEM((48, 768), BF),
            pltpu.VMEM((48, 768), BF),
            sems(3),
        ],
        [],
        run,
    )


def pack_gu(l, gate, up):
    def run(p, ins, outs, scratch):
        packed, gs, us, sem = scratch
        loaded(p, [(ins[0].at[l], gs), (ins[1].at[l], us)], sem)
        row, col = iotas((512, 128))
        inside = lax.rem(row, 128) // 32 == p.x
        turn = mask_matrix(inside & (row // 128 * 32 + lax.rem(row, 32) == col))
        for n, ref in enumerate((gs, us)):
            for t in range(8):
                packed[:, n * 1024 + t * 128 : n * 1024 + (t + 1) * 128] = jnp.dot(
                    ref[:, t * 512 : (t + 1) * 512], turn, preferred_element_type=F32
                ).astype(BF)
        yield

    return Op(
        [gate, up],
        [],
        [
            pltpu.VMEM((48, 2048), BF),
            pltpu.VMEM((48, 4096), BF),
            pltpu.VMEM((48, 4096), BF),
            sems(2),
        ],
        [],
        run,
    )


def output_op(part, res):
    def run(p, ins, outs, scratch):
        own, r0, tm, out, s, r, k = scratch
        net = Links(p, s, r, k)
        backs = [scatter_half(net, q, ins[0], tm) for q in range(2)]
        loads = [net.near(ins[1], r0)]
        for q in range(2):
            loads.append(net.near(ins[0].at[rows_of(q * 4 + p.x, 64)], own.at[q]))
        yield
        wait(loads)
        for q in range(2):
            wait(backs[q])
            total = own[q].astype(F32) + tm[0, q].astype(F32)
            total = total + tm[1, q].astype(F32) + tm[2, q].astype(F32)
            out[q] = (r0[rows_of(q, 64)] + total).astype(BF)
        done = net.near(out, outs[0])
        yield
        done.wait()

    return Op(
        [part, res],
        [((2, 64, D), BF)],
        [
            pltpu.VMEM((2, 64, D), BF),
            pltpu.VMEM((128, D), F32),
            pltpu.VMEM((3, 2, 64, D), BF),
            pltpu.VMEM((2, 64, D), BF),
            sems(8),
            sems(8),
            sems(8),
        ],
        X_OFF,
        run,
    )


def add_into(dst, terms, rows):
    def body(k, carry):
        at = pl.ds(pl.multiple_of(k * 16, 16), 16)
        for n in range(dst.shape[0]):
            total = terms[0][n, at].astype(F32)
            for t in terms[1:]:
                total = total + t[n, at].astype(F32)
            dst[n, at] = total.astype(BF)
        return carry

    lax.fori_loop(0, rows // 16, body, 0)


def along(p, axis, d):
    return lax.rem(p.y + d, 4) if axis == "y" else z_slot(lax.rem(p.z + d, 4))


def rs_line(g, crossed, order, first=0, cols=None):
    rows, cols = g.shape[2], cols or g.shape[3]
    chunk = (4, rows, cols)

    def run(p, ins, outs, scratch, keep=False):
        mine, other, got, load, s, r, k = scratch
        loads = []
        for d in (1, 3, 2, 0):
            at = along(p, order[0], d)
            if order[0] == "y":
                a, b = ins[0].at[at], ins[1].at[at]
            else:
                a, b = ins[0].at[:, at], ins[1].at[:, at]
            if cols != g.shape[3]:
                a, b = a.at[:, :, pl.ds(first, cols)], b.at[:, :, pl.ds(first, cols)]
            loads.append(
                (d, copy(a, mine.at[d], load.at[d]), copy(b, other.at[d], load.at[4 + d]))
            )
        copies = []
        for d, a, b in loads:
            a.wait()
            b.wait()
            add_into(mine.at[d], [mine.at[d], other.at[d]], rows)
            if d:
                copies.append(
                    send(
                        mine.at[d],
                        got.at[d - 1],
                        s.at[d - 1],
                        r.at[d - 1],
                        dev(p, **{"d" + order[0]: d}),
                    )
                )
        yield
        for c in copies:
            c.wait()
        add_into(other.at[0], [mine.at[0], got.at[0], got.at[1], got.at[2]], rows)
        if keep:
            return
        out = copy(other.at[0], outs[0], k.at[0])
        yield
        out.wait()

    return Op(
        [g, crossed],
        [(chunk, BF)],
        [
            pltpu.VMEM((4,) + chunk, BF),
            pltpu.VMEM((4,) + chunk, BF),
            pltpu.VMEM((3,) + chunk, BF),
            sems(8),
            sems(3),
            sems(3),
            sems(1),
        ],
        line_off(order[0]),
        run,
    )


def rs_ring(g, crossed, order, first=0, cols=None):
    rows, cols = g.shape[2], cols or g.shape[3]
    chunk = (4, rows, cols)

    def run(p, ins, outs, scratch, keep=False):
        mine, other, half, got, load, s, r, k = scratch
        axis = "d" + order[0]
        loads = []
        for d in (2, 1, 3, 0):
            at = along(p, order[0], d)
            pair = []
            for ref in ins:
                a = ref.at[at] if order[0] == "y" else ref.at[:, at]
                pair.append(a if cols == g.shape[3] else a.at[:, :, pl.ds(first, cols)])
            loads.append(copy(pair[0], mine.at[d], load.at[d]))
            loads.append(copy(pair[1], other.at[d], load.at[4 + d]))
        ways = (1, 3)
        for d in (2, 1, 3, 0):
            wait(loads[:2])
            loads = loads[2:]
            add_into(mine.at[d], [mine.at[d], other.at[d]], rows)
            if d == 2:
                copies = [
                    send(
                        mine.at[2, pl.ds(2 * n, 2)], half.at[n], s.at[n], r.at[n], dev(p, **{axis: w})
                    )
                    for n, w in enumerate(ways)
                ]
        yield
        wait(copies)
        copies = []
        for n, w in enumerate(ways):
            part = mine.at[w, pl.ds(2 * n, 2)]
            add_into(part, [part, half.at[n]], rows)
            copies.append(
                send(mine.at[w], got.at[n], s.at[2 + n], r.at[2 + n], dev(p, **{axis: w}))
            )
        yield
        wait(copies)
        add_into(other.at[0], [mine.at[0], got.at[0], got.at[1]], rows)
        if keep:
            return
        out = copy(other.at[0], outs[0], k.at[0])
        yield
        out.wait()

    return Op(
        [g, crossed],
        [(chunk, BF)],
        [
            pltpu.VMEM((4,) + chunk, BF),
            pltpu.VMEM((4,) + chunk, BF),
            pltpu.VMEM((2, 2, rows, cols), BF),
            pltpu.VMEM((2,) + chunk, BF),
            sems(8),
            sems(4),
            sems(4),
            sems(1),
        ],
        line_off(order[0], (1, 3)),
        run,
    )


def rs_second(part, order):
    rows, cols = part.shape[1:]
    one = (1, rows, cols)

    def run(p, ins, outs, scratch):
        own, got, total, k, s, r = scratch
        load = copy(ins[0].at[pl.ds(along(p, order[1], 0), 1)], own, k.at[0])
        copies = []
        for i, o in enumerate(line_off(order[1])):
            d = o["d" + order[1]]
            copies.append(
                send(
                    ins[0].at[pl.ds(along(p, order[1], d), 1)],
                    got.at[i],
                    s.at[i],
                    r.at[i],
                    dev(p, **o),
                )
            )
        yield
        load.wait()
        for c in copies:
            c.wait()
        add_into(total, [own, got.at[0], got.at[1], got.at[2]], rows)
        out = copy(total, outs[0], k.at[1])
        yield
        out.wait()

    return Op(
        [part],
        [(one, BF)],
        [
            pltpu.VMEM(one, BF),
            pltpu.VMEM((3,) + one, BF),
            pltpu.VMEM(one, BF),
            sems(2),
            sems(3),
            sems(3),
        ],
        line_off(order[1]),
        run,
    )


def share_x(part):
    rows, cols = part.shape[1:]

    def run(p, ins, outs, scratch):
        hold, k, s, r = scratch
        inward = copy(ins[0], hold, k.at[0])
        dst = outs[0].at[pl.ds(p.x, 1)]
        copies = [send(ins[0], dst, s.at[i], r.at[i], dev(p, **o)) for i, o in enumerate(X_OFF)]
        inward.wait()
        near = copy(hold, dst, k.at[1])
        yield
        near.wait()
        for c in copies:
            c.wait()

    return Op(
        [part],
        [((4, rows, cols), BF)],
        [pltpu.VMEM(part.shape, BF), sems(2), sems(3), sems(3)],
        X_OFF,
        run,
    )


def rs_end(part, order):
    rows, cols = part.shape[1:]
    one = (1, rows, cols)

    def run(p, ins, outs, scratch):
        own, got, total, k, s, r = scratch
        load = copy(ins[0].at[pl.ds(along(p, order[1], 0), 1)], own, k.at[0])
        copies = []
        for i, o in enumerate(line_off(order[1])):
            src = ins[0].at[pl.ds(along(p, order[1], o["d" + order[1]]), 1)]
            copies.append(send(src, got.at[i], s.at[i], r.at[i], dev(p, **o)))
        yield
        load.wait()
        wait(copies)
        add_into(total, [own, got.at[0], got.at[1], got.at[2]], rows)
        dst = outs[0].at[pl.ds(p.x, 1)]
        copies = [
            send(total, dst, s.at[3 + i], r.at[3 + i], dev(p, **o)) for i, o in enumerate(X_OFF)
        ]
        copies.append(copy(total, dst, k.at[1]))
        yield
        wait(copies)

    return Op(
        [part],
        [((4, rows, cols), BF)],
        [
            pltpu.VMEM(one, BF),
            pltpu.VMEM((3,) + one, BF),
            pltpu.VMEM(one, BF),
            sems(2),
            sems(6),
            sems(6),
        ],
        line_off(order[1]) + X_OFF,
        run,
    )


def series(*ops):
    def run(p, ins, outs, scratch):
        for n, op in enumerate(ops):
            here, outs = outs[: len(op.outs)], outs[len(op.outs) :]
            yield from op.run(p, ins, here, scratch[: len(op.scratch)])
            scratch = scratch[len(op.scratch) :]
            ins = here

    return Op(
        ops[0].ins,
        [o for op in ops for o in op.outs],
        [c for op in ops for c in op.scratch],
        [f for op in ops for f in op.offsets],
        run,
    )


def shaped(op):
    return jax.ShapeDtypeStruct(*op.outs[-1])


def rs_all(line, order):
    end = rs_end(shaped(line), order)
    n = len(line.scratch)

    def run(p, ins, outs, scratch):
        yield from line.run(p, ins, None, scratch[:n], True)
        yield from end.run(p, [scratch[1].at[0]], outs, scratch[n:])

    return Op(line.ins, end.outs, line.scratch + end.scratch, line.offsets + end.offsets, run)


def sum_all(*rows):
    shape = (8, D)
    hops = (("dy", (1, 2, 3)), ("dz", (1, 2, 3)), ("dc", (1,)), ("dx", (1, 2, 3)))

    def run(p, ins, outs, scratch):
        acc, got, k, s, r = scratch
        acc[0] = jnp.zeros(shape, F32)
        wait([copy(ins[i], acc.at[0, pl.ds(i, 1)], k.at[i]) for i in range(4)])
        at = 0
        for n, (axis, steps) in enumerate(hops):
            copies = []
            for i, d in enumerate(steps):
                j = at + i
                copies.append(send(acc.at[n], got.at[j], s.at[j], r.at[j], dev(p, **{axis: d})))
            yield
            wait(copies)
            total = acc[n]
            for i in range(len(steps)):
                total = total + got[at + i]
            acc[n + 1] = total
            at += len(steps)
        copy(acc.at[4], outs[0], k.at[0]).wait()

    return Op(
        rows,
        [(shape, F32)],
        [pltpu.VMEM((5,) + shape, F32), pltpu.VMEM((10,) + shape, F32), sems(4), sems(10), sems(10)],
        X_OFF + Y_OFF + Z_OFF + CORE_OFF,
        run,
    )


def pick(a, index, axis):
    return lax.dynamic_index_in_dim(a, index, axis, keepdims=False)


def rotated(y, cosine, sine):
    lane = lax.broadcasted_iota(jnp.int32, y.shape, 1)
    low = lax.rem(lane, HEAD) < HEAD // 2
    width = y.shape[1]
    turned = jnp.where(low, pltpu.roll(y, width - HEAD // 2, 1), pltpu.roll(y, HEAD // 2, 1))
    return y * cosine + turned * sine


def contract(a, b, da, db):
    return lax.dot_general(a, b, (((da,), (db,)), ((), ())), preferred_element_type=F32)


SCALE = HEAD ** (-0.5)


def masked(st, i):
    width = st.shape[0]
    key = lax.broadcasted_iota(jnp.int32, (256, 256), 0)
    query = lax.broadcasted_iota(jnp.int32, (256, 256), 1)
    last = jnp.where(key <= query, st[width - 256 :], NEG)
    return last if width == 256 else jnp.concatenate([st[: width - 256], last], axis=0)


def attend(qkv, out, lse):
    for i in range(4):
        rows = pl.ds(i * 256, 256)
        k = jnp.concatenate([qkv[j, :, 2 * HEAD : 3 * HEAD] for j in range(i + 1)], axis=0)
        v = jnp.concatenate([qkv[j, :, 3 * HEAD : 4 * HEAD] for j in range(i + 1)], axis=0)
        outs = []
        for n in range(2):
            q = qkv[i, :, n * HEAD : (n + 1) * HEAD]
            st = masked(contract(k, q, 1, 1) * SCALE, i)
            top = jnp.max(st, axis=0, keepdims=True)
            e = jnp.exp(st - top)
            total = jnp.sum(e, axis=0, keepdims=True)
            ot = contract(v, e.astype(BF), 0, 0)
            outs.append(ot * (1.0 / total))
            lse[n : n + 1, rows] = top + jnp.log(total)
        out[i] = jnp.concatenate(outs, axis=0).T.astype(BF)


def attend_back(qkv, do, lse, out, dq, dk, dv):
    dk[...] = jnp.zeros_like(dk)
    dv[...] = jnp.zeros_like(dv)
    for i in range(4):
        rows = pl.ds(i * 256, 256)
        width = (i + 1) * 256
        k = jnp.concatenate([qkv[j, :, 2 * HEAD : 3 * HEAD] for j in range(i + 1)], axis=0)
        v = jnp.concatenate([qkv[j, :, 3 * HEAD : 4 * HEAD] for j in range(i + 1)], axis=0)
        for n in range(2):
            cols = slice(n * HEAD, (n + 1) * HEAD)
            q, go = qkv[i, :, cols], do[i, :, cols]
            st = masked(contract(k, q, 1, 1) * SCALE, i)
            pr = jnp.exp(st - lse[n : n + 1, rows])
            dpt = contract(v, go, 1, 1)
            delta = jnp.sum(pr * dpt, axis=0, keepdims=True)
            ds = (pr * (dpt - delta)).astype(BF)
            dq[cols, rows] = contract(k, ds, 0, 0)
            dk[:width] += jnp.dot(ds, q, preferred_element_type=F32)
            dv[:width] += jnp.dot(pr.astype(BF), go, preferred_element_type=F32)
    for i in range(4):
        rows = pl.ds(i * 256, 256)
        g = jnp.concatenate([dq[:, rows].T * SCALE, dk[rows] * SCALE, dv[rows]], axis=1)
        out[i] = g.astype(BF)


def sigmoid(v):
    return 1.0 / (1.0 + jnp.exp(-v))


def row_scale(h):
    return lax.rsqrt(jnp.mean(h * h, axis=-1, keepdims=True) + EPS)


def own_rows(x):
    return pl.ds(pl.multiple_of(x * 64, 64), 64)


def tables(tab):
    cosine, sine = tab[:, :48], tab[:, 48:96]
    one = jnp.ones((tab.shape[0], 96), F32)
    return (
        jnp.concatenate([cosine] * 6 + [one], axis=1),
        jnp.concatenate([-sine, sine] * 3 + [one * 0.0], axis=1),
    )


GAINS = (4, 4, 2, 16, 128)


def gain_row(gains, k):
    rows = [
        gains[y, j, c, k : k + 1, :48].astype(F32)
        for y in range(4)
        for j in range(4)
        for c in range(2)
    ]
    return jnp.concatenate(rows, axis=1)


class Links:
    def __init__(self, p, s, r, k):
        self.p, self.s, self.r, self.k, self.n, self.m = p, s, r, k, 0, 0

    def to(self, src, dst, target):
        c = send(src, dst, self.s.at[self.n], self.r.at[self.n], target)
        self.n += 1
        return c

    def near(self, src, dst):
        c = copy(src, dst, self.k.at[self.m])
        self.m += 1
        return c


def wait(copies):
    for c in copies:
        c.wait()


def rows_of(s, size=256, first=0):
    return pl.ds(pl.multiple_of(s * size + first, 64), size)


def gather_half(net, s, own, dst):
    at = dst.at[pl.ds(pl.multiple_of(s * 256 + net.p.x * 64, 64), 64)]
    return [net.to(own.at[s], at, dev(net.p, **o)) for o in X_OFF] + [net.near(own.at[s], at)]


def gather_halves(net, own, dst, order=(0, 1)):
    return [gather_half(net, s, own, dst) for s in order]


def scatter_half(net, s, part, terms):
    copies = []
    for i, o in enumerate(X_OFF):
        t = dev(net.p, **o)
        src = part.at[pl.ds(pl.multiple_of(s * 256 + t[2] * 64, 64), 64)]
        copies.append(net.to(src, terms.at[i, s], t))
    return copies


def summed(x, s, part, terms):
    own = part[pl.ds(pl.multiple_of(s * 256 + x * 64, 64), 64)].astype(F32)
    return own + terms[0, s].astype(F32) + terms[1, s].astype(F32) + terms[2, s].astype(F32)


def swap_units(net, un, qv, offsets):
    copies = []
    for o in offsets:
        t = dev(net.p, **o)
        copies.append(net.to(un.at[t[1]], qv.at[net.p.ctx], t))
    return copies


CTX_FAR, CTX_NEAR = CTX_OFF[:2], CTX_OFF[2:]
SEQ_NEAR = [o for o in SEQ_OFF if o["dz"] == 0]
SEQ_FAR = [o for o in SEQ_OFF if o["dz"] == 2]


def columns(whole, cols):
    w = whole[:, :, :, :, cols]
    return w.reshape(32 * w.shape[3], w.shape[4])


N_SEMS = 96
LINK_SCRATCH = [sems(N_SEMS), sems(N_SEMS), sems(N_SEMS)]


def forward_op(l, normed, w_qkv, tabs, wholes, hidden, gains, cotangent=None, gradient=None):
    last = l == LAYERS - 1
    ins = [normed, w_qkv, tabs, hidden, gains] + list(wholes)
    if last:
        ins += [cotangent, gradient]
    outs = dict(
        qv=((4, 256, 384), BF),
        lse=((2, 1024), F32),
        tok=((128, D), BF),
        res=((128, D), F32),
        xg=((512, D), BF),
    )
    if last:
        outs.update(pt2=((512, D), BF), **MLP_BACK_OUTS)
    else:
        outs.update(x2=((512, D), BF))
        outs.update(gu=((512, 2048), F32))
        outs.update(ac=((512, 1024), BF))
        outs.update(hid=((2, 64, D), F32))
        outs.update(nxt=((2, 64, D), BF))
    names = list(outs)
    scratch = dict(
        xg=((512, D), BF),
        wq=(w_qkv.shape, BF),
        tab=((512, 128), F32),
        cs=((512, 384), F32),
        sn=((512, 384), F32),
        un=((4, 256, 384), BF),
        qv=((4, 256, 384), BF),
        lse=((2, 1024), F32),
        mx=((4, 256, 192), BF),
        mr=((8, 128, 192), BF),
        tok=((128, D), BF),
        wo=(wholes[0].shape, BF),
        wo2=(wholes[1].shape, BF),
        hid=((2, 64, D), F32),
        res=((128, D), F32),
        n2=((2, 64, D), BF),
        x2=((512, D), BF),
        wg=(wholes[3].shape, BF),
        wu=(wholes[4].shape, BF),
        wd=(wholes[2].shape, BF),
        ac=((512, 1024), BF),
        pt=((512, D), BF),
        tm=((3, 2, 64, D), BF),
        gains=(GAINS, BF),
        nxt=((2, 64, D), BF),
    )
    if last:
        scratch.update(pt2=((512, D), BF), gb=((512, D), BF), **MLP_BACK_SCRATCH)
    else:
        scratch.update(gu=((512, 2048), F32))
    keys = list(scratch)

    def run(p, ins, out_refs, refs):
        v = named(keys, refs)
        net = Links(p, *refs[len(keys) :])
        o = named(names, out_refs)
        whole = ins[5:10]
        x = p.x
        saves = []

        def save(src, dst):
            saves.append(net.near(src, dst))

        there, here = 1 - p.zhi, p.zhi
        if l:
            halves = gather_halves(net, ins[0], v.xg, (there, here))
            cots = gather_halves(net, ins[10], v.gb, (here, there))
        else:
            halves = [
                [
                    net.near(ins[0].at[s, k], v.xg.at[rows_of(s * 4 + k, 64)])
                    for k in range(4)
                ]
                for s in (there, here)
            ]
        early = [net.near(ins[1], v.wq), net.near(ins[4], v.gains)]
        for s in range(2):
            for k in range(4):
                early.append(
                    net.near(
                        ins[2].at[k, pl.ds(64 * s, 64)],
                        v.tab.at[pl.ds(s * 256 + k * 64, 64)],
                    )
                )
        late = [net.near(ins[3], v.hid if l else v.nxt)]
        yield
        wait(early)
        cosine, sine = tables(v.tab[...])
        v.cs[...] = cosine
        v.sn[...] = sine
        moves = []
        for n, s in enumerate((there, here)):
            wait(halves[n])
            rows = rows_of(s)
            if not l:
                gain = gain_row(v.gains, 0)
                for k in range(4):
                    part = rows_of(s * 4 + k, 64)
                    h = v.xg[part].astype(F32)
                    v.xg[part] = (h * row_scale(h) * gain).astype(BF)
            for u in range(2):
                y = jnp.dot(
                    v.xg[rows], columns(v.wq, slice(u * 384, u * 384 + 384)), preferred_element_type=F32
                )
                v.un[s * 2 + u] = rotated(y, v.cs[rows], v.sn[rows]).astype(BF)
            moves += swap_units(net, v.un, v.qv, (CTX_FAR, CTX_NEAR)[n])
            if n == 0:
                yield
        v.qv[pl.ds(p.ctx, 1)] = v.un[pl.ds(p.ctx, 1)]
        save(v.xg, o.xg)
        yield
        wait(moves)
        save(v.qv, o.qv)
        attend(v.qv, v.mx, v.lse)
        save(v.lse, o.lse)
        moves = []
        for offsets in (SEQ_NEAR, SEQ_FAR):
            group = []
            for off in offsets:
                t = dev(p, **off)
                group.append(
                    net.to(
                        v.mx.at[t[1], own_rows(t[2])],
                        v.mr.at[p.x * 2 + p.core, own_rows(p.zhi)],
                        t,
                    )
                )
            moves.append(group)
        v.mr[pl.ds(x * 2 + p.core, 1), own_rows(p.zhi)] = v.mx[
            pl.ds(p.ctx, 1), own_rows(x)
        ]
        yield
        load = [net.near(whole[0], v.wo), net.near(whole[1], v.wo2)]
        gain = gain_row(v.gains, 2 + l)
        wait(load)
        wait(late)
        if not l:
            v.hid[...] = v.nxt[...].astype(F32)
        halves = []
        for n, s in enumerate((here, there)):
            wait(moves[n])
            rows = rows_of(s, 64)
            v.tok[rows] = jnp.concatenate([v.mr[g, rows] for g in range(8)], axis=1)
            for c in range(2):
                cols = slice(c * 768, (c + 1) * 768)
                w = columns((v.wo, v.wo2)[c], slice(None))
                v.res[rows, cols] = v.hid[s, :, cols] + jnp.dot(
                    v.tok[rows], w, preferred_element_type=F32
                )
            h = v.res[rows]
            v.n2[s] = (h * row_scale(h) * gain).astype(BF)
            halves.append(gather_half(net, s, v.n2, v.x2))
        save(v.tok, o.tok)
        save(v.res, o.res)
        yield
        yield
        loads = [net.near(whole[3], v.wg), net.near(whole[4], v.wu)]
        wait(loads)
        if last:
            net.near(whole[2], v.wd).wait()
            backs = []
            for n, s in enumerate((here, there)):
                wait(halves[n])
                wait(cots[n])
                rows = rows_of(s)
                for j in range(2):
                    cols, high = slice(j * 512, (j + 1) * 512), slice(1024 + j * 512, 1536 + j * 512)
                    gate = jnp.dot(v.x2[rows], columns(v.wg, cols), preferred_element_type=F32)
                    up = jnp.dot(v.x2[rows], columns(v.wu, cols), preferred_element_type=F32)
                    sg = sigmoid(gate)
                    v.ac[rows, cols] = (gate * sg * up).astype(BF)
                    ga = contract(v.gb[rows], v.wd[2 * j : 2 * j + 2].reshape(512, D), 1, 1)
                    v.dgu[rows, cols] = (ga * up * sg * (1.0 + gate * (1.0 - sg))).astype(BF)
                    v.dgu[rows, high] = (ga * gate * sg).astype(BF)
                yield
                for c in range(4):
                    cols = slice(c * 384, (c + 1) * 384)
                    g = contract(v.dgu[rows, :1024], v.wg[c].reshape(384, 1024), 1, 1)
                    g = g + contract(v.dgu[rows, 1024:], v.wu[c].reshape(384, 1024), 1, 1)
                    v.pt[rows, cols] = g.astype(BF)
                backs.append(scatter_half(net, s, v.pt, v.tm))
                yield

            def forward_part():
                for c in range(3):
                    cols = slice(c * 512, (c + 1) * 512)
                    v.pt2[:, cols] = jnp.dot(
                        v.ac[...], columns(v.wd, cols), preferred_element_type=F32
                    ).astype(BF)
                save(v.pt2, o.pt2)

            loads = [net.near(ins[11], v.gr)]
            yield from mlp_back_rest(
                net, o, v, loads, backs, (here, there), l, True, forward_part, saves
            )
            return
        backs = []
        for n, s in enumerate((here, there)):
            wait(halves[n])
            rows = rows_of(s)
            for j in range(2):
                cols, more = slice(j * 512, (j + 1) * 512), slice(1024 + j * 512, 1536 + j * 512)
                gate = jnp.dot(v.x2[rows], columns(v.wg, cols), preferred_element_type=F32)
                up = jnp.dot(v.x2[rows], columns(v.wu, cols), preferred_element_type=F32)
                v.gu[rows, cols] = gate
                v.gu[rows, more] = up
                v.ac[rows, cols] = (gate * sigmoid(gate) * up).astype(BF)
            yield
            if n == 0:
                net.near(whole[2], v.wd).wait()
            for c in range(3):
                cols = slice(c * 512, (c + 1) * 512)
                v.pt[rows, cols] = jnp.dot(
                    v.ac[rows], columns(v.wd, cols), preferred_element_type=F32
                ).astype(BF)
            backs.append(scatter_half(net, s, v.pt, v.tm))
            yield
        save(v.x2, o.x2)
        save(v.gu, o.gu)
        save(v.ac, o.ac)
        gain = gain_row(v.gains, 1)
        for n, s in enumerate((here, there)):
            wait(backs[n])
            h = v.res[rows_of(s, 64)] + summed(x, s, v.pt, v.tm)
            v.hid[s] = h
            if last:
                v.nxt[s] = h.astype(BF)
            else:
                v.nxt[s] = (h * row_scale(h) * gain).astype(BF)
        save(v.hid, o.hid)
        save(v.nxt, o.nxt)
        yield
        wait(saves)

    return names, Op(
        ins,
        list(outs.values()),
        [pltpu.VMEM(*scratch[k]) for k in keys] + LINK_SCRATCH,
        X_OFF + CTX_OFF + SEQ_OFF,
        run,
    )


def norm_back_rows(h, gain, upstream):
    scale = row_scale(h)
    unit = h * scale
    weighted = upstream * gain
    back = scale * (weighted - unit * jnp.mean(weighted * unit, axis=-1, keepdims=True))
    return back, jnp.sum(upstream * unit, axis=0, keepdims=True)


def cross(net, g, mine, crossed):
    p = net.p
    return [
        net.to(g.at[:, :, 1 - p.core], crossed, dev(p, dc=1)),
        net.near(g.at[:, :, p.core], mine),
    ]


MLP_BACK_OUTS = dict(
    md=((4, 4, 32, D), BF),
    cd=((4, 4, 32, D), BF),
    mg=((4, 4, 48, 2048), BF),
    cg=((4, 4, 48, 2048), BF),
    mo=((4, 4, 48, D), BF),
    co=((4, 4, 48, D), BF),
    gr=((128, D), F32),
    gg=((1, D), F32),
    gm=((8, 128, 192), BF),
)
MLP_BACK_SCRATCH = dict(
    gr=((128, D), F32),
    dgu=((512, 2048), BF),
    gd=((4, 4, 2, 32, D), BF),
    gg2=((4, 4, 2, 48, 2048), BF),
    go=((4, 4, 2, 48, D), BF),
    rb=((128, D), BF),
    gg=((1, D), F32),
    gm=((8, 128, 192), BF),
)


def mlp_back_rest(net, o, v, loads, backs, order, l, whole, filler, ends):
    x = net.p.x
    wait(loads)
    for i in range(4):
        for c in range(3):
            cols = slice(c * 512, (c + 1) * 512)
            g = contract(v.ac[:, i * 256 : (i + 1) * 256], v.gb[:, cols], 0, 0)
            v.gd[i, :, :, :, cols] = g.astype(BF).reshape(4, 2, 32, 512)
    ends += cross(net, v.gd, o.md, o.cd)
    for i in range(4):
        for c in range(4):
            cols = slice(c * 512, (c + 1) * 512)
            g = contract(v.x2[:, i * 384 : (i + 1) * 384], v.dgu[:, cols], 0, 0)
            v.gg2[i, :, :, :, cols] = g.astype(BF).reshape(4, 2, 48, 512)
    ends += cross(net, v.gg2, o.mg, o.cg)
    filler()
    yield
    total = jnp.zeros((1, D), F32)
    gain = gain_row(v.gains, 2 + l)
    for n, s in enumerate(order):
        wait(backs[n])
        rows = rows_of(s, 64)
        back, gain_grad = norm_back_rows(v.res[rows], gain, summed(x, s, v.pt, v.tm))
        total = total + gain_grad
        gr = v.gr[rows] + back
        v.gr[rows] = gr
        v.rb[rows] = gr.astype(BF)
    v.gg[...] = total
    ends += [net.near(v.gr, o.gr), net.near(v.gg, o.gg)]
    for i in range(4):
        for c in range(3):
            cols = slice(c * 512, (c + 1) * 512)
            g = contract(v.tok[:, i * 384 : (i + 1) * 384], v.rb[:, cols], 0, 0)
            v.go[i, :, :, :, cols] = g.astype(BF).reshape(4, 2, 48, 512)
    ends += cross(net, v.go, o.mo, o.co)
    for j in range(4):
        if whole:
            w = [a[j].reshape(384, 768) for a in (v.wo, v.wo2)]
        else:
            w = [a[j * 384 : (j + 1) * 384] for a in (v.wo, v.wo2)]
        g = contract(v.rb[:, :768], w[0], 1, 1)
        g = (g + contract(v.rb[:, 768:], w[1], 1, 1)).astype(BF)
        v.gm[2 * j] = g[:, :192]
        v.gm[2 * j + 1] = g[:, 192:]
    ends += [net.near(v.gm, o.gm)]
    yield
    wait(ends)


def mlp_back_op(
    l, grad_b, gradient, w_gate, w_up, w_down, w_out, w_out2, gu, ac, x2, res, tok, gains
):
    ins = [grad_b, gradient, w_gate, w_down, w_out, gu, ac, x2, res, tok, gains, w_out2, w_up]
    outs = MLP_BACK_OUTS
    names = list(outs)
    scratch = dict(
        gb=((512, D), BF),
        wg=((D, 1024), BF),
        wu=((D, 1024), BF),
        wd=((1024, D), BF),
        wo=((D, 768), BF),
        wo2=((D, 768), BF),
        gu=((512, 2048), F32),
        ac=((512, 1024), BF),
        x2=((512, D), BF),
        res=((128, D), F32),
        tok=((128, D), BF),
        gains=(GAINS, BF),
        pt=((512, D), BF),
        tm=((3, 2, 64, D), BF),
        **MLP_BACK_SCRATCH,
    )
    keys = list(scratch)

    def run(p, ins, out_refs, refs):
        v = named(keys, refs)
        net = Links(p, *refs[len(keys) :])
        o = named(names, out_refs)
        x = p.x
        halves = gather_halves(net, ins[0], v.gb)
        loads = [net.near(ins[3], v.wd), net.near(ins[5], v.gu), net.near(ins[2], v.wg)]
        loads.append(net.near(ins[12], v.wu))
        more = [
            net.near(ins[6], v.ac),
            net.near(ins[7], v.x2),
            net.near(ins[8], v.res),
            net.near(ins[1], v.gr),
            net.near(ins[10], v.gains),
            net.near(ins[4], v.wo),
            net.near(ins[11], v.wo2),
            net.near(ins[9], v.tok),
        ]
        yield
        wait(loads[:2])
        backs = []
        for s in range(2):
            wait(halves[s])
            rows = pl.ds(s * 256, 256)
            for j in range(2):
                cols, high = slice(j * 512, (j + 1) * 512), slice(1024 + j * 512, 1536 + j * 512)
                ga = contract(v.gb[rows], v.wd[cols], 1, 1)
                gate, up = v.gu[rows, cols], v.gu[rows, high]
                sg = sigmoid(gate)
                v.dgu[rows, cols] = (ga * up * sg * (1.0 + gate * (1.0 - sg))).astype(BF)
                v.dgu[rows, high] = (ga * gate * sg).astype(BF)
            if s == 0:
                wait(loads[2:])
            for c in range(3):
                cols = slice(c * 512, (c + 1) * 512)
                g = contract(v.dgu[rows, :1024], v.wg[cols], 1, 1)
                g = g + contract(v.dgu[rows, 1024:], v.wu[cols], 1, 1)
                v.pt[rows, cols] = g.astype(BF)
            backs.append(scatter_half(net, s, v.pt, v.tm))
            yield
        yield from mlp_back_rest(net, o, v, more, backs, (0, 1), l, False, lambda: None, [])

    return names, Op(
        ins,
        list(outs.values()),
        [pltpu.VMEM(*scratch[k]) for k in keys] + LINK_SCRATCH,
        X_OFF + CORE_OFF,
        run,
    )


def attend_back_op(l, gm, qv, lse, tabs, w_qkv, xg, hidden, gains, gr):
    ins = [gm, qv, lse, tabs, w_qkv, xg, hidden, gains, gr]
    outs = dict(
        mq=((4, 4, 48, 768), BF),
        cq=((4, 4, 48, 768), BF),
        gr=((2, 64, D), F32),
        gb=((2, 64, D), BF),
        gg=((1, D), F32),
    )
    names = list(outs)
    scratch = dict(
        do=((4, 256, 192), BF),
        qv=((4, 256, 384), BF),
        lse=((2, 1024), F32),
        tab=((512, 128), F32),
        cs=((512, 384), F32),
        sn=((512, 384), F32),
        un=((4, 256, 384), BF),
        dqkv=((4, 256, 384), BF),
        dq=((192, 1024), F32),
        dk=((1024, HEAD), F32),
        dv=((1024, HEAD), F32),
        wq=((D, 768), BF),
        xg=((512, D), BF),
        hid=((2, 64, D), F32),
        gains=(GAINS, BF),
        gr=((2, 64, D), F32),
        gb=((2, 64, D), BF),
        gg=((1, D), F32),
        pt=((512, D), BF),
        tm=((3, 2, 64, D), BF),
        gq=((4, 4, 2, 48, 768), BF),
    )
    keys = list(scratch)

    def run(p, ins, out_refs, refs):
        v = named(keys, refs)
        net = Links(p, *refs[len(keys) :])
        o = named(names, out_refs)
        x = p.x
        dst = v.do.at[p.ctx, own_rows(x)]
        moves = []
        for off in SEQ_OFF:
            t = dev(p, **off)
            src = ins[0].at[t[2] * 2 + lax.rem(t[1], 2), own_rows(lax.div(t[1], 2))]
            moves.append(net.to(src, dst, t))
        moves.append(net.near(ins[0].at[x * 2 + p.core, own_rows(p.zhi)], dst))
        moves += [net.near(ins[1], v.qv), net.near(ins[2], v.lse)]
        tabs = []
        for n in range(2):
            for k in range(4):
                tabs.append(
                    net.near(
                        ins[3].at[k, pl.ds(64 * n, 64)],
                        v.tab.at[pl.ds(n * 256 + k * 64, 64)],
                    )
                )
        loads = [net.near(ins[4], v.wq), net.near(ins[5], v.xg), net.near(ins[6], v.hid)]
        loads += [net.near(ins[7], v.gains), net.near(ins[8], v.gr)]
        wait(tabs)
        cosine, sine = tables(v.tab[...])
        v.cs[...] = cosine
        v.sn[...] = sine
        yield
        wait(moves)
        attend_back(v.qv, v.do, v.lse, v.un, v.dq, v.dk, v.dv)
        there, here = 1 - p.zhi, p.zhi
        far = swap_units(net, v.un, v.dqkv, CTX_FAR)
        near = swap_units(net, v.un, v.dqkv, CTX_NEAR)
        v.dqkv[pl.ds(p.ctx, 1)] = v.un[pl.ds(p.ctx, 1)]
        yield
        wait(loads)
        backs = []
        for n, s in enumerate((here, there)):
            wait((near, far)[n])
            rows = rows_of(s)
            for u in range(2):
                g = v.dqkv[2 * s + u].astype(F32)
                v.dqkv[2 * s + u] = rotated(g, v.cs[rows], -v.sn[rows]).astype(BF)
            d = jnp.concatenate([v.dqkv[2 * s], v.dqkv[2 * s + 1]], axis=1)
            for c in range(3):
                cols = slice(c * 512, (c + 1) * 512)
                v.pt[rows, cols] = contract(d, v.wq[cols], 1, 1).astype(BF)
            backs.append(scatter_half(net, s, v.pt, v.tm))
        yield
        for u in range(2):
            d = jnp.concatenate([v.dqkv[u], v.dqkv[2 + u]], axis=0)
            for i in range(4):
                g = contract(v.xg[:, i * 384 : (i + 1) * 384], d, 0, 0)
                cols = slice(u * 384, (u + 1) * 384)
                v.gq[i, :, :, :, cols] = g.astype(BF).reshape(4, 2, 48, 384)
        ends = cross(net, v.gq, o.mq, o.cq)
        yield
        total = jnp.zeros((1, D), F32)
        gain = gain_row(v.gains, l)
        for n, s in enumerate((here, there)):
            wait(backs[n])
            back, gain_grad = norm_back_rows(v.hid[s], gain, summed(x, s, v.pt, v.tm))
            total = total + gain_grad
            gr = v.gr[s] + back
            v.gr[s] = gr
            v.gb[s] = gr.astype(BF)
        v.gg[...] = total
        ends += [net.near(v.gr, o.gr), net.near(v.gb, o.gb), net.near(v.gg, o.gg)]
        yield
        wait(ends)

    return names, Op(
        ins,
        list(outs.values()),
        [pltpu.VMEM(*scratch[k]) for k in keys] + LINK_SCRATCH,
        X_OFF + CTX_OFF + SEQ_OFF,
        run,
    )


def rope_rows(positions):
    half = HEAD // 2
    frequency = BASE ** (-(jnp.arange(half, dtype=F32) * 2.0 / HEAD))
    angles = positions.astype(F32)[:, None] * frequency
    return jnp.concatenate([jnp.cos(angles), jnp.sin(angles), jnp.zeros((128, 32), F32)], axis=1)


def unpack_kernel(*refs):
    ins, outs, holds, sem = refs[: 7 * LAYERS], refs[7 * LAYERS : -8], refs[-8:-1], refs[-1]
    row, col = iotas((512, 512))
    place_of = lax.rem(row, 128) // 32 * 128 + row // 128 * 32 + lax.rem(row, 32)
    turn = mask_matrix(place_of == col)
    copies = []

    def done(l, n):
        copies.append(copy(holds[n].at[l], outs[n].at[l], sem.at[7 * l + n]))

    q_ref, k_ref, v_ref, o_ref, gate_ref, up_ref, down_ref = holds
    for l in reversed(range(LAYERS)):
        u0, u1, out, out2, down, gate, up = ins[7 * l : 7 * l + 7]
        for x in range(4):
            down_ref[l, x * 32 : (x + 1) * 32] = down[x].astype(F32)
        done(l, 6)
        for n, half in enumerate((out, out2)):
            o_ref[l, :, n * 768 : (n + 1) * 768] = (
                half[0].astype(F32) + half[1].astype(F32)
            ) + (half[2].astype(F32) + half[3].astype(F32))
        done(l, 3)
        for n, part, ref in ((4, gate, gate_ref), (5, up, up_ref)):
            for t in range(8):
                at = t * 128
                piece = jnp.concatenate([part[x, :, at : at + 128] for x in range(4)], axis=1)
                ref[l, :, t * 512 : (t + 1) * 512] = jnp.dot(
                    piece, turn, preferred_element_type=F32
                )
            done(l, n)
        for n, ref, at, width in ((0, q_ref, 0, 192), (1, k_ref, 192, 96), (2, v_ref, 288, 96)):
            ref[l] = jnp.concatenate(
                [u[x, :, at : at + width] for x in range(4) for u in (u0, u1)], axis=1
            ).astype(F32)
            done(l, n)
    wait(copies)


def unpack(ends):
    sizes = [(48, D), (48, 768), (48, 768), (48, D), (48, 4096), (48, 4096), (128, D)]
    return pl.pallas_call(
        unpack_kernel,
        out_shape=[jax.ShapeDtypeStruct((LAYERS,) + z, F32) for z in sizes],
        out_specs=[pl.BlockSpec(memory_space=pl.ANY)] * 7,
        scratch_shapes=[pltpu.VMEM((LAYERS,) + z, F32) for z in sizes] + [sems(7 * LAYERS)],
        compiler_params=pltpu.CompilerParams(vmem_limit_bytes=VMEM_LIMIT),
        cost_estimate=pl.CostEstimate(flops=10**9, bytes_accessed=10**7, transcendentals=0),
    )(*ends)


RS_UNIT, RS_UNIT2, RS_DOWN, RS_GATE, RS_UP, RS_OUT, RS_OUT2 = "yz", "zy", "yz", "yz", "zy", "yz", "zy"


def per_device(
    inputs,
    positions,
    cotangent,
    attn_gain,
    query_weight,
    key_matrix,
    value_matrix,
    out_weight,
    mlp_gain,
    gate_weight,
    up_weight,
    down_weight,
):
    p = place()

    def shard(l, which, packed=None):
        if which == "qkv":
            return ag_first(From(packed), "zy", (48, 768), lambda r, p: r), "zy"
        if which in ("gate", "up"):
            order, at = "zy", 1024 * (which == "up")
            return ag_first(From(packed), order, (48, 1024), lambda r, p: r.at[:, pl.ds(at, 1024)]), order
        if which == "down":
            view = lambda r, p: r.at[l, pl.ds(pl.multiple_of(p.x * 32, 32), 32)]
            return ag_first(down_weight, "yz", (32, D), view), "yz"
        half = 768 * (which == "out2")
        order = "zy" if half else "yz"
        view = lambda r, p: r.at[l, :, pl.ds(half, 768)]
        return ag_first(out_weight, order, (48, 768), view), order

    gains = jnp.pad(jnp.concatenate([attn_gain, mlp_gain], axis=0), ((0, 12), (0, 80)))

    saved = []
    whole = []
    tokens = timed(gather_x(inputs), 0, 4)
    tab = timed(rows_x(rope_rows(positions.reshape(128))), 0, 4)
    gain = timed(ag_all(ag_first(gains, "zy", (16, 128), lambda r, p: r), "zy"), 0, 1, 2, 3, 4)
    packs = [
        pack_qkv(0, query_weight, key_matrix, value_matrix),
        timed(pack_gu(0, gate_weight, up_weight), 1),
    ]
    packs[0].early = True
    w = [
        timed(ag_all(*shard(0, "qkv", packs[0])), 0, 1, 2, 3, 4),
        timed(ag_all(*shard(0, "out")), 0, 1, 3, 7, 8),
        timed(ag_all(*shard(0, "out2")), 1, 3, 4, 7, 8),
        timed(ag_all(*shard(0, "down")), 0, 2, 9, 10, 11),
        timed(ag_all(*shard(0, "gate", packs[1])), 1, 4, 8, 9, 10),
        timed(ag_all(*shard(0, "up", packs[1])), 1, 4, 8, 9, 10),
    ]
    names, fg = forward_op(
        0, From(tokens), From(w[0]), From(tab), [From(a) for a in w[1:]], inputs, From(gain)
    )
    late = [
        timed(pack_qkv(1, query_weight, key_matrix, value_matrix), 6),
        timed(pack_gu(1, gate_weight, up_weight), 6),
    ]
    nxt = [
        timed(ag_all(*shard(1, "qkv", late[0])), 9, 11, 12, 13, 15),
        timed(shard(1, "out")[0], 9, 14),
        timed(shard(1, "out2")[0], 9, 14),
        timed(shard(1, "down")[0], 9, 14),
        timed(shard(1, "gate", late[1])[0], 9, 14),
        timed(shard(1, "up", late[1])[0], 9, 14),
    ]
    fg = timed(fg, 4)
    ops = packs[:1] + w[:1] + [gain] + w[1:3] + [tokens, tab] + packs[1:] + w[4:] + w[3:4] + [fg] + late + nxt
    done = dict(zip(map(id, ops), build(1, ops)))
    whole.append([done[id(a)][0] for a in w])
    tabs, gains_g = done[id(tab)][0], done[id(gain)][0]
    kept = named(names, done[id(fg)])
    kept.hidden = inputs.astype(F32)
    saved.append(kept)
    second = [done[id(a)][0] for a in nxt]
    hidden = kept.hid
    w = [
        timed(ag_rest(second[1], "yz"), 0, 1, 3, 4),
        timed(ag_rest(second[2], "zy"), 0, 1, 3, 4),
        timed(ag_rest(second[3], "yz"), 0, 3, 4, 5),
        timed(ag_rest(second[4], "zy"), 1, 4, 5, 6),
        timed(ag_rest(second[5], "zy"), 2, 4, 5, 6),
    ]
    names, fg = forward_op(
        1, kept.nxt, second[0], tabs, [From(a) for a in w], hidden, gains_g,
        cotangent, cotangent.astype(F32).reshape(128, D),
    )
    done = build(2, w + [fg])
    whole.append([second[0]] + [d[0] for d in done[:5]])
    kept = named(names, done[5])
    kept.hidden = hidden
    saved.append(kept)

    ends = [None] * LAYERS
    gain_grads = [None] * 4
    for l in reversed(range(LAYERS)):
        kept = saved[l]
        w_qkv, w_out, w_out2, w_down, w_gate, w_up = [
            a.reshape(32 * a.shape[3], a.shape[4]) for a in whole[l]
        ]
        if l == 1:
            names = list(MLP_BACK_OUTS)
            r = [getattr(kept, k) for k in names]
        else:
            names, fg = mlp_back_op(
                l, grad_b, gradient.reshape(128, D), w_gate, w_up, w_down, w_out, w_out2, kept.gu,
                kept.ac, kept.x2, kept.res, kept.tok, gains_g,
            )
            r, (gate,), (up,), (down,), (part_u,), (part_u2,), (part_out,), (part_out2,) = build(
                5,
                [
                    fg,
                    timed(rs_second(part_gate, RS_GATE), 0, 4, 5),
                    timed(rs_second(part_up, RS_UP), 0, 4, 5),
                    timed(rs_second(part_down, RS_DOWN), 0, 4, 5),
                    timed(rs_line(q.mq, q.cq, RS_UNIT, 0, 384), 0, 4, 5),
                    timed(rs_line(q.mq, q.cq, RS_UNIT2, 384, 384), 0, 4, 5),
                    timed(rs_line(r.mo, r.co, RS_OUT, 0, 768), 0, 4, 5),
                    timed(rs_line(r.mo, r.co, RS_OUT2, 768, 768), 0, 4, 5),
                ],
            )
            thirds = [down, gate, up]
        r = named(names, r)
        gain_grads[2 + l] = r.gg
        names, fg = attend_back_op(
            l, r.gm, kept.qv, kept.lse, tabs, w_qkv, kept.xg, kept.hidden, gains_g,
            r.gr.reshape(2, 64, D),
        )
        if l == 1:
            out = timed(output_op(kept.pt2, kept.res), 0, 2)
            bg = [
                timed(rs_line(r.mg, r.cg, RS_GATE, 0, 1024), 0, 4, 5),
                timed(rs_line(r.md, r.cd, RS_DOWN), 0, 4, 5),
                timed(rs_line(r.mg, r.cg, RS_UP, 1024, 1024), 1, 4, 5),
            ]
            q, (output,), (part_gate,), (part_down,), (part_up,) = build(6, [fg, out] + bg)
        else:
            first = [
                timed(rs_end(part_u, RS_UNIT), 0, 1, 4),
                timed(rs_end(part_u2, RS_UNIT2), 0, 1, 4),
                timed(rs_end(part_out, RS_OUT), 0, 1, 4),
                timed(rs_end(part_out2, RS_OUT2), 0, 1, 4),
                *[timed(share_x(a), 0, 3) for a in thirds],
            ]
            bg = [
                timed(rs_ring(r.mg, r.cg, RS_GATE, 0, 1024), 0, 1, 4, 5),
                timed(rs_ring(r.md, r.cd, RS_DOWN), 0, 1, 4, 5),
                timed(rs_ring(r.mo, r.co, RS_OUT, 0, 768), 0, 1, 4, 5),
                timed(rs_ring(r.mg, r.cg, RS_UP, 1024, 1024), 1, 2, 4, 5),
                timed(rs_ring(r.mo, r.co, RS_OUT2, 768, 768), 1, 2, 4, 5),
            ]
            q, *rest = build(7, [fg] + first + bg)
            ends[1] = [a[0] for a in rest[:7]]
            part_gate, part_down, part_out, part_up, part_out2 = [a[0] for a in rest[7:]]
        q = named(names, q)
        gain_grads[l] = q.gg
        gradient, grad_b = q.gr, q.gb

    tail = build(
        8,
        [
            sum_all(*gain_grads),
            timed(rs_end(part_gate, RS_GATE), 0, 1, 4),
            timed(rs_end(part_down, RS_DOWN), 0, 1, 4),
            timed(rs_end(part_up, RS_UP), 0, 1, 4),
            timed(rs_end(part_out, RS_OUT), 0, 1, 4),
            timed(rs_end(part_out2, RS_OUT2), 0, 1, 4),
            timed(rs_all(rs_line(q.mq, q.cq, RS_UNIT, 0, 384), RS_UNIT), 0, 2, 3, 4),
            timed(rs_all(rs_line(q.mq, q.cq, RS_UNIT2, 384, 384), RS_UNIT2), 0, 2, 3, 4),
        ],
    )
    sums, gate, down, up, out, out2, u, u2 = [t[-1] for t in tail]
    ends[0] = [u, u2, out, out2, down, gate, up]
    grads = unpack(ends[0] + ends[1])

    block = p.dp * 4 + p.ctx
    gain_own = pick(sums[:4].reshape(4, 32, 48), block, 1)
    return (
        output,
        gradient.reshape(2, 64, D),
        gain_own[:2],
        grads[0],
        grads[1],
        grads[2],
        grads[3],
        gain_own[2:],
        grads[4],
        grads[5],
        grads[6],
    )


def solution(mesh):
    tokens = P("dp", ("ctx", "head"), None)
    vector = P(None, ("dp", "ctx"))
    matrix = P(None, ("dp", "ctx"), None)
    return jax.shard_map(
        per_device,
        mesh=mesh,
        in_specs=(
            tokens,
            P("dp", ("ctx", "head")),
            tokens,
            vector,
            matrix,
            matrix,
            matrix,
            matrix,
            vector,
            matrix,
            matrix,
            matrix,
        ),
        out_specs=(
            tokens,
            tokens,
            vector,
            matrix,
            matrix,
            matrix,
            matrix,
            vector,
            matrix,
            matrix,
            matrix,
        ),
        check_vma=False,
    )
```
